32 devices in a mesh: dp: 4 (over z), expert: 8 (over y, x, core).
Axes of the slice: x: 2, y: 2, z: 4, core: 2. Of those that a mesh axis runs over, the one named last changes fastest.
Arguments:
- tokens: bfloat16 [30976, 768], P(('dp', 'expert')), may hold values from -6 to 6
- first_gain: float32 [768], replicated, may hold values from 0.5 to 1.5
- first_shift: float32 [768], replicated, may hold values from -0.6 to 0.6
- query_weight: bfloat16 [768, 768], replicated, may hold values from -0.21875 to 0.21875
- query_bias: float32 [768], replicated, may hold values from -0.6 to 0.6
- key_weight: bfloat16 [768, 768], replicated, may hold values from -0.21875 to 0.21875
- value_weight: bfloat16 [768, 768], replicated, may hold values from -0.21875 to 0.21875
- value_bias: float32 [768], replicated, may hold values from -0.6 to 0.6
- out_weight: bfloat16 [768, 768], replicated, may hold values from -3.5 to 3.5
- out_bias: float32 [768], replicated, may hold values from -0.6 to 0.6
- second_gain: float32 [768], replicated, may hold values from 0.5 to 1.5
- second_shift: float32 [768], replicated, may hold values from -0.6 to 0.6
- router: bfloat16 [768, 8], replicated, may hold values from -0.15625 to 0.15625
- expert_up: bfloat16 [8, 768, 3072], P('expert'), may hold values from -0.21875 to 0.21875
- expert_up_bias: float32 [8, 3072], P('expert'), may hold values from -0.6 to 0.6
- expert_down: bfloat16 [8, 3072, 768], P('expert'), may hold values from -1.75 to 1.75
- expert_down_bias: float32 [8, 768], P('expert'), may hold values from -6 to 6
- choices: int32 [30976, 2], P(('dp', 'expert')), may hold values from 0 to 7, all different within a row; in each aligned block of 968 rows (0 to 967, 968 to 1935, ...) at most 384 rows name the same one
- priority: int32 [32, 968], P(('dp', 'expert')), may hold values from 0 to 967, each once within a row
- cotangent: bfloat16 [30976, 768], P(('dp', 'expert')), may hold values from -6 to 6
Outputs:
- block_output: bfloat16 [30976, 768], P(('dp', 'expert'))
- input_grad: bfloat16 [30976, 768], P(('dp', 'expert'))
- first_gain_grad: float32 [768], replicated
- first_shift_grad: float32 [768], replicated
- query_weight_grad: float32 [768, 768], replicated
- query_bias_grad: float32 [768], replicated
- key_weight_grad: float32 [768, 768], replicated
- value_weight_grad: float32 [768, 768], replicated
- value_bias_grad: float32 [768], replicated
- out_weight_grad: float32 [768, 768], replicated
- out_bias_grad: float32 [768], replicated
- second_gain_grad: float32 [768], replicated
- second_shift_grad: float32 [768], replicated
- router_grad: float32 [768, 8], replicated
- expert_up_grad: float32 [8, 768, 3072], P('expert', 'dp')
- expert_up_bias_grad: float32 [8, 3072], P('expert', 'dp')
- expert_down_grad: float32 [8, 3072, 768], P('expert', 'dp')
- expert_down_bias_grad: float32 [8, 768], P('expert', 'dp')
The draws below stay inside these ranges and needn't reach their ends.
Inputs may be any that keep to these rules, and one draw needn't show every extreme that they name: `choices`: the two experts of a patch differ; among the pairs of one device's patches no expert is named more than 384 times. `priority`: each row holds every number from 0 to 967 once.
All inputs are finite; a program needn't handle non-finite values.
Results may differ from the reference program's by a relative error of at most 0.015.
Values may be sent and summed in bfloat16 or wider, within the bound.
No kernel may reach another device: no remote copies, remote signals or barrier semaphores. Data moves between devices by JAX's collectives and lax.ppermute only.
A program may use at most 320 MiB of HBM per device.

```python
import math
import jax
import jax.numpy as jnp
import numpy as np
from jax import lax

D = 768
HEADS = 12
HEAD_DIM = 64
FF = 3072
BIG = 576
SMALL = 196
TOK_DEV = 968
TOKENS = 30976
EXPERTS = 8
CAP = 256
MOST = 384
N_DP = 4
N_EXPERT = 8


def block_scale(rng, dims, cuts, smallest, top_value):
    factor_of, own = 1.0, jax.random.fold_in(rng, 6)
    for dim, parts in cuts:
        steps = jnp.exp(jax.random.uniform(jax.random.fold_in(own, dim), (parts,), jnp.float32, smallest / len(cuts), top_value / len(cuts)))
        factor_of = factor_of * jnp.repeat(steps, dims[dim] // parts).reshape([-1 if axis == dim else 1 for axis in range(len(dims))])
    return factor_of


def routed_block(key, own, number, rows, number_of, top, bound, skew):
    order = jax.random.permutation(key, number_of)
    packed, ordinary = portions_of(number_of, rows * top, bound, skew, True), portions_of(number_of, rows * top, bound, skew, False)
    places = jnp.arange(number_of)

    def named(lengths, turn):
        used = int((lengths > 0).sum())
        fixed = max(1, used // 4)
        moved = fixed + (places - fixed + turn * (used - fixed)) % max(1, number_of - fixed)
        return jnp.zeros((number_of,), jnp.int32).at[order[jnp.where(places < fixed, places, moved)]].set(jnp.asarray(lengths, jnp.int32))

    lengths = jnp.where(number % 4 == 0, named(packed, number // 4), named(ordinary, number - number // 4 - 1))
    mixed = jax.random.permutation(jax.random.fold_in(own, 3), number_of)
    giver, receiver = mixed[0:number_of // 2 * 2:2], mixed[1:number_of // 2 * 2:2]
    margin = jnp.minimum(lengths[giver] - 1, bound - lengths[receiver]) // 2
    margin = jnp.where((giver == order[0]) | (receiver == order[0]) | (lengths[receiver] == 0), 0, jnp.maximum(margin, 0))
    moved = jax.random.randint(jax.random.fold_in(own, 4), (number_of // 2,), 0, 1 << 20) % (margin + 1)
    lengths = lengths.at[giver].add(-moved).at[receiver].add(moved)
    items = jnp.searchsorted(jnp.cumsum(lengths), jnp.arange(rows * top), side="right").astype(jnp.int32)
    table = items.reshape(top, rows).T
    table = table[jax.random.permutation(jax.random.fold_in(own, 1), rows)]
    turn = jax.random.randint(jax.random.fold_in(own, 2), (rows, 1), 0, top)
    return jnp.take_along_axis(table, (jnp.arange(top)[None, :] + turn) % top, axis=1)


def portions_of(number_of, total, reach, lean, full):
    portions = [(1 << 20) // math.isqrt(standing ** lean) + 1 for standing in range(1, number_of + 1)]
    largest = reach if full else min(reach, max(-(-total // number_of), total * portions[0] // sum(portions)))
    least = 1 if total - largest >= number_of - 1 else 0
    holding, spare = [largest] + [least] * (number_of - 1), total - largest - least * (number_of - 1)
    while spare > 0:
        free = [i for i in range(1, number_of) if holding[i] < largest] or [i for i in range(1, number_of) if holding[i] < reach]
        pool, left = sum([portions[i] for i in free]), spare
        for i in free:
            addition = min(reach - holding[i], max(1, left * portions[i] // pool), spare)
            holding[i] = holding[i] + addition
            spare = spare - addition
    return np.array(holding)


def bell_draw(key, extent, scale, bound, cuts=(), held_as=jnp.bfloat16):
    gain = block_scale(key, extent, cuts, -0.22, 0.18) if cuts else 1.0
    result = jax.random.normal(key, extent, jnp.float32) * scale * gain
    return jnp.minimum(jnp.maximum(result, -bound), bound).astype(held_as)


def setup_inputs(seed: int = 0) -> dict:
    seeds = jax.random.split(jax.random.key(seed), 21)
    tokens = bell_draw(seeds[0], (TOKENS, D), 1.0, 6.0, ((0, 32),))
    first_gain = jnp.clip(1.0 + 0.1 * jax.random.normal(seeds[1], (D,), jnp.float32), 0.5, 1.5)
    first_shift = bell_draw(seeds[2], (D,), 0.1, 0.6, (), jnp.float32)
    query_weight = bell_draw(seeds[3], (D, D), D ** -0.5, 0.21875)
    query_bias = bell_draw(seeds[4], (D,), 0.1, 0.6, (), jnp.float32)
    key_weight = bell_draw(seeds[5], (D, D), D ** -0.5, 0.21875)
    value_weight = bell_draw(seeds[6], (D, D), D ** -0.5, 0.21875)
    value_bias = bell_draw(seeds[7], (D,), 0.1, 0.6, (), jnp.float32)
    out_weight = bell_draw(seeds[8], (D, D), (max(2, D // 256)) ** -0.5, 3.5)
    out_bias = bell_draw(seeds[9], (D,), 0.1, 0.6, (), jnp.float32)
    second_gain = jnp.clip(1.0 + 0.1 * jax.random.normal(seeds[10], (D,), jnp.float32), 0.5, 1.5)
    second_shift = bell_draw(seeds[11], (D,), 0.1, 0.6, (), jnp.float32)
    router = bell_draw(seeds[12], (D, EXPERTS), (2 * D) ** -0.5, 0.15625)
    expert_up = bell_draw(seeds[13], (EXPERTS, D, FF), D ** -0.5, 0.21875, ((0, 8),))
    expert_up_bias = bell_draw(seeds[14], (EXPERTS, FF), 0.1, 0.6, ((0, 8),), jnp.float32)
    expert_down = bell_draw(seeds[15], (EXPERTS, FF, D), (max(4, FF // 256)) ** -0.5, 1.75, ((0, 8),))
    expert_down_bias = bell_draw(seeds[16], (EXPERTS, D), 1.0, 6.0, ((0, 8),), jnp.float32)
    choices_keys = jax.random.split(jax.random.fold_in(seeds[17], 1), TOKENS // TOK_DEV)
    choices_turns = jax.random.permutation(jax.random.fold_in(seeds[17], 3), TOKENS // TOK_DEV)
    choices = jax.vmap(lambda own, number: routed_block(jax.random.fold_in(seeds[17], 2), own, number, TOK_DEV, EXPERTS, 2, MOST, 1))(choices_keys, choices_turns).reshape((TOKENS, 2))
    priority = jax.vmap(lambda own: jax.random.permutation(own, TOK_DEV))(jax.random.split(seeds[18], (N_DP * N_EXPERT))).reshape((N_DP * N_EXPERT, TOK_DEV)).astype(jnp.int32)
    cotangent = bell_draw(seeds[19], (TOKENS, D), 1.0, 6.0, ((0, 32),))
    return dict(tokens=tokens, first_gain=first_gain, first_shift=first_shift, query_weight=query_weight, query_bias=query_bias, key_weight=key_weight, value_weight=value_weight, value_bias=value_bias, out_weight=out_weight, out_bias=out_bias, second_gain=second_gain, second_shift=second_shift, router=router, expert_up=expert_up, expert_up_bias=expert_up_bias, expert_down=expert_down, expert_down_bias=expert_down_bias, choices=choices, priority=priority, cotangent=cotangent)


@jax.custom_vjp
def low(v):
    return lax.optimization_barrier(v.astype(jnp.bfloat16)).astype(jnp.float32)

@jax.custom_vjp
def low_back(v):
    return v

def low_keep(v):
    return (low(v), None)

def low_pass(kept, grad):
    return (grad,)

def back_keep(v):
    return (v, None)

def back_low(kept, grad):
    return (low(grad),)
low.defvjp(low_keep, low_pass)
low_back.defvjp(back_keep, back_low)

def rounded_both(values):
    return low(low_back(values))

def product(left, right):
    return jnp.dot(left, right, precision=lax.Precision.HIGHEST, preferred_element_type=jnp.float32)

def layer_norm(values, norm_gain, norm_shift):
    row_mean = lax.optimization_barrier(jnp.mean(values, axis=-1, keepdims=True))
    centered = values - row_mean
    row_var = lax.optimization_barrier(jnp.mean(centered * centered, axis=-1, keepdims=True))
    return centered * lax.rsqrt(row_var + 1e-06) * norm_gain + norm_shift

def image_ids(tok_count):
    position = jnp.arange(tok_count, dtype=jnp.int32)
    return jnp.where(position < BIG, 0, 1 + (position - BIG) // SMALL).astype(jnp.int32)

def slot_table(choice_rows, priority_row, expert_count, capacity):
    tok_count = priority_row.shape[0]
    order_key = jnp.concatenate([priority_row, priority_row + tok_count]).astype(jnp.int32)
    expert_flat = jnp.concatenate([choice_rows[:, 0], choice_rows[:, 1]]).astype(jnp.int32)
    by_key = jnp.zeros((2 * tok_count,), jnp.int32).at[order_key].set(expert_flat)
    onehot = (by_key[:, None] == jnp.arange(expert_count, dtype=jnp.int32)[None, :]).astype(jnp.int32)
    before = jnp.cumsum(onehot, axis=0) - onehot
    place_by_key = lax.optimization_barrier(jnp.sum(before * onehot, axis=1)).astype(jnp.int32)
    place = place_by_key[order_key]
    kept_mask = place < capacity
    slot_index = jnp.where(kept_mask, expert_flat * capacity + place, expert_count * capacity).astype(jnp.int32)
    return (slot_index.reshape(2, tok_count).T, kept_mask.reshape(2, tok_count).T)

def slot_owner(slot_index, slot_total, tok_count):
    owners = jnp.full((slot_total,), tok_count, jnp.int32)
    token_index = jnp.repeat(jnp.arange(tok_count, dtype=jnp.int32), 2)
    return owners.at[slot_index.reshape(-1)].set(token_index, mode='drop')

def reference(tokens, first_gain, first_shift, query_weight, query_bias, key_weight, value_weight, value_bias, out_weight, out_bias, second_gain, second_shift, router, expert_up, expert_up_bias, expert_down, expert_down_bias, choices, priority, cotangent):
    groups = N_DP * N_EXPERT
    choice_groups = choices.reshape(groups, TOK_DEV, 2)
    slots, kept_mask = jax.vmap(lambda group_choice, group_rank: slot_table(group_choice, group_rank, EXPERTS, CAP))(choice_groups, priority)
    owners = jax.vmap(lambda group_slot: slot_owner(group_slot, EXPERTS * CAP, TOK_DEV))(slots)
    kept_float = kept_mask.astype(jnp.float32)
    image = image_ids(TOK_DEV)
    allowed = image[:, None] == image[None, :]
    score_scale = HEAD_DIM ** (-0.5)

    def forward(params, flat_tokens):
        gain_one, shift_one, w_query, b_query, w_key, w_value, b_value, w_attn_out, b_attn_out, gain_two, shift_two, w_router, w_up, b_up, w_down, b_down = params

        def front(group_tokens):
            normed_one = low(layer_norm(group_tokens, gain_one, shift_one))
            query3 = rounded_both(product(normed_one, w_query) + b_query).reshape(TOK_DEV, HEADS, HEAD_DIM)
            key3 = rounded_both(product(normed_one, w_key)).reshape(TOK_DEV, HEADS, HEAD_DIM)
            value3 = rounded_both(product(normed_one, w_value) + b_value).reshape(TOK_DEV, HEADS, HEAD_DIM)
            raw = jnp.einsum('qhd,khd->hqk', query3, key3, precision=lax.Precision.HIGHEST) * score_scale
            scores = low_back(jnp.where(allowed[None], raw, -1000000000.0))
            att_weights = low(jax.nn.softmax(scores, axis=-1))
            attended = jnp.einsum('hqk,khd->qhd', att_weights, value3, precision=lax.Precision.HIGHEST).reshape(TOK_DEV, D)
            attended = rounded_both(attended)
            middle = group_tokens + low_back(product(attended, w_attn_out) + b_attn_out)
            normed_two = low(layer_norm(middle, gain_two, shift_two))
            router_probs = jax.nn.softmax(product(normed_two, w_router), axis=-1)
            return (middle, normed_two, router_probs)
        middle, normed_two, router_probs = lax.map(jax.checkpoint(front), flat_tokens.reshape(groups, TOK_DEV, D))
        padded_two = jnp.concatenate([normed_two, jnp.zeros((groups, 1, D), jnp.float32)], axis=1)
        sent = low_back(jax.vmap(lambda group_rows, group_owner: group_rows[group_owner])(padded_two, owners))
        expert_rows = sent.reshape(groups, EXPERTS, CAP, D).transpose(1, 0, 2, 3).reshape(EXPERTS, groups * CAP, D)

        def expert(pieces):
            block_rows, up_one, up_bias_one, down_one, down_bias_one = pieces
            pre_act = low_back(product(block_rows, up_one) + up_bias_one)
            act_low = low(jax.nn.gelu(pre_act, approximate=False))
            return rounded_both(product(act_low, down_one) + down_bias_one)
        results = lax.map(jax.checkpoint(expert), (expert_rows, w_up, b_up, w_down, b_down))
        results = results.reshape(EXPERTS, groups, CAP, D).transpose(1, 0, 2, 3).reshape(groups, EXPERTS * CAP, D)
        padded_result = jnp.concatenate([results, jnp.zeros((groups, 1, D), jnp.float32)], axis=1)
        picked = jax.vmap(lambda group_rows, group_slot: group_rows[group_slot])(padded_result, slots)
        gate_values = jnp.take_along_axis(router_probs, choice_groups, axis=2) * kept_float
        mixed = middle + lax.optimization_barrier(jnp.sum(gate_values[..., None] * picked, axis=2))
        return mixed.reshape(TOKENS, D)
    params = (first_gain, first_shift, query_weight.astype(jnp.float32), query_bias, key_weight.astype(jnp.float32), value_weight.astype(jnp.float32), value_bias, out_weight.astype(jnp.float32), out_bias, second_gain, second_shift, router.astype(jnp.float32), expert_up.astype(jnp.float32), expert_up_bias, expert_down.astype(jnp.float32), expert_down_bias)
    mixed, pull = jax.vjp(forward, params, tokens.astype(jnp.float32))
    grads, grad_tokens = pull(cotangent.astype(jnp.float32))
    return (mixed.astype(jnp.bfloat16), grad_tokens.astype(jnp.bfloat16), grads[0], grads[1], grads[2], grads[3], grads[4], grads[5], grads[6], grads[7], grads[8], grads[9], grads[10], grads[11], grads[12], grads[13], grads[14], grads[15])
```

```python
import functools

import jax
import jax.numpy as jnp
from jax import lax
from jax.experimental import pallas as pl
from jax.experimental.pallas import tpu as pltpu
from jax.sharding import PartitionSpec as P

HEADS = 12
BIG = 576
SMALL = 196
LANES = 128
HEAD_GROUPS = 3

half_type = jnp.bfloat16
full_type = jnp.float32
norm_eps = 1e-06
masked_score = -1000000000.0
vmem_bytes = 56 * 2**20


def dot_full(left, right, dims):
    return lax.dot_general(left, right, (dims, ((), ())), preferred_element_type=full_type)


def mul(left, right):
    return dot_full(left, right, ((1,), (0,)))


def mul_t(left, right):
    return dot_full(left, right, ((1,), (1,)))


def t_mul(left, right):
    return dot_full(left, right, ((0,), (0,)))


def row_blocks(rows, step=256):
    return [(start, min(step, rows - start)) for start in range(0, rows, step)]


def iota(shape, dim):
    return lax.broadcasted_iota(jnp.int32, shape, dim)


def ones_where(mask):
    return jnp.where(mask, 1.0, 0.0).astype(half_type)


def normalize(values):
    row_mean = jnp.mean(values, axis=-1, keepdims=True)
    centered = values - row_mean
    inverse = lax.rsqrt(jnp.mean(centered * centered, axis=-1, keepdims=True) + norm_eps)
    return centered * inverse, inverse


def norm_backward(upstream, normed, inverse, norm_gain):
    scaled = upstream * norm_gain
    first_mean = jnp.mean(scaled, axis=-1, keepdims=True)
    second_mean = jnp.mean(scaled * normed, axis=-1, keepdims=True)
    return inverse * (scaled - first_mean - normed * second_mean)


def split_thirds(values, lane, expert_count):
    high = values.astype(half_type).astype(full_type)
    rest = values - high
    middle = rest.astype(half_type).astype(full_type)
    low = rest - middle
    picked = jnp.where(lane < expert_count, high, jnp.where(lane < 2 * expert_count, middle, low))
    return jnp.where(lane < 3 * expert_count, picked, 0.0).astype(half_type)


def call(body, out_shape, name, **kwargs):
    return pl.pallas_call(
        body,
        out_shape=out_shape,
        name=name,
        compiler_params=pltpu.CompilerParams(vmem_limit_bytes=vmem_bytes),
        **kwargs,
    )


def out(shape, dtype):
    return jax.ShapeDtypeStruct(shape, dtype)


def for_experts(expert_count, step):
    if expert_count <= 8:
        for e in range(expert_count):
            step(e)
    else:
        lax.fori_loop(0, expert_count, lambda e, c: (step(e), c)[1], 0)


def expert_rows(e, capacity):
    if isinstance(e, int):
        return pl.ds(e * capacity, capacity)
    return pl.ds(pl.multiple_of(e * capacity, capacity), capacity)


def route_body(expert_count, capacity, cols_ref, rows_ref, rank_col_ref, rank_row_ref, cot_ref, place_ref, slot_ref, sent_ref):
    tok_count = cot_ref.shape[0]
    rank_col, rank_row = rank_col_ref[...], rank_row_ref[...]
    lane = iota((tok_count, LANES), 1)
    first, second = cols_ref[:, 0:1], cols_ref[:, 1:2]
    first_hot, second_hot = ones_where(first == lane), ones_where(second == lane)
    earlier = ones_where(rank_row < rank_col)
    first_total = jnp.sum(first_hot.astype(full_type), axis=0, keepdims=True)
    first_count = mul(earlier, first_hot)
    second_count = mul(earlier, second_hot) + first_total
    first_place = jnp.sum(jnp.where(first == lane, first_count, 0.0), axis=1, keepdims=True).astype(jnp.int32)
    second_place = jnp.sum(jnp.where(second == lane, second_count, 0.0), axis=1, keepdims=True).astype(jnp.int32)
    slot_ref[:, 0:1] = jnp.where(first_place < capacity, first * capacity + first_place, -1)
    slot_ref[:, 1:2] = jnp.where(second_place < capacity, second * capacity + second_place, -1)

    padded = place_ref.shape[0]
    sub = iota((padded, tok_count), 0)
    first, second = rows_ref[0:1, :], rows_ref[1:2, :]
    first_hot, second_hot = ones_where(first == sub), ones_where(second == sub)
    earlier = ones_where(rank_col < rank_row)
    first_total = jnp.sum(first_hot.astype(full_type), axis=1, keepdims=True)
    first_count = mul(first_hot, earlier)
    second_count = mul(second_hot, earlier) + first_total
    place = jnp.where(
        (first == sub) & (first_count < capacity),
        first_count,
        jnp.where((second == sub) & (second_count < capacity), second_count, -1.0),
    )
    place_ref[...] = place.astype(jnp.int32)
    cot = cot_ref[...]
    within = iota((capacity, tok_count), 0)

    def send(e):
        hot = ones_where(place_ref[pl.ds(e, 1), :] == within)
        sent_ref[expert_rows(e, capacity), :] = mul(hot, cot).astype(half_type)

    for_experts(expert_count, send)


def route(choices, priority, cotangent, expert_count, capacity):
    tok_count, feat = cotangent.shape
    padded = -(-expert_count // 32) * 32
    return call(
        functools.partial(route_body, expert_count, capacity),
        (
            out((padded, tok_count), jnp.int32),
            out((tok_count, 2), jnp.int32),
            out((expert_count * capacity, feat), half_type),
        ),
        "route",
    )(choices, choices.T, priority.reshape(tok_count, 1), priority, cotangent)


def image_mask(size):
    key_image = iota((size, 1), 0) // SMALL
    query_image = iota((1, size), 1) // SMALL
    return key_image == query_image


def images(tok_count):
    return ((0, BIG), (BIG, tok_count - BIG))


def head_lanes(value, head):
    lane = iota((1, LANES), 1)
    return jnp.where((lane < LANES // 2) == (head == 0), value, jnp.zeros((), value.dtype))


def front_body(
    expert_count,
    capacity,
    tokens_ref,
    gain_ref,
    shift_ref,
    wq_ref,
    bq_ref,
    wk_ref,
    wv_ref,
    bv_ref,
    wo_ref,
    bo_ref,
    gain2_ref,
    shift2_ref,
    router_ref,
    place_ref,
    first_ref,
    q_ref,
    k_ref,
    v_ref,
    log_big_ref,
    log_small_ref,
    attended_ref,
    middle_ref,
    second_ref,
    probs_ref,
    sent_ref,
    gate_ref,
):
    tok_count, feat = tokens_ref.shape
    scale = (feat // HEADS) ** (-0.5)
    for start, size in row_blocks(tok_count):
        rows = pl.ds(start, size)
        normed, _ = normalize(tokens_ref[rows, :].astype(full_type))
        low = (normed * gain_ref[...] + shift_ref[...]).astype(half_type)
        first_ref[rows, :] = low
        q_ref[rows, :] = (mul(low, wq_ref[...]) + bq_ref[...]).astype(half_type)
        k_ref[rows, :] = mul(low, wk_ref[...]).astype(half_type)
        v_ref[rows, :] = (mul(low, wv_ref[...]) + bv_ref[...]).astype(half_type)

    def pair(number, carry):
        lanes = pl.ds(pl.multiple_of(number * LANES, LANES), LANES)
        for place, (start, size) in enumerate(images(tok_count)):
            rows = pl.ds(start, size)
            query, key, value = q_ref[rows, lanes], k_ref[rows, lanes], v_ref[rows, lanes]
            key = key * jnp.asarray(scale, half_type)
            log_ref = (log_big_ref, log_small_ref)[place]
            value_t = value.T
            halves = []
            for head in range(2):
                scores = mul_t(head_lanes(key, head), query)
                if place:
                    scores = jnp.where(image_mask(size), scores, masked_score)
                top = jnp.max(scores, axis=0, keepdims=True)
                weights = jnp.exp(scores - top)
                total = jnp.sum(weights, axis=0, keepdims=True)
                log_ref[pl.ds(2 * number + head, 1), :] = top + jnp.log(total)
                mixed = mul(value_t[head * 64 : head * 64 + 64], weights.astype(half_type))
                halves.append(mixed * (1.0 / total))
            attended_ref[rows, lanes] = jnp.concatenate(halves, axis=0).T.astype(half_type)
        return carry

    lax.fori_loop(0, HEADS // 2, pair, 0)

    for start, size in row_blocks(tok_count):
        rows = pl.ds(start, size)
        lane = iota((size, LANES), 1)
        middle = tokens_ref[rows, :].astype(full_type) + mul(attended_ref[rows, :], wo_ref[...]) + bo_ref[...]
        middle_ref[rows, :] = middle
        normed, _ = normalize(middle)
        low = (normed * gain2_ref[...] + shift2_ref[...]).astype(half_type)
        second_ref[rows, :] = low
        logits = jnp.where(lane < 3 * expert_count, mul(low, router_ref[...]), masked_score)
        top = jnp.max(logits, axis=1, keepdims=True)
        raised = jnp.exp(logits - top)
        total = jnp.sum(jnp.where(lane < expert_count, raised, 0.0), axis=1, keepdims=True)
        probs_ref[rows, :] = raised / total

    low = second_ref[...]
    lane = iota((tok_count, LANES), 1)
    thirds = split_thirds(probs_ref[...], lane, expert_count)
    within = iota((capacity, tok_count), 0)
    slot_lane = iota((capacity, LANES), 1)

    def send(e):
        hot = ones_where(place_ref[pl.ds(e, 1), :] == within)
        rows = expert_rows(e, capacity)
        sent_ref[rows, :] = mul(hot, low).astype(half_type)
        gates = mul(hot, thirds)
        own = (slot_lane == e) | (slot_lane == e + expert_count) | (slot_lane == e + 2 * expert_count)
        gate_ref[rows, :] = jnp.sum(jnp.where(own, gates, 0.0), axis=1, keepdims=True)

    for_experts(expert_count, send)


def front(tokens, vectors, weights, router3, place, expert_count, capacity):
    tok_count, feat = tokens.shape
    slots = expert_count * capacity
    gain, shift, bq, bv, bo, gain2, shift2 = vectors
    wq, wk, wv, wo = weights
    low = out((tok_count, feat), half_type)
    return call(
        functools.partial(front_body, expert_count, capacity),
        (
            low,
            low,
            low,
            low,
            out((HEADS, BIG), full_type),
            out((HEADS, tok_count - BIG), full_type),
            low,
            out((tok_count, feat), full_type),
            low,
            out((tok_count, LANES), full_type),
            out((slots, feat), half_type),
            out((slots, 1), full_type),
        ),
        "front",
    )(tokens, gain, shift, wq, bq, wk, wv, bv, wo, bo, gain2, shift2, router3, place)


def act_grad_body(cot_ref, gate_ref, down_ref, grad_ref, grad_act_ref, bias_ref):
    @pl.when(pl.program_id(0) == 0)
    def _():
        total = jnp.zeros(bias_ref.shape, full_type)
        for start, size in row_blocks(cot_ref.shape[0]):
            rows = pl.ds(start, size)
            grad = (cot_ref[rows, :].astype(full_type) * gate_ref[rows, :]).astype(half_type)
            grad_ref[rows, :] = grad
            total = total + jnp.sum(grad.astype(full_type), axis=0, keepdims=True)
        bias_ref[...] = total

    for start, size in row_blocks(cot_ref.shape[0]):
        rows = pl.ds(start, size)
        grad_act_ref[rows, :] = mul_t(grad_ref[rows, :], down_ref[...]).astype(half_type)


def act_grad(cot, gate, down, step=512):
    slots, feat = cot.shape
    hidden = down.shape[0]
    return call(
        act_grad_body,
        (out((slots, feat), half_type), out((slots, hidden), half_type), out((1, feat), full_type)),
        "act_grad",
        grid=(hidden // step,),
        in_specs=[
            pl.BlockSpec((slots, feat), lambda f: (0, 0)),
            pl.BlockSpec((slots, 1), lambda f: (0, 0)),
            pl.BlockSpec((step, feat), lambda f: (f, 0)),
        ],
        out_specs=[
            pl.BlockSpec((slots, feat), lambda f: (0, 0)),
            pl.BlockSpec((slots, step), lambda f: (0, f)),
            pl.BlockSpec((1, feat), lambda f: (0, 0)),
        ],
    )(cot, gate, down)


def gelu_parts(values):
    size = jnp.abs(values)
    t = 1.0 / (1.0 + size * (0.3275911 * 0.7071067811865476))
    poly = t * (0.5 * 0.254829592 + t * (0.5 * -0.284496736 + t * (0.5 * 1.421413741 + t * (0.5 * -1.453152027 + t * (0.5 * 1.061405429)))))
    bell = jnp.exp(values * values * -0.5)
    tail = poly * bell
    area = jnp.where(values >= 0.0, 1.0 - tail, tail)
    return values * area, area + values * bell * 0.3989422804014327


def expert_body(rows_ref, up_ref, up_bias_ref, grad_act_ref, act_ref, grad_pre_ref, grad_in_ref, bias_ref, acc_ref):
    step = pl.program_id(0)
    total = jnp.zeros(bias_ref.shape, full_type)

    @pl.when(step == 0)
    def _():
        acc_ref[...] = jnp.zeros(acc_ref.shape, full_type)

    for start, size in row_blocks(rows_ref.shape[0]):
        rows = pl.ds(start, size)
        pre = mul(rows_ref[rows, :], up_ref[...]) + up_bias_ref[...]
        act, slope = gelu_parts(pre)
        act_ref[rows, :] = act.astype(half_type)
        grad_pre = (grad_act_ref[rows, :].astype(full_type) * slope).astype(half_type)
        grad_pre_ref[rows, :] = grad_pre
        total = total + jnp.sum(grad_pre.astype(full_type), axis=0, keepdims=True)
        acc_ref[rows, :] += mul_t(grad_pre, up_ref[...])
    bias_ref[...] = total

    @pl.when(step == pl.num_programs(0) - 1)
    def _():
        grad_in_ref[...] = acc_ref[...].astype(half_type)


def expert(rows, up, up_bias, grad_act, step=512):
    slots, feat = rows.shape
    hidden = up.shape[1]
    wide = pl.BlockSpec((slots, step), lambda f: (0, f))
    return call(
        expert_body,
        (
            out((slots, hidden), half_type),
            out((slots, hidden), half_type),
            out((slots, feat), half_type),
            out((1, hidden), full_type),
        ),
        "expert",
        grid=(hidden // step,),
        in_specs=[
            pl.BlockSpec((slots, feat), lambda f: (0, 0)),
            pl.BlockSpec((feat, step), lambda f: (0, f)),
            pl.BlockSpec((1, step), lambda f: (0, f)),
            wide,
        ],
        out_specs=[
            wide,
            wide,
            pl.BlockSpec((slots, feat), lambda f: (0, 0)),
            pl.BlockSpec((1, step), lambda f: (0, f)),
        ],
        scratch_shapes=[pltpu.VMEM((slots, feat), full_type)],
    )(rows, up, up_bias, grad_act)


def result_body(act_ref, down_ref, down_bias_ref, cot_ref, result_ref, gate_grad_ref):
    result = (mul(act_ref[...], down_ref[...]) + down_bias_ref[...]).astype(half_type)
    result_ref[...] = result
    gate_grad_ref[...] = jnp.sum(result.astype(full_type) * cot_ref[...].astype(full_type), axis=1, keepdims=True)


def expert_result(act, down, down_bias, cot, step=256):
    slots, hidden = act.shape
    feat = down.shape[1]
    narrow = pl.BlockSpec((step, feat), lambda r: (r, 0))
    return call(
        result_body,
        (out((slots, feat), half_type), out((slots, 1), full_type)),
        "result",
        grid=(slots // step,),
        in_specs=[
            pl.BlockSpec((step, hidden), lambda r: (r, 0)),
            pl.BlockSpec((hidden, feat), lambda r: (0, 0)),
            pl.BlockSpec((1, feat), lambda r: (0, 0)),
            narrow,
        ],
        out_specs=[narrow, pl.BlockSpec((step, 1), lambda r: (r, 0))],
    )(act, down, down_bias, cot)


def combine_body(
    expert_count,
    capacity,
    back_ref,
    gate_grad_ref,
    slot_ref,
    probs_ref,
    middle_ref,
    cot_ref,
    attended_ref,
    wo_ref,
    router_ref,
    gain_ref,
    shift_ref,
    grad_middle_ref,
    grad_attended_ref,
    wo_grad_ref,
    router_grad_ref,
    vector_ref,
):
    tok_count, feat = cot_ref.shape
    slots = back_ref.shape[0]
    owner = iota((slots, LANES), 0) // capacity
    lane = iota((slots, LANES), 1)
    same = (lane == owner) | (lane == owner + expert_count) | (lane == owner + 2 * expert_count)
    gate_table = split_thirds(jnp.where(same, gate_grad_ref[...], 0.0), lane, expert_count)
    wo_grad = jnp.zeros(wo_grad_ref.shape, full_type)
    router_grad = jnp.zeros(router_grad_ref.shape, full_type)
    gain_grad = jnp.zeros((1, feat), full_type)
    shift_grad = jnp.zeros((1, feat), full_type)
    bias_grad = jnp.zeros((1, feat), full_type)
    for start, size in row_blocks(tok_count):
        rows = pl.ds(start, size)
        number = iota((size, slots), 1)
        hot = ones_where((number == slot_ref[rows, 0:1]) | (number == slot_ref[rows, 1:2]))
        lane = iota((size, LANES), 1)
        folded = mul(hot, gate_table)
        folded = folded + pltpu.roll(folded, LANES - expert_count, 1) + pltpu.roll(folded, LANES - 2 * expert_count, 1)
        probs = jnp.where(lane < expert_count, probs_ref[rows, :], 0.0)
        grad_probs = jnp.where(lane < expert_count, folded, 0.0)
        grad_logits = probs * (grad_probs - jnp.sum(grad_probs * probs, axis=1, keepdims=True))
        grad_logits = grad_logits + pltpu.roll(grad_logits, expert_count, 1) + pltpu.roll(grad_logits, 2 * expert_count, 1)
        thirds = split_thirds(grad_logits, lane, expert_count)
        upstream = mul_t(thirds, router_ref[...]) + mul(hot, back_ref[...])
        normed, inverse = normalize(middle_ref[rows, :])
        low = (normed * gain_ref[...] + shift_ref[...]).astype(half_type)
        router_grad = router_grad + t_mul(low, thirds)
        gain_grad = gain_grad + jnp.sum(upstream * normed, axis=0, keepdims=True)
        shift_grad = shift_grad + jnp.sum(upstream, axis=0, keepdims=True)
        grad_middle = cot_ref[rows, :].astype(full_type) + norm_backward(upstream, normed, inverse, gain_ref[...])
        grad_middle_ref[rows, :] = grad_middle
        branch = grad_middle.astype(half_type)
        bias_grad = bias_grad + jnp.sum(branch.astype(full_type), axis=0, keepdims=True)
        grad_attended_ref[rows, :] = mul_t(branch, wo_ref[...]).astype(half_type)
        wo_grad = wo_grad + t_mul(attended_ref[rows, :], branch)
    wo_grad_ref[...] = wo_grad.astype(half_type)
    router_grad = router_grad + pltpu.roll(router_grad, LANES - expert_count, 1) + pltpu.roll(router_grad, LANES - 2 * expert_count, 1)
    router_grad_ref[...] = router_grad
    vector_ref[0:1, :] = gain_grad
    vector_ref[1:2, :] = shift_grad
    vector_ref[2:3, :] = bias_grad


def combine(back, gate_grad, slot, probs, middle, cot, attended, wo, router3, gain, shift, expert_count, capacity):
    tok_count, feat = cot.shape
    return call(
        functools.partial(combine_body, expert_count, capacity),
        (
            out((tok_count, feat), full_type),
            out((tok_count, feat), half_type),
            out((feat, feat), half_type),
            out((feat, LANES), full_type),
            out((3, feat), full_type),
        ),
        "combine",
    )(back, gate_grad, slot, probs, middle, cot, attended, wo, router3, gain, shift)


def attention_grad_body(first_head, q_ref, k_ref, v_ref, grad_ref, log_big_ref, log_small_ref, first_ref, dq_ref, dk_ref, dv_ref, wq_ref, wk_ref, wv_ref, bias_ref):
    tok_count, width = q_ref.shape
    scale = 64 ** (-0.5)

    def pair(number, carry):
        lanes = pl.ds(pl.multiple_of(number * LANES, LANES), LANES)
        for place, (start, size) in enumerate(images(tok_count)):
            rows = pl.ds(start, size)
            query, key, value, grad = q_ref[rows, lanes], k_ref[rows, lanes], v_ref[rows, lanes], grad_ref[rows, lanes]
            key = key * jnp.asarray(scale, half_type)
            log_ref = (log_big_ref, log_small_ref)[place]
            key_t = key.T
            halves = []
            grad_value = jnp.zeros((size, LANES), full_type)
            grad_key = jnp.zeros((size, LANES), full_type)
            for head in range(2):
                scores = mul_t(head_lanes(key, head), query)
                if place:
                    scores = jnp.where(image_mask(size), scores, masked_score)
                probs = jnp.exp(scores - log_ref[pl.ds(first_head + 2 * number + head, 1), :])
                grad_probs = mul_t(head_lanes(value, head), grad)
                inner = jnp.sum(grad_probs * probs, axis=0, keepdims=True)
                grad_scores = (probs * (grad_probs - inner)).astype(half_type)
                grad_value = grad_value + mul(probs.astype(half_type), head_lanes(grad, head))
                grad_key = grad_key + mul(grad_scores, head_lanes(query, head))
                halves.append(mul(key_t[head * 64 : head * 64 + 64], grad_scores))
            dv_ref[rows, lanes] = grad_value.astype(half_type)
            dk_ref[rows, lanes] = (grad_key * scale).astype(half_type)
            dq_ref[rows, lanes] = jnp.concatenate(halves, axis=0).T.astype(half_type)
        return carry

    lax.fori_loop(0, width // LANES, pair, 0)
    first = first_ref[...]
    wq_ref[...] = t_mul(first, dq_ref[...]).astype(half_type)
    wk_ref[...] = t_mul(first, dk_ref[...]).astype(half_type)
    wv_ref[...] = t_mul(first, dv_ref[...]).astype(half_type)
    bias_ref[0:1, :] = jnp.sum(dq_ref[...].astype(full_type), axis=0, keepdims=True)
    bias_ref[1:2, :] = jnp.sum(dv_ref[...].astype(full_type), axis=0, keepdims=True)


def attention_grad(group, q, k, v, grad, log_big, log_small, first):
    tok_count, feat = q.shape
    width = feat // HEAD_GROUPS
    columns = pl.BlockSpec((tok_count, width), lambda i: (0, group))
    whole = lambda a: pl.BlockSpec(a.shape, lambda i: (0, 0))
    low = out((tok_count, width), half_type)
    grads = out((feat, width), half_type)
    return call(
        functools.partial(attention_grad_body, group * HEADS // HEAD_GROUPS),
        (low, low, low, grads, grads, grads, out((2, width), full_type)),
        f"attention_grad_{group}",
        grid=(1,),
        in_specs=[columns, columns, columns, columns, whole(log_big), whole(log_small), whole(first)],
    )(q, k, v, grad, log_big, log_small, first)


def input_grad_body(*refs):
    grads = refs[: 3 * HEAD_GROUPS]
    wq_ref, wk_ref, wv_ref, tokens_ref, gain_ref, middle_ref, result_ref, vector_ref = refs[3 * HEAD_GROUPS :]
    tok_count, feat = tokens_ref.shape
    width = feat // HEAD_GROUPS
    gain_grad = jnp.zeros((1, feat), full_type)
    shift_grad = jnp.zeros((1, feat), full_type)
    for start, size in row_blocks(tok_count):
        rows = pl.ds(start, size)
        upstream = jnp.zeros((size, feat), full_type)
        for group in range(HEAD_GROUPS):
            lanes = pl.ds(group * width, width)
            for grad_ref, weight_ref in zip(grads[3 * group : 3 * group + 3], (wq_ref, wk_ref, wv_ref)):
                upstream = upstream + mul_t(grad_ref[rows, :], weight_ref[:, lanes])
        normed, inverse = normalize(tokens_ref[rows, :].astype(full_type))
        gain_grad = gain_grad + jnp.sum(upstream * normed, axis=0, keepdims=True)
        shift_grad = shift_grad + jnp.sum(upstream, axis=0, keepdims=True)
        grad = middle_ref[rows, :] + norm_backward(upstream, normed, inverse, gain_ref[...])
        result_ref[rows, :] = grad.astype(half_type)
    vector_ref[0:1, :] = gain_grad
    vector_ref[1:2, :] = shift_grad


def input_grad(grads, wq, wk, wv, tokens, gain, grad_middle):
    tok_count, feat = tokens.shape
    return call(
        input_grad_body,
        (out((tok_count, feat), half_type), out((2, feat), full_type)),
        "input_grad",
    )(*grads, wq, wk, wv, tokens, gain, grad_middle)


def output_body(returned_ref, slot_ref, choice_ref, probs_ref, middle_ref, result_ref):
    tok_count, feat = middle_ref.shape
    slots = returned_ref.shape[0]
    for start, size in row_blocks(tok_count):
        rows = pl.ds(start, size)
        lane = iota((size, LANES), 1)
        number = iota((size, slots), 1)
        probs = probs_ref[rows, :]
        table = jnp.zeros((size, slots), full_type)
        for k in range(2):
            gate = jnp.sum(jnp.where(lane == choice_ref[rows, k : k + 1], probs, 0.0), axis=1, keepdims=True)
            table = jnp.where(number == slot_ref[rows, k : k + 1], gate, table)
        high = table.astype(half_type)
        low = (table - high.astype(full_type)).astype(half_type)
        mixed = mul(high, returned_ref[...]) + mul(low, returned_ref[...])
        result_ref[rows, :] = (middle_ref[rows, :] + mixed).astype(half_type)


def block_result(returned, slot, choices, probs, middle):
    return call(output_body, out(middle.shape, half_type), "block_result")(returned, slot, choices, probs, middle)


def exchange(values, expert_count):
    split = values.reshape(expert_count, -1, values.shape[1])
    swapped = lax.all_to_all(split, "expert", split_axis=0, concat_axis=0, tiled=True)
    return swapped.reshape(values.shape)


def exchange_column(values, expert_count):
    split = values.reshape(expert_count, -1)
    return lax.all_to_all(split, "expert", split_axis=0, concat_axis=0, tiled=True).reshape(values.shape)


def scatter_sum(values):
    return lax.psum_scatter(values[None], "dp", scatter_dimension=1, tiled=True).astype(full_type)


def shards(
    tokens,
    first_gain,
    first_shift,
    query_weight,
    query_bias,
    key_weight,
    value_weight,
    value_bias,
    out_weight,
    out_bias,
    second_gain,
    second_shift,
    router,
    expert_up,
    expert_up_bias,
    expert_down,
    expert_down_bias,
    choices,
    priority,
    cotangent,
):
    tok_count, feat = tokens.shape
    expert_count = lax.axis_size("expert")
    capacity = (21 * tok_count + 80 * expert_count - 1) // (80 * expert_count) * 8
    row = lambda v: v.reshape(1, -1)
    gain, shift, gain2, shift2 = row(first_gain), row(first_shift), row(second_gain), row(second_shift)
    router3 = jnp.pad(jnp.concatenate([router] * 3, axis=1), ((0, 0), (0, LANES - 3 * expert_count)))
    up, down = expert_up[0], expert_down[0]

    place, slot, cot_sent = route(choices, priority, cotangent, expert_count, capacity)
    cot_rows = exchange(cot_sent, expert_count)
    first, q, k, v, log_big, log_small, attended, middle, _, probs, sent, gate = front(
        tokens,
        (gain, shift, row(query_bias), row(value_bias), row(out_bias), gain2, shift2),
        (query_weight, key_weight, value_weight, out_weight),
        router3,
        place,
        expert_count,
        capacity,
    )
    gate_rows = exchange_column(gate, expert_count)
    arrived = exchange(sent, expert_count)
    grad_rows, grad_act, down_bias_part = act_grad(cot_rows, gate_rows, down)
    act, grad_pre, grad_in, up_bias_part = expert(arrived, up, row(expert_up_bias), grad_act)
    back = exchange(grad_in, expert_count)
    down_grad = t_mul(act, grad_rows).astype(half_type)
    expert_down_grad = scatter_sum(down_grad)
    result, gate_grad = expert_result(act, down, row(expert_down_bias), cot_rows)
    gate_grad_back = exchange_column(gate_grad, expert_count)
    returned = exchange(result, expert_count)
    up_grad = t_mul(arrived, grad_pre).astype(half_type)
    expert_up_grad = scatter_sum(up_grad)
    expert_up_bias_grad = scatter_sum(up_bias_part.reshape(-1).astype(half_type))
    expert_down_bias_grad = scatter_sum(down_bias_part.reshape(-1).astype(half_type))

    grad_middle, grad_attended, wo_grad, router_part, second_parts = combine(
        back, gate_grad_back, slot, probs, middle, cotangent, attended, out_weight, router3, gain2, shift2, expert_count, capacity
    )
    both = ("dp", "expert")
    out_weight_grad = lax.psum(wo_grad, both).astype(full_type)
    grads, bias_parts, weight_parts = [], [], []
    for group in range(HEAD_GROUPS):
        dq, dk, dv, wq_part, wk_part, wv_part, bias_part = attention_grad(
            group, q, k, v, grad_attended, log_big, log_small, first
        )
        grads += [dq, dk, dv]
        bias_parts.append(bias_part)
        weight_parts.append(lax.psum(jnp.stack([wq_part, wk_part, wv_part]), both))
    weight_grads = jnp.concatenate(weight_parts, axis=2).astype(full_type)
    bias_part = jnp.concatenate(bias_parts, axis=1)
    token_grad, first_parts = input_grad(grads, query_weight, key_weight, value_weight, tokens, gain, grad_middle)
    block_output = block_result(returned, slot, choices, probs, middle)
    vectors, router_grad = lax.psum(
        (jnp.concatenate([first_parts, bias_part, second_parts]), router_part[:, :expert_count]), both
    )
    return (
        block_output,
        token_grad,
        vectors[0],
        vectors[1],
        weight_grads[0],
        vectors[2],
        weight_grads[1],
        weight_grads[2],
        vectors[3],
        out_weight_grad,
        vectors[6],
        vectors[4],
        vectors[5],
        router_grad,
        expert_up_grad,
        expert_up_bias_grad,
        expert_down_grad,
        expert_down_bias_grad,
    )


def solution(mesh):
    tokens_spec = P(("dp", "expert"), None)
    return jax.shard_map(
        shards,
        mesh=mesh,
        in_specs=(tokens_spec,)
        + (P(),) * 12
        + (P("expert", None, None), P("expert", None), P("expert", None, None), P("expert", None))
        + (tokens_spec,) * 3,
        out_specs=(tokens_spec,) * 2
        + (P(),) * 12
        + (P("expert", "dp", None), P("expert", "dp"), P("expert", "dp", None), P("expert", "dp")),
        check_vma=False,
    )
```

```python
import functools

import jax
import jax.numpy as jnp
from jax import lax
from jax.experimental import pallas as pl
from jax.experimental.pallas import tpu as pltpu
from jax.sharding import PartitionSpec as P

HEADS = 12
BIG = 576
SMALL = 196
LANES = 128
EXTRA = 16
HEAD_GROUPS = 2

half_type = jnp.bfloat16
full_type = jnp.float32
norm_eps = 1e-06
masked_score = -1000000000.0
vmem_bytes = 56 * 2**20


def dot_full(left, right, dims):
    return lax.dot_general(left, right, (dims, ((), ())), preferred_element_type=full_type)


def mul(left, right):
    return dot_full(left, right, ((1,), (0,)))


def mul_t(left, right):
    return dot_full(left, right, ((1,), (1,)))


def t_mul(left, right):
    return dot_full(left, right, ((0,), (0,)))


def row_blocks(rows, step=256):
    return [(start, min(step, rows - start)) for start in range(0, rows, step)]


def iota(shape, dim):
    return lax.broadcasted_iota(jnp.int32, shape, dim)


def ones_where(mask):
    return jnp.where(mask, 1.0, 0.0).astype(half_type)


def normalize(values):
    row_mean = jnp.mean(values, axis=-1, keepdims=True)
    centered = values - row_mean
    inverse = lax.rsqrt(jnp.mean(centered * centered, axis=-1, keepdims=True) + norm_eps)
    return centered * inverse, inverse


def norm_backward(upstream, normed, inverse, norm_gain):
    scaled = upstream * norm_gain
    first_mean = jnp.mean(scaled, axis=-1, keepdims=True)
    second_mean = jnp.mean(scaled * normed, axis=-1, keepdims=True)
    return inverse * (scaled - first_mean - normed * second_mean)


def split_thirds(values, lane, expert_count):
    high = values.astype(half_type).astype(full_type)
    rest = values - high
    middle = rest.astype(half_type).astype(full_type)
    low = rest - middle
    picked = jnp.where(lane < expert_count, high, jnp.where(lane < 2 * expert_count, middle, low))
    return jnp.where(lane < 3 * expert_count, picked, 0.0).astype(half_type)


def call(body, out_shape, name, after=(), grid=(1,), in_specs=None, flops=1024, **kwargs):
    def build(*operands):
        specs = list(in_specs) if in_specs else [whole(a) for a in operands]
        used = len(specs)
        if "out_specs" not in kwargs:
            kwargs["out_specs"] = jax.tree.map(whole, out_shape)

        def inner(*refs):
            body(*refs[:used], *refs[used + len(after) :])

        return pl.pallas_call(
            inner,
            out_shape=out_shape,
            name=name,
            grid=grid,
            in_specs=specs + [pl.BlockSpec(memory_space=pl.ANY)] * len(after),
            compiler_params=pltpu.CompilerParams(vmem_limit_bytes=vmem_bytes),
            cost_estimate=pl.CostEstimate(flops=flops, bytes_accessed=1024, transcendentals=0),
            **kwargs,
        )(*operands, *after)

    return build


def whole(array):
    zeros = (0,) * len(array.shape)
    return pl.BlockSpec(array.shape, lambda *_: zeros)


def out(shape, dtype):
    return jax.ShapeDtypeStruct(shape, dtype)


def vec(ref):
    return ref[...].reshape(1, -1)


def for_experts(expert_count, step):
    if expert_count <= 8:
        for e in range(expert_count):
            step(e)
    else:
        lax.fori_loop(0, expert_count, lambda e, c: (step(e), c)[1], 0)


def expert_rows(e, capacity):
    if isinstance(e, int):
        return pl.ds(e * capacity, capacity)
    return pl.ds(pl.multiple_of(e * capacity, capacity), capacity)


def row_thirds(row):
    high = row.astype(half_type).astype(full_type)
    rest = row - high
    middle = rest.astype(half_type).astype(full_type)
    sub = iota((8, row.shape[1]), 0)
    picked = jnp.where(sub == 0, high, jnp.where(sub == 1, middle, jnp.where(sub == 2, rest - middle, 0.0)))
    return picked.astype(half_type)


def thirds_to_lanes(thirds):
    return t_mul(thirds, jnp.ones((thirds.shape[0], LANES), half_type))


def store_thirds(ref, start, row):
    ref[pl.ds(start, EXTRA), :] = jnp.zeros((EXTRA, ref.shape[1]), ref.dtype)
    thirds = jnp.concatenate([row_thirds(row), jnp.zeros((EXTRA - 8, row.shape[1]), half_type)], axis=0)
    ref[pl.ds(start, EXTRA), 0 : row.shape[1]] = thirds


def part_start(e, size, offset=0):
    if isinstance(e, int):
        return e * size + offset
    return pl.multiple_of(e * size + offset, 16)


def lanes_to_row(values):
    ones = jnp.ones((8, LANES), half_type)
    high = values.astype(half_type)
    rest = values - high.astype(full_type)
    middle = rest.astype(half_type)
    low = (rest - middle.astype(full_type)).astype(half_type)
    return (mul_t(ones, high) + mul_t(ones, middle) + mul_t(ones, low))[0:1]


def route_body(expert_count, capacity, rows_ref, rank_ref, cot_ref, place_ref, slot_ref, sent_ref):
    tok_count = cot_ref.shape[0]
    half = capacity // 2
    rows = jnp.concatenate([rows_ref[...], rank_ref[...], jnp.zeros((5, tok_count), jnp.int32)], axis=0)
    columns = rows.astype(full_type).T.astype(jnp.int32)
    first, second, rank_col = columns[:, 0:1], columns[:, 1:2], columns[:, 2:3]
    rank_row = rank_ref[...]
    lane = iota((tok_count, LANES), 1)
    first_hot, second_hot = ones_where(first == lane), ones_where(second == lane)
    earlier = ones_where(rank_row < rank_col)
    first_total = jnp.sum(first_hot.astype(full_type), axis=0, keepdims=True)
    first_count = mul(earlier, first_hot)
    second_count = mul(earlier, second_hot) + first_total
    for k, (expert, count) in enumerate(((first, first_count), (second, second_count))):
        place = jnp.sum(jnp.where(expert == lane, count, 0.0), axis=1, keepdims=True).astype(jnp.int32)
        part = half + EXTRA
        place = jnp.where(place < half, place, jnp.where(place < capacity, place + expert_count * part - half, -1))
        slot_ref[:, k : k + 1] = jnp.where(place < 0, -1, expert * part + place)

    padded = place_ref.shape[0]
    sub = iota((padded, tok_count), 0)
    first, second = rows_ref[0:1, :], rows_ref[1:2, :]
    first_hot, second_hot = ones_where(first == sub), ones_where(second == sub)
    earlier = ones_where(rank_col < rank_row)
    first_total = jnp.sum(first_hot.astype(full_type), axis=1, keepdims=True)
    first_count = mul(first_hot, earlier)
    second_count = mul(second_hot, earlier) + first_total
    place = jnp.where(
        (first == sub) & (first_count < capacity),
        first_count,
        jnp.where((second == sub) & (second_count < capacity), second_count, -1.0),
    )
    place_ref[...] = place.astype(jnp.int32)
    cot = cot_ref[...]
    within = iota((capacity, tok_count), 0)

    def send(e):
        hot = ones_where(place_ref[pl.ds(e, 1), :] == within)
        sent_ref[expert_rows(e, capacity), :] = mul(hot, cot).astype(half_type)

    for_experts(expert_count, send)


def route(choice_rows, priority, cotangent, expert_count, capacity):
    tok_count, feat = cotangent.shape
    padded = -(-expert_count // 32) * 32
    sent = out((expert_count * capacity, feat), half_type)
    return call(
        functools.partial(route_body, expert_count, capacity),
        (out((padded, tok_count), jnp.int32), out((tok_count, 2), jnp.int32), sent),
        "route",
    )(choice_rows, priority, cotangent)


def image_mask(size):
    key_image = iota((size, 1), 0) // SMALL
    query_image = iota((1, size), 1) // SMALL
    return key_image == query_image


def images(tok_count):
    return ((0, BIG), (BIG, tok_count - BIG))


def head_lanes(value, head):
    lane = iota((1, LANES), 1)
    return jnp.where((lane < LANES // 2) == (head == 0), value, jnp.zeros((), value.dtype))


def front_body(
    expert_count,
    capacity,
    tokens_ref,
    gain_ref,
    shift_ref,
    wq_ref,
    bq_ref,
    wk_ref,
    wv_ref,
    bv_ref,
    wo_ref,
    bo_ref,
    gain2_ref,
    shift2_ref,
    router_ref,
    place_ref,
    first_ref,
    q_ref,
    k_ref,
    v_ref,
    log_big_ref,
    log_small_ref,
    attended_ref,
    middle_ref,
    second_ref,
    probs_ref,
    sent_a_ref,
    sent_b_ref,
):
    tok_count, feat = tokens_ref.shape
    scale = (feat // HEADS) ** (-0.5)
    for start, size in row_blocks(tok_count):
        rows = pl.ds(start, size)
        normed, _ = normalize(tokens_ref[rows, :].astype(full_type))
        low = (normed * vec(gain_ref) + vec(shift_ref)).astype(half_type)
        first_ref[rows, :] = low
        q_ref[rows, :] = (mul(low, wq_ref[...]) + vec(bq_ref)).astype(half_type)
        k_ref[rows, :] = mul(low, wk_ref[...]).astype(half_type)
        v_ref[rows, :] = (mul(low, wv_ref[...]) + vec(bv_ref)).astype(half_type)

    def pair(number, carry):
        lanes = pl.ds(pl.multiple_of(number * LANES, LANES), LANES)
        for place, (start, size) in enumerate(images(tok_count)):
            rows = pl.ds(start, size)
            query, key, value = q_ref[rows, lanes], k_ref[rows, lanes], v_ref[rows, lanes]
            key = key * jnp.asarray(scale, half_type)
            log_ref = (log_big_ref, log_small_ref)[place]
            value_t = value.T
            halves = []
            for head in range(2):
                scores = mul_t(head_lanes(key, head), query)
                if place:
                    scores = jnp.where(image_mask(size), scores, masked_score)
                top = jnp.max(scores, axis=0, keepdims=True)
                weights = jnp.exp(scores - top)
                total = jnp.sum(weights, axis=0, keepdims=True)
                log_ref[pl.ds(2 * number + head, 1), :] = top + jnp.log(total)
                mixed = mul(value_t[head * 64 : head * 64 + 64], weights.astype(half_type))
                halves.append(mixed * (1.0 / total))
            attended_ref[rows, lanes] = jnp.concatenate(halves, axis=0).T.astype(half_type)
        return carry

    lax.fori_loop(0, HEADS // 2, pair, 0)

    for start, size in row_blocks(tok_count):
        rows = pl.ds(start, size)
        lane = iota((size, LANES), 1)
        middle = tokens_ref[rows, :].astype(full_type) + mul(attended_ref[rows, :], wo_ref[...]) + vec(bo_ref)
        middle_ref[rows, :] = middle
        normed, _ = normalize(middle)
        low = (normed * vec(gain2_ref) + vec(shift2_ref)).astype(half_type)
        second_ref[rows, :] = low
        logits = jnp.where(lane < 3 * expert_count, mul(low, router_ref[...]), masked_score)
        top = jnp.max(logits, axis=1, keepdims=True)
        raised = jnp.exp(logits - top)
        total = jnp.sum(jnp.where(lane < expert_count, raised, 0.0), axis=1, keepdims=True)
        probs_ref[rows, :] = raised / total

    low = second_ref[...]
    lane = iota((tok_count, LANES), 1)
    thirds = split_thirds(probs_ref[...], lane, expert_count)
    within = iota((capacity, tok_count), 0)
    slot_lane = iota((capacity, LANES), 1)

    def send(e):
        hot = ones_where(place_ref[pl.ds(e, 1), :] == within)
        rows = mul(hot, low).astype(half_type)
        half = capacity // 2
        part = half + EXTRA
        sent_a_ref[pl.ds(part_start(e, part), half), :] = rows[:half]
        sent_b_ref[pl.ds(part_start(e, half), half), :] = rows[half:]
        gates = mul(hot, thirds)
        own = (slot_lane == e) | (slot_lane == e + expert_count) | (slot_lane == e + 2 * expert_count)
        picked = jnp.where(own, gates, 0.0).astype(half_type)
        store_thirds(sent_a_ref, part_start(e, part, half), mul_t(jnp.ones((8, LANES), half_type), picked)[0:1])

    for_experts(expert_count, send)


def front(tokens, vectors, weights, router3, place, expert_count, capacity):
    tok_count, feat = tokens.shape
    half = expert_count * capacity // 2
    gain, shift, bq, bv, bo, gain2, shift2 = vectors
    wq, wk, wv, wo = weights
    low = out((tok_count, feat), half_type)
    return call(
        functools.partial(front_body, expert_count, capacity),
        (
            low,
            low,
            low,
            low,
            out((HEADS, BIG), full_type),
            out((HEADS, tok_count - BIG), full_type),
            low,
            out((tok_count, feat), full_type),
            low,
            out((tok_count, LANES), full_type),
            out((half + expert_count * EXTRA, feat), half_type),
            out((half, feat), half_type),
        ),
        "front",
    )(tokens, gain, shift, wq, bq, wk, wv, bv, wo, bo, gain2, shift2, router3, place)


def fold_lanes(values):
    folded = values[:, :LANES]
    for start in range(LANES, values.shape[1], LANES):
        folded = folded + values[:, start : start + LANES]
    return folded


def act_grad_body(half, cot_ref, down_ref, down_bias_ref, grad_act_ref, score_ref):
    slots = cot_ref.shape[0]
    experts = slots // half // 2

    @pl.when(pl.program_id(0) == 0)
    def _():
        for number in range(2 * experts):
            product = cot_ref[number * half : number * half + half, :].astype(full_type) * down_bias_ref[...]
            place = (number % 2 * experts + number // 2) * half
            score_ref[place : place + half, :] = fold_lanes(product)

    for start, size in row_blocks(slots, 512):
        grad_act = mul_t(cot_ref[start : start + size, :], down_ref[...]).astype(half_type)
        for piece in range(size // half):
            number = start // half + piece
            place = (number % 2 * experts + number // 2) * half
            grad_act_ref[place : place + half, :] = grad_act[piece * half : piece * half + half]


def act_grad(cot, down, down_bias, expert_count, step=512):
    slots, feat = cot.shape
    hidden = down.shape[0]
    return call(
        functools.partial(act_grad_body, slots // expert_count // 2),
        (out((slots, hidden), half_type), out((slots, LANES), full_type)),
        "act_grad",
        grid=(hidden // step,),
        in_specs=[whole(cot), pl.BlockSpec((step, feat), lambda f: (f, 0)), whole(down_bias)],
        out_specs=[pl.BlockSpec((slots, step), lambda f: (0, f)), pl.BlockSpec((slots, LANES), lambda f: (0, 0))],
    )(cot, down, down_bias)


def gelu_parts(values):
    area = 0.5 + 0.5 * lax.erf(values * 0.7071067811865476)
    bell = jnp.exp(values * values * -0.5) * 0.3989422804014327
    return values * area, area + values * bell


def expert_core(x_ref, up_ref, up_bias_ref, grad_act_ref, start_ref, cot_ref, gate_ref, act_ref, grad_pre_ref, gated_ref, grad_ref, grad_in_ref, acc_ref, sum_ref, pre_ref):
    slots, feat = x_ref.shape
    width = up_ref.shape[1]
    half = cot_ref.shape[2]
    part = half + EXTRA
    number = pl.program_id(0)

    @pl.when(number == 0)
    def _():
        acc_ref[...] = jnp.zeros(acc_ref.shape, full_type)
        sum_ref[...] = jnp.zeros(sum_ref.shape, full_type)
        for e in range(slots // half):
            rows = pl.ds(e * half, half)
            wide = jnp.concatenate([gate_ref[rows, :]] * (feat // LANES), axis=1)
            gated_ref[rows, :] = (x_ref[rows, :].astype(full_type) * wide).astype(half_type)
            grad_ref[rows, :] = (cot_ref[e, 0].astype(full_type) * wide).astype(half_type)

    blocks = row_blocks(slots, pre_ref.shape[1])
    pre_ref[0] = mul(x_ref[pl.ds(*blocks[0]), :], up_ref[...])
    for b, (start, size) in enumerate(blocks):
        if b + 1 < len(blocks):
            pre_ref[(b + 1) % 2] = mul(x_ref[pl.ds(*blocks[b + 1]), :], up_ref[...])
        if b:
            rows = pl.ds(*blocks[b - 1])
            acc_ref[rows, :] += mul_t(grad_pre_ref[rows, :], up_ref[...])
        for inner in range(0, size, 16):
            rows = pl.ds(start + inner, 16)
            act, slope = gelu_parts(pre_ref[b % 2, inner : inner + 16, :] + up_bias_ref[...])
            act_ref[rows, :] = act.astype(half_type)
            grad_act = grad_act_ref[rows, :].astype(full_type)
            sum_ref[rows, :] += fold_lanes(act * grad_act)
            grad_pre_ref[rows, :] = (grad_act * slope).astype(half_type)
    rows = pl.ds(*blocks[-1])
    acc_ref[rows, :] += mul_t(grad_pre_ref[rows, :], up_ref[...])

    @pl.when(number == pl.num_programs(0) - 1)
    def _():
        for e in range(slots // half):
            rows = pl.ds(e * half, half)
            gate = gate_ref[rows, :]
            wide = jnp.concatenate([gate] * (feat // LANES), axis=1)
            grad_in_ref[pl.ds(e * part, half), :] = (acc_ref[rows, :] * wide).astype(half_type)
            store_thirds(grad_in_ref, e * part + half, lanes_to_row((start_ref[rows, :] + sum_ref[rows, :]) * gate))


def first_expert_body(rows_ref, up_ref, up_bias_ref, grad_act_ref, start_ref, cot_ref, act_ref, grad_pre_ref, gated_ref, grad_ref, grad_in_ref, gate_ref, x_ref, *scratch):
    slots = x_ref.shape[0]
    half = cot_ref.shape[2]
    part = half + EXTRA

    @pl.when(pl.program_id(0) == 0)
    def _():
        for e in range(slots // half):
            x_ref[pl.ds(e * half, half), :] = rows_ref[pl.ds(e * part, half), :]
            for h in range(2):
                thirds = rows_ref[pl.ds(e * part + half, EXTRA), h * half : h * half + half]
                gate_ref[pl.ds(h * slots + e * half, half), :] = thirds_to_lanes(thirds)

    expert_core(
        x_ref, up_ref, up_bias_ref, grad_act_ref, start_ref, cot_ref, gate_ref.at[pl.ds(0, slots), :],
        act_ref, grad_pre_ref, gated_ref, grad_ref, grad_in_ref, *scratch,
    )


def second_expert_body(*refs):
    expert_core(*refs[:7], *refs[11:])


def expert(h, rows, up, up_bias, grad_act, start, cot, earlier=(), step=512):
    feat, hidden = up.shape
    expert_count, _, half, _ = cot.shape
    slots = expert_count * half
    wide = pl.BlockSpec((slots, step), lambda f: (h, f))
    narrow = pl.BlockSpec((slots, feat), lambda f: (h, 0))
    lanes = pl.BlockSpec((slots, LANES), lambda f: (h, 0))
    grad_in = out((slots + expert_count * EXTRA, feat), half_type)
    shapes = [out((2 * slots, hidden), half_type)] * 2 + [out((2 * slots, feat), half_type)] * 2 + [grad_in]
    out_specs = [wide, wide, narrow, narrow, whole(grad_in)]
    scratch = [pltpu.VMEM((slots, feat), full_type), pltpu.VMEM((slots, LANES), full_type), pltpu.VMEM((2, 256, step), full_type)]
    in_specs = [
        whole(rows),
        pl.BlockSpec((feat, step), lambda f: (0, f)),
        pl.BlockSpec((1, step), lambda f: (0, f)),
        wide,
        lanes,
        pl.BlockSpec((expert_count, 1, half, feat), lambda f: (0, h, 0, 0)),
    ]
    aliases = {}
    if h == 0:
        gates = out((2 * slots, LANES), full_type)
        shapes, out_specs = shapes + [gates], out_specs + [whole(gates)]
        scratch = [pltpu.VMEM((slots, feat), half_type)] + scratch
    else:
        in_specs += [lanes] + [pl.BlockSpec(memory_space=pl.ANY)] * 4
        aliases = {7: 0, 8: 1, 9: 2, 10: 3}
        earlier = (earlier[5], *earlier[:4])
    return call(
        second_expert_body if h else first_expert_body,
        tuple(shapes),
        f"expert_{h}",
        grid=(hidden // step,),
        in_specs=in_specs,
        out_specs=out_specs,
        scratch_shapes=scratch,
        input_output_aliases=aliases,
    )(rows, up, up_bias, grad_act, start, cot, *earlier)


def weight_grad_body(act_ref, pre_ref, gated_ref, grad_ref, gate_ref, sum_ref, up_bias_ref, down_bias_ref, up_ref, down_ref, sems):
    slots, feat = gated_ref.shape
    steps, replicas, share = up_ref.shape[:3]
    number = pl.program_id(0)
    down_rows = steps * share
    size = min(down_rows, feat)

    def copies(step):
        pairs = [(up_ref.at[step], sum_ref.at[:, pl.ds(step * share, share), :])]
        for piece in range(feat // size):
            row = step * feat + piece * size
            target = sum_ref.at[row // down_rows, pl.ds(down_rows + row % down_rows, size), :]
            pairs.append((down_ref.at[step, pl.ds(piece * size, size)], target))
        return [pltpu.make_async_copy(a, b, sems.at[step, i]) for i, (a, b) in enumerate(pairs)]

    up = t_mul(gated_ref[...], pre_ref[...])
    up_ref[number] = up.astype(half_type).reshape(replicas, share, feat)
    down_ref[number] = t_mul(act_ref[...], grad_ref[...]).astype(half_type)
    total = jnp.zeros((16, feat), full_type)
    for start in range(0, slots, 16):
        wide = jnp.concatenate([gate_ref[start : start + 16, :]] * (feat // LANES), axis=1)
        total = total + pre_ref[start : start + 16, :].astype(full_type) * wide
    up_bias_ref[...] = jnp.sum(total, axis=0, keepdims=True)
    for step in range(steps):

        @pl.when(number == step)
        def _():
            for copy in copies(step):
                copy.start()

    @pl.when(number == steps - 1)
    def _():
        down_bias_ref[...] = jnp.sum(grad_ref[...].astype(full_type), axis=0, keepdims=True)
        for step in range(steps):
            for copy in copies(step):
                copy.wait()


def weight_grad(act, grad_pre, gated, grad, gate, replicas, after=()):
    slots, hidden = act.shape
    feat = gated.shape[1]
    steps, share = hidden // feat, feat // replicas
    wide = pl.BlockSpec((slots, feat), lambda f: (0, f))
    return call(
        weight_grad_body,
        (out((replicas, 2 * steps * share, feat), half_type), out((1, hidden), full_type), out((1, feat), full_type)),
        "weight_grad",
        after,
        grid=(steps,),
        in_specs=[wide, wide, whole(gated), whole(grad), whole(gate)],
        out_specs=[
            pl.BlockSpec(memory_space=pl.ANY),
            pl.BlockSpec((1, feat), lambda f: (0, f)),
            pl.BlockSpec((1, feat), lambda f: (0, 0)),
        ],
        scratch_shapes=[
            pltpu.VMEM((steps, replicas, share, feat), half_type),
            pltpu.VMEM((steps, feat, feat), half_type),
            pltpu.SemaphoreType.DMA((steps, 1 + max(1, feat // (steps * share)))),
        ],
    )(act, grad_pre, gated, grad, gate)


def result_body(expert_count, act_ref, down_ref, down_bias_ref, result_ref):
    number = pl.program_id(0)
    steps = pl.num_programs(0) // 2
    size = act_ref.shape[0]
    half = size * steps // expert_count
    result = (mul(act_ref[...], down_ref[...]) + down_bias_ref[...]).astype(half_type)
    for e in range(size // half):
        order = number % steps * (size // half) + e
        start = pl.multiple_of((order * 2 + number // steps) * half, half)
        result_ref[pl.ds(start, half), :] = result[e * half : e * half + half]


def expert_result(act, down, down_bias, expert_count, after=(), step=512):
    slots, hidden = act.shape
    feat = down.shape[1]
    return call(
        functools.partial(result_body, expert_count),
        out((slots, feat), half_type),
        "result",
        after,
        grid=(slots // step,),
        in_specs=[pl.BlockSpec((step, hidden), lambda r: (r, 0)), whole(down), whole(down_bias)],
    )(act, down, down_bias)


def combine_body(
    expert_count,
    capacity,
    back_a_ref,
    back_b_ref,
    slot_ref,
    probs_ref,
    middle_ref,
    cot_ref,
    attended_ref,
    wo_ref,
    router_ref,
    gain_ref,
    shift_ref,
    grad_middle_ref,
    grad_attended_ref,
    wo_grad_ref,
    router_grad_ref,
    vector_ref,
):
    tok_count, feat = cot_ref.shape
    slots = back_a_ref.shape[0]
    half = capacity // 2
    lane = iota((half, LANES), 1)
    tables = []
    for h in range(2):
        parts = []
        for e in range(expert_count):
            same = (lane == e) | (lane == e + expert_count) | (lane == e + 2 * expert_count)
            thirds = (back_a_ref, back_b_ref)[h][pl.ds(e * (half + EXTRA) + half, EXTRA), 0:half]
            score = jnp.where(same, thirds_to_lanes(thirds), 0.0)
            parts.append(split_thirds(score, lane, expert_count))
            parts.append(jnp.zeros((EXTRA, LANES), half_type))
        tables.append(jnp.concatenate(parts, axis=0))
    wo_grad = jnp.zeros(wo_grad_ref.shape, full_type)
    router_grad = jnp.zeros(router_grad_ref.shape, full_type)
    gain_grad = jnp.zeros((1, feat), full_type)
    shift_grad = jnp.zeros((1, feat), full_type)
    bias_grad = jnp.zeros((1, feat), full_type)
    for start, size in row_blocks(tok_count):
        rows = pl.ds(start, size)
        number = iota((size, slots), 1)
        slot_one, slot_two = slot_ref[rows, 0:1], slot_ref[rows, 1:2]
        hot_a = ones_where((number == slot_one) | (number == slot_two))
        hot_b = ones_where((number == slot_one - slots) | (number == slot_two - slots))
        lane = iota((size, LANES), 1)
        folded = mul(hot_a, tables[0]) + mul(hot_b, tables[1])
        folded = folded + pltpu.roll(folded, LANES - expert_count, 1) + pltpu.roll(folded, LANES - 2 * expert_count, 1)
        probs = jnp.where(lane < expert_count, probs_ref[rows, :], 0.0)
        scores = jnp.where(lane < expert_count, folded, 0.0)
        grad_logits = scores - probs * jnp.sum(scores, axis=1, keepdims=True)
        grad_logits = grad_logits + pltpu.roll(grad_logits, expert_count, 1) + pltpu.roll(grad_logits, 2 * expert_count, 1)
        thirds = split_thirds(grad_logits, lane, expert_count)
        upstream = mul_t(thirds, router_ref[...]) + mul(hot_a, back_a_ref[...]) + mul(hot_b, back_b_ref[...])
        normed, inverse = normalize(middle_ref[rows, :])
        low = (normed * vec(gain_ref) + vec(shift_ref)).astype(half_type)
        router_grad = router_grad + t_mul(low, thirds)
        gain_grad = gain_grad + jnp.sum(upstream * normed, axis=0, keepdims=True)
        shift_grad = shift_grad + jnp.sum(upstream, axis=0, keepdims=True)
        grad_middle = cot_ref[rows, :].astype(full_type) + norm_backward(upstream, normed, inverse, vec(gain_ref))
        grad_middle_ref[rows, :] = grad_middle
        branch = grad_middle.astype(half_type)
        bias_grad = bias_grad + jnp.sum(branch.astype(full_type), axis=0, keepdims=True)
        grad_attended_ref[rows, :] = mul_t(branch, wo_ref[...]).astype(half_type)
        wo_grad = wo_grad + t_mul(attended_ref[rows, :], branch)
    wo_grad_ref[...] = wo_grad.astype(half_type)
    router_grad = router_grad + pltpu.roll(router_grad, LANES - expert_count, 1) + pltpu.roll(router_grad, LANES - 2 * expert_count, 1)
    router_grad_ref[...] = router_grad
    vector_ref[0:1, :] = gain_grad
    vector_ref[1:2, :] = shift_grad
    vector_ref[2:3, :] = bias_grad


def combine(back_a, back_b, slot, probs, middle, cot, attended, wo, router3, gain, shift, expert_count, capacity, after=()):
    tok_count, feat = cot.shape
    return call(
        functools.partial(combine_body, expert_count, capacity),
        (
            out((tok_count, feat), full_type),
            out((tok_count, feat), half_type),
            out((feat, feat), half_type),
            out((feat, LANES), full_type),
            out((3, feat), full_type),
        ),
        "combine",
        after,
        flops=4 * 10**11,
    )(back_a, back_b, slot, probs, middle, cot, attended, wo, router3, gain, shift)


def attention_grad_body(first_head, q_ref, k_ref, v_ref, grad_ref, log_big_ref, log_small_ref, first_ref, dq_ref, dk_ref, dv_ref, weight_ref, bias_ref):
    tok_count, width = q_ref.shape
    scale = 64 ** (-0.5)

    def pair(number, carry):
        lanes = pl.ds(pl.multiple_of(number * LANES, LANES), LANES)
        for place, (start, size) in enumerate(images(tok_count)):
            rows = pl.ds(start, size)
            query, key, value, grad = q_ref[rows, lanes], k_ref[rows, lanes], v_ref[rows, lanes], grad_ref[rows, lanes]
            key = key * jnp.asarray(scale, half_type)
            log_ref = (log_big_ref, log_small_ref)[place]
            key_t = key.T
            halves = []
            grad_value = jnp.zeros((size, LANES), full_type)
            grad_key = jnp.zeros((size, LANES), full_type)
            for head in range(2):
                scores = mul_t(head_lanes(key, head), query)
                if place:
                    scores = jnp.where(image_mask(size), scores, masked_score)
                probs = jnp.exp(scores - log_ref[pl.ds(first_head + 2 * number + head, 1), :])
                grad_probs = mul_t(head_lanes(value, head), grad)
                inner = jnp.sum(grad_probs * probs, axis=0, keepdims=True)
                grad_scores = (probs * (grad_probs - inner)).astype(half_type)
                grad_value = grad_value + mul(probs.astype(half_type), head_lanes(grad, head))
                grad_key = grad_key + mul(grad_scores, head_lanes(query, head))
                halves.append(mul(key_t[head * 64 : head * 64 + 64], grad_scores))
            dv_ref[rows, lanes] = grad_value.astype(half_type)
            dk_ref[rows, lanes] = (grad_key * scale).astype(half_type)
            dq_ref[rows, lanes] = jnp.concatenate(halves, axis=0).T.astype(half_type)
        return carry

    lax.fori_loop(0, width // LANES, pair, 0)
    first = first_ref[...]
    for kind, grad_ref in enumerate((dq_ref, dk_ref, dv_ref)):
        weight_ref[:, kind * width : kind * width + width] = t_mul(first, grad_ref[...]).astype(half_type)
    bias_ref[0:1, :] = jnp.sum(dq_ref[...].astype(full_type), axis=0, keepdims=True)
    bias_ref[1:2, :] = jnp.sum(dv_ref[...].astype(full_type), axis=0, keepdims=True)


def attention_grad(group, q, k, v, grad, log_big, log_small, first, after=()):
    tok_count, feat = q.shape
    width = feat // HEAD_GROUPS
    columns = pl.BlockSpec((tok_count, width), lambda i: (0, group))
    low = out((tok_count, width), half_type)
    grads = out((feat, 3 * width), half_type)
    return call(
        functools.partial(attention_grad_body, group * HEADS // HEAD_GROUPS),
        (low, low, low, grads, out((2, width), full_type)),
        f"attention_grad_{group}",
        after,
        in_specs=[columns, columns, columns, columns, whole(log_big), whole(log_small), whole(first)],
    )(q, k, v, grad, log_big, log_small, first)


def input_grad_body(*refs):
    grads = refs[: 3 * HEAD_GROUPS]
    wq_ref, wk_ref, wv_ref, tokens_ref, gain_ref, middle_ref, result_ref, vector_ref = refs[3 * HEAD_GROUPS :]
    tok_count, feat = tokens_ref.shape
    width = feat // HEAD_GROUPS
    gain_grad = jnp.zeros((1, feat), full_type)
    shift_grad = jnp.zeros((1, feat), full_type)
    for start, size in row_blocks(tok_count):
        rows = pl.ds(start, size)
        upstream = jnp.zeros((size, feat), full_type)
        for group in range(HEAD_GROUPS):
            lanes = pl.ds(group * width, width)
            for grad_ref, weight_ref in zip(grads[3 * group : 3 * group + 3], (wq_ref, wk_ref, wv_ref)):
                upstream = upstream + mul_t(grad_ref[rows, :], weight_ref[:, lanes])
        normed, inverse = normalize(tokens_ref[rows, :].astype(full_type))
        gain_grad = gain_grad + jnp.sum(upstream * normed, axis=0, keepdims=True)
        shift_grad = shift_grad + jnp.sum(upstream, axis=0, keepdims=True)
        grad = middle_ref[rows, :] + norm_backward(upstream, normed, inverse, vec(gain_ref))
        result_ref[rows, :] = grad.astype(half_type)
    vector_ref[0:1, :] = gain_grad
    vector_ref[1:2, :] = shift_grad


def input_grad(grads, wq, wk, wv, tokens, gain, grad_middle, after=()):
    tok_count, feat = tokens.shape
    return call(
        input_grad_body,
        (out((tok_count, feat), half_type), out((2, feat), full_type)),
        "input_grad",
        after,
    )(*grads, wq, wk, wv, tokens, gain, grad_middle)


def output_body(expert_count, returned_ref, slot_ref, probs_ref, middle_ref, result_ref):
    tok_count, feat = middle_ref.shape
    slots = returned_ref.shape[0]
    capacity = slots // expert_count
    half = capacity // 2
    part = half + EXTRA
    place = iota((1, slots), 1)
    within = place % capacity
    number = jnp.where(within < half, 0, expert_count * part) + place // capacity * part + within % half
    for start, size in row_blocks(tok_count):
        rows = pl.ds(start, size)
        lane = iota((size, LANES), 1)
        probs = probs_ref[rows, :]
        table = jnp.zeros((size, slots), full_type)
        for k in range(2):
            slot = slot_ref[rows, k : k + 1]
            chosen = jnp.where(slot < expert_count * part, slot, slot - expert_count * part) // part
            gate = jnp.sum(jnp.where(lane == chosen, probs, 0.0), axis=1, keepdims=True)
            table = jnp.where(number == slot, gate, table)
        high = table.astype(half_type)
        low = (table - high.astype(full_type)).astype(half_type)
        mixed = mul(high, returned_ref[...]) + mul(low, returned_ref[...])
        result_ref[rows, :] = (middle_ref[rows, :] + mixed).astype(half_type)


def block_result(returned, slot, probs, middle, expert_count, after=()):
    return call(
        functools.partial(output_body, expert_count), out(middle.shape, half_type), "block_result", after
    )(returned, slot, probs, middle)


def behind(values, *before):
    anywhere = pl.BlockSpec(memory_space=pl.ANY)
    return pl.pallas_call(
        lambda *refs: None,
        out_shape=out(values.shape, values.dtype),
        name="behind",
        in_specs=[anywhere] * (1 + len(before)),
        out_specs=anywhere,
        input_output_aliases={0: 0},
        cost_estimate=pl.CostEstimate(flops=1024, bytes_accessed=1024, transcendentals=0),
    )(values, *before)


def exchange(values, expert_count):
    split = values.reshape(expert_count, -1, values.shape[1])
    swapped = lax.all_to_all(split, "expert", split_axis=0, concat_axis=0, tiled=True)
    return swapped.reshape(values.shape)


def swap(values, axis, bit):
    count = lax.axis_size(axis)
    return lax.ppermute(values, axis, [(i, i ^ (1 << bit)) for i in range(count)])


def bits_of(axis):
    return range(lax.axis_size(axis).bit_length() - 1)


def sum_axis(values, axis):
    for bit in bits_of(axis):
        other = swap(values, axis, bit)
        values = (values.astype(full_type) + other.astype(full_type)).astype(values.dtype)
    return values


def send_blocks(values, *before):
    split = behind(values, *before).reshape(lax.axis_size("expert"), -1, values.shape[1])
    return lax.all_to_all(split, "expert", split_axis=0, concat_axis=0, tiled=True)


def sum_blocks(parts):
    return jnp.sum(parts.astype(full_type), axis=0).astype(parts.dtype)


def gather_expert(values, order):
    place = lax.axis_index("expert")
    shape = values.shape
    values = values.reshape((1,) * len(order) + shape)
    for bit in order:
        axis = len(order) - 1 - bit
        other = swap(values, "expert", bit)
        own = (place >> bit) & 1
        values = jnp.where(
            own == 0, jnp.concatenate([values, other], axis=axis), jnp.concatenate([other, values], axis=axis)
        )
    return values.reshape(-1, shape[1])


def own_part(values):
    size = values.shape[1] // lax.axis_size("dp")
    return lax.dynamic_slice_in_dim(values, lax.axis_index("dp") * size, size, 1)


def shards(
    tokens,
    first_gain,
    first_shift,
    query_weight,
    query_bias,
    key_weight,
    value_weight,
    value_bias,
    out_weight,
    out_bias,
    second_gain,
    second_shift,
    router,
    expert_up,
    expert_up_bias,
    expert_down,
    expert_down_bias,
    choices,
    priority,
    cotangent,
):
    tok_count, feat = tokens.shape
    expert_count = lax.axis_size("expert")
    capacity = (21 * tok_count + 80 * expert_count - 1) // (80 * expert_count) * 8
    router3 = jnp.pad(jnp.concatenate([router] * 3, axis=1), ((0, 0), (0, LANES - 3 * expert_count)))
    up, down = expert_up[0], expert_down[0]

    place, slot, cot_sent = route(choices.T, priority, cotangent, expert_count, capacity)
    cot = exchange(cot_sent, expert_count)
    first, q, k, v, log_big, log_small, attended, middle, _, probs, sent_a, sent_b = front(
        tokens,
        (first_gain, first_shift, query_bias, value_bias, out_bias, second_gain, second_shift),
        (query_weight, key_weight, value_weight, out_weight),
        router3,
        place,
        expert_count,
        capacity,
    )
    rows_a = exchange(behind(sent_a, cot), expert_count)
    grad_act, start = act_grad(cot, down, expert_down_bias, expert_count)
    rows_b = exchange(behind(sent_b, rows_a, start), expert_count)
    cot_parts = cot.reshape(expert_count, 2, capacity // 2, feat)
    earlier = expert(0, rows_a, up, expert_up_bias, grad_act, start, cot_parts)
    back_a = exchange(earlier[4], expert_count)
    act, grad_pre, gated, grad_rows, grad_in_b = expert(1, rows_b, up, expert_up_bias, grad_act, start, cot_parts, earlier)
    replicas = lax.axis_size("dp")
    grad_in_b = behind(grad_in_b, back_a)
    weight_part, up_bias_part, down_bias_part = weight_grad(
        act, grad_pre, gated, grad_rows, earlier[5], replicas, (back_a, grad_in_b)
    )
    expert_sum = lax.psum_scatter(weight_part, "dp", scatter_dimension=0, tiled=True)[0]
    back_b = exchange(grad_in_b, expert_count)
    grad_middle, grad_attended, wo_grad, router_part, second_parts = combine(
        back_a,
        back_b,
        slot,
        probs,
        middle,
        cotangent,
        attended,
        out_weight,
        router3,
        second_gain,
        second_shift,
        expert_count,
        capacity,
        (weight_part,),
    )
    parts = [send_blocks(wo_grad, back_b)]
    grads, bias_parts = [], []
    for group in range(HEAD_GROUPS):
        dq, dk, dv, group_part, bias_part = attention_grad(
            group, q, k, v, grad_attended, log_big, log_small, first, tuple(grads[-1:])
        )
        grads += [dq, dk, dv]
        bias_parts.append(bias_part)
        parts.append(send_blocks(group_part, parts[-1]))
    bias_part = jnp.concatenate(bias_parts, axis=1)
    result = expert_result(act, down, expert_down_bias, expert_count, (grads[-1], parts[0]))
    returned = exchange(behind(result, parts[-1]), expert_count)
    token_grad, first_parts = input_grad(
        grads, query_weight, key_weight, value_weight, tokens, first_gain, grad_middle, (result, parts[1])
    )
    block_output = block_result(returned, slot, probs, middle, expert_count, (token_grad,))
    hidden = up.shape[1]
    bias_sum = sum_axis(jnp.concatenate([up_bias_part, down_bias_part], axis=1), "dp")
    expert_up_bias_grad, expert_down_bias_grad = own_part(bias_sum[:, :hidden]), own_part(bias_sum[:, hidden:])
    router_rows = router_part[:, :expert_count].reshape(-1, feat)
    vectors = jnp.concatenate([first_parts, bias_part, second_parts, router_rows])
    vectors = sum_axis(sum_axis(vectors, "expert"), "dp")
    parts = [sum_blocks(part) for part in parts]
    high_bits = list(bits_of("expert"))[1:]
    early = gather_expert(sum_axis(jnp.concatenate(parts[:2], axis=1), "dp"), high_bits + [0])
    late = gather_expert(sum_axis(parts[2], "dp"), high_bits[::-1] + [0])
    out_weight_grad = early[:, :feat].astype(full_type)
    width = feat // HEAD_GROUPS
    weight_grads = []
    for kind in range(3):
        pieces = [total[:, kind * width : kind * width + width] for total in (early[:, feat:], late)]
        weight_grads.append(jnp.concatenate(pieces, axis=1).astype(full_type))
    share, steps = feat // replicas, up.shape[1] // feat
    expert_up_grad = jnp.concatenate([expert_sum[c * share : c * share + share] for c in range(steps)], axis=1)
    expert_up_grad = expert_up_grad.astype(full_type)[None]
    expert_down_grad = expert_sum[steps * share :].astype(full_type)[None]
    return (
        block_output,
        token_grad,
        vectors[0],
        vectors[1],
        weight_grads[0],
        vectors[2],
        weight_grads[1],
        weight_grads[2],
        vectors[3],
        out_weight_grad,
        vectors[6],
        vectors[4],
        vectors[5],
        vectors[7:].reshape(feat, expert_count),
        expert_up_grad,
        expert_up_bias_grad,
        expert_down_grad,
        expert_down_bias_grad,
    )


def solution(mesh):
    tokens_spec = P(("dp", "expert"), None)
    return jax.shard_map(
        shards,
        mesh=mesh,
        in_specs=(tokens_spec,)
        + (P(),) * 12
        + (P("expert", None, None), P("expert", None), P("expert", None, None), P("expert", None))
        + (tokens_spec,) * 3,
        out_specs=(tokens_spec,) * 2
        + (P(),) * 12
        + (P("expert", "dp", None), P("expert", "dp"), P("expert", "dp", None), P("expert", "dp")),
        check_vma=False,
    )
```

```python
import functools

import jax
import jax.numpy as jnp
from jax import lax
from jax.experimental import pallas as pl
from jax.experimental.pallas import tpu as pltpu
from jax.sharding import PartitionSpec as P

HEADS = 12
BIG = 576
SMALL = 196
LANES = 128
EXTRA = 16
HEAD_GROUPS = 2

half_type = jnp.bfloat16
full_type = jnp.float32
norm_eps = 1e-06
masked_score = -1000000000.0
vmem_bytes = 56 * 2**20


def dot_full(left, right, dims):
    return lax.dot_general(left, right, (dims, ((), ())), preferred_element_type=full_type)


def mul(left, right):
    return dot_full(left, right, ((1,), (0,)))


def mul_t(left, right):
    return dot_full(left, right, ((1,), (1,)))


def t_mul(left, right):
    return dot_full(left, right, ((0,), (0,)))


def row_blocks(rows, step=256):
    return [(start, min(step, rows - start)) for start in range(0, rows, step)]


def iota(shape, dim):
    return lax.broadcasted_iota(jnp.int32, shape, dim)


def ones_where(mask):
    return jnp.where(mask, 1.0, 0.0).astype(half_type)


def normalize(values):
    row_mean = jnp.mean(values, axis=-1, keepdims=True)
    centered = values - row_mean
    inverse = lax.rsqrt(jnp.mean(centered * centered, axis=-1, keepdims=True) + norm_eps)
    return centered * inverse, inverse


def norm_backward(upstream, normed, inverse, norm_gain):
    scaled = upstream * norm_gain
    first_mean = jnp.mean(scaled, axis=-1, keepdims=True)
    second_mean = jnp.mean(scaled * normed, axis=-1, keepdims=True)
    return inverse * (scaled - first_mean - normed * second_mean)


def split_thirds(values, lane, expert_count):
    high = values.astype(half_type).astype(full_type)
    rest = values - high
    middle = rest.astype(half_type).astype(full_type)
    low = rest - middle
    picked = jnp.where(lane < expert_count, high, jnp.where(lane < 2 * expert_count, middle, low))
    return jnp.where(lane < 3 * expert_count, picked, 0.0).astype(half_type)


def call(body, out_shape, name, after=(), grid=(1,), in_specs=None, flops=1024, **kwargs):
    def build(*operands):
        specs = list(in_specs) if in_specs else [whole(a) for a in operands]
        used = len(specs)
        if "out_specs" not in kwargs:
            kwargs["out_specs"] = jax.tree.map(whole, out_shape)

        def inner(*refs):
            body(*refs[:used], *refs[used + len(after) :])

        return pl.pallas_call(
            inner,
            out_shape=out_shape,
            name=name,
            grid=grid,
            in_specs=specs + [pl.BlockSpec(memory_space=pl.ANY)] * len(after),
            compiler_params=pltpu.CompilerParams(vmem_limit_bytes=vmem_bytes),
            cost_estimate=pl.CostEstimate(flops=flops, bytes_accessed=1024, transcendentals=0),
            **kwargs,
        )(*operands, *after)

    return build


def whole(array):
    zeros = (0,) * len(array.shape)
    return pl.BlockSpec(array.shape, lambda *_: zeros)


def out(shape, dtype):
    return jax.ShapeDtypeStruct(shape, dtype)


def vec(ref):
    return ref[...].reshape(1, -1)


def for_experts(expert_count, step):
    if expert_count <= 8:
        for e in range(expert_count):
            step(e)
    else:
        lax.fori_loop(0, expert_count, lambda e, c: (step(e), c)[1], 0)


def expert_rows(e, capacity):
    if isinstance(e, int):
        return pl.ds(e * capacity, capacity)
    return pl.ds(pl.multiple_of(e * capacity, capacity), capacity)


def row_thirds(row):
    high = row.astype(half_type).astype(full_type)
    rest = row - high
    middle = rest.astype(half_type).astype(full_type)
    sub = iota((8, row.shape[1]), 0)
    picked = jnp.where(sub == 0, high, jnp.where(sub == 1, middle, jnp.where(sub == 2, rest - middle, 0.0)))
    return picked.astype(half_type)


def thirds_to_lanes(thirds):
    return t_mul(thirds, jnp.ones((thirds.shape[0], LANES), half_type))


def store_thirds(ref, start, row):
    ref[pl.ds(start, EXTRA), :] = jnp.zeros((EXTRA, ref.shape[1]), ref.dtype)
    thirds = jnp.concatenate([row_thirds(row), jnp.zeros((EXTRA - 8, row.shape[1]), half_type)], axis=0)
    ref[pl.ds(start, EXTRA), 0 : row.shape[1]] = thirds


def part_start(e, size, offset=0):
    if isinstance(e, int):
        return e * size + offset
    return pl.multiple_of(e * size + offset, 16)


def lanes_to_row(values):
    ones = jnp.ones((8, LANES), half_type)
    high = values.astype(half_type)
    rest = values - high.astype(full_type)
    middle = rest.astype(half_type)
    low = (rest - middle.astype(full_type)).astype(half_type)
    return (mul_t(ones, high) + mul_t(ones, middle) + mul_t(ones, low))[0:1]


def rank_column(rows):
    tok_count = rows.shape[1]
    rows = jnp.concatenate([rows, jnp.zeros((8 - rows.shape[0], tok_count), jnp.int32)], axis=0)
    return rows.astype(full_type).T.astype(jnp.int32)


def route_body(expert_count, capacity, rows_ref, rank_ref, cot_ref, place_ref, sent_ref):
    tok_count = cot_ref.shape[0]
    padded = place_ref.shape[0]
    sub = iota((padded, tok_count), 0)
    first, second = rows_ref[0:1, :], rows_ref[1:2, :]
    first_hot, second_hot = ones_where(first == sub), ones_where(second == sub)
    earlier = ones_where(rank_column(rank_ref[...])[:, 0:1] < rank_ref[...])
    first_total = jnp.sum(first_hot.astype(full_type), axis=1, keepdims=True)
    counts = mul(jnp.concatenate([first_hot, second_hot], axis=0), earlier)
    first_count, second_count = counts[:padded], counts[padded:] + first_total
    place = jnp.where(
        (first == sub) & (first_count < capacity),
        first_count,
        jnp.where((second == sub) & (second_count < capacity), second_count, -1.0),
    )
    place_ref[...] = place.astype(jnp.int32)
    cot = cot_ref[...]
    within = iota((capacity, tok_count), 0)

    def send(e):
        hot = ones_where(place_ref[pl.ds(e, 1), :] == within)
        sent_ref[pl.ds(part_start(e, capacity), capacity), :] = mul(hot, cot).astype(half_type)

    for_experts(expert_count, send)


def route(choice_rows, priority, cotangent, expert_count, capacity):
    tok_count, feat = cotangent.shape
    padded = -(-expert_count // 32) * 32
    return call(
        functools.partial(route_body, expert_count, capacity),
        (out((padded, tok_count), jnp.int32), out((expert_count * capacity, feat), half_type)),
        "route",
    )(choice_rows, priority, cotangent)


def slots_body(capacity, rows_ref, place_ref, slot_ref):
    part = capacity + EXTRA
    padded, tok_count = place_ref.shape
    sub = iota((padded, tok_count), 0)
    slots = []
    for k in range(2):
        place = jnp.sum(jnp.where(rows_ref[k : k + 1, :] == sub, place_ref[...], 0), axis=0, keepdims=True)
        slots.append(jnp.where(place < 0, -1, rows_ref[k : k + 1, :] * part + place))
    slot_ref[...] = rank_column(jnp.concatenate(slots, axis=0))[:, 0:2]


def slot_columns(choice_rows, place, capacity, after):
    return call(
        functools.partial(slots_body, capacity), out((choice_rows.shape[1], 2), jnp.int32), "slot_columns", after
    )(choice_rows, place)


def image_mask(size):
    key_image = iota((size, 1), 0) // SMALL
    query_image = iota((1, size), 1) // SMALL
    return key_image == query_image


def images(tok_count):
    return ((0, BIG), (BIG, tok_count - BIG))


def head_lanes(value, head):
    lane = iota((1, LANES), 1)
    return jnp.where((lane < LANES // 2) == (head == 0), value, jnp.zeros((), value.dtype))


def front_body(
    expert_count,
    capacity,
    tokens_ref,
    gain_ref,
    shift_ref,
    wq_ref,
    bq_ref,
    wk_ref,
    wv_ref,
    bv_ref,
    wo_ref,
    bo_ref,
    gain2_ref,
    shift2_ref,
    router_ref,
    place_ref,
    first_ref,
    q_ref,
    k_ref,
    v_ref,
    log_big_ref,
    log_small_ref,
    attended_ref,
    middle_ref,
    second_ref,
    probs_ref,
    sent_ref,
):
    tok_count, feat = tokens_ref.shape
    scale = (feat // HEADS) ** (-0.5)
    for start, size in row_blocks(tok_count):
        rows = pl.ds(start, size)
        normed, _ = normalize(tokens_ref[rows, :].astype(full_type))
        low = (normed * vec(gain_ref) + vec(shift_ref)).astype(half_type)
        first_ref[rows, :] = low
        q_ref[rows, :] = (mul(low, wq_ref[...]) + vec(bq_ref)).astype(half_type)
        k_ref[rows, :] = mul(low, wk_ref[...]).astype(half_type)
        v_ref[rows, :] = (mul(low, wv_ref[...]) + vec(bv_ref)).astype(half_type)

    def pair(number, carry):
        lanes = pl.ds(pl.multiple_of(number * LANES, LANES), LANES)
        for place, (start, size) in enumerate(images(tok_count)):
            rows = pl.ds(start, size)
            query, key, value = q_ref[rows, lanes], k_ref[rows, lanes], v_ref[rows, lanes]
            key = key * jnp.asarray(scale, half_type)
            log_ref = (log_big_ref, log_small_ref)[place]
            value_t = value.T
            halves = []
            for head in range(2):
                scores = mul_t(head_lanes(key, head), query)
                if place:
                    scores = jnp.where(image_mask(size), scores, masked_score)
                top = jnp.max(scores, axis=0, keepdims=True)
                weights = jnp.exp(scores - top)
                total = jnp.sum(weights, axis=0, keepdims=True)
                log_ref[pl.ds(2 * number + head, 1), :] = top + jnp.log(total)
                mixed = mul(value_t[head * 64 : head * 64 + 64], weights.astype(half_type))
                halves.append(mixed * (1.0 / total))
            attended_ref[rows, lanes] = jnp.concatenate(halves, axis=0).T.astype(half_type)
        return carry

    lax.fori_loop(0, HEADS // 2, pair, 0)

    for start, size in row_blocks(tok_count):
        rows = pl.ds(start, size)
        lane = iota((size, LANES), 1)
        middle = tokens_ref[rows, :].astype(full_type) + mul(attended_ref[rows, :], wo_ref[...]) + vec(bo_ref)
        middle_ref[rows, :] = middle
        normed, _ = normalize(middle)
        low = (normed * vec(gain2_ref) + vec(shift2_ref)).astype(half_type)
        second_ref[rows, :] = low
        logits = jnp.where(lane < 3 * expert_count, mul(low, router_ref[...]), masked_score)
        top = jnp.max(logits, axis=1, keepdims=True)
        raised = jnp.exp(logits - top)
        total = jnp.sum(jnp.where(lane < expert_count, raised, 0.0), axis=1, keepdims=True)
        probs_ref[rows, :] = raised / total

    low = second_ref[...]
    lane = iota((tok_count, LANES), 1)
    thirds = split_thirds(probs_ref[...], lane, expert_count)
    within = iota((capacity, tok_count), 0)
    slot_lane = iota((capacity, LANES), 1)

    def send(e):
        hot = ones_where(place_ref[pl.ds(e, 1), :] == within)
        rows = mul(hot, low).astype(half_type)
        part = capacity + EXTRA
        sent_ref[pl.ds(part_start(e, part), capacity), :] = rows
        gates = mul(hot, thirds)
        own = (slot_lane == e) | (slot_lane == e + expert_count) | (slot_lane == e + 2 * expert_count)
        picked = jnp.where(own, gates, 0.0).astype(half_type)
        store_thirds(sent_ref, part_start(e, part, capacity), mul_t(jnp.ones((8, LANES), half_type), picked)[0:1])

    for_experts(expert_count, send)


def front(tokens, vectors, weights, router3, place, expert_count, capacity):
    tok_count, feat = tokens.shape
    gain, shift, bq, bv, bo, gain2, shift2 = vectors
    wq, wk, wv, wo = weights
    low = out((tok_count, feat), half_type)
    return call(
        functools.partial(front_body, expert_count, capacity),
        (
            low,
            low,
            low,
            low,
            out((HEADS, BIG), full_type),
            out((HEADS, tok_count - BIG), full_type),
            low,
            out((tok_count, feat), full_type),
            low,
            out((tok_count, LANES), full_type),
            out((expert_count * (capacity + EXTRA), feat), half_type),
        ),
        "front",
    )(tokens, gain, shift, wq, bq, wk, wv, bv, wo, bo, gain2, shift2, router3, place)


def fold_lanes(values):
    folded = values[:, :LANES]
    for start in range(LANES, values.shape[1], LANES):
        folded = folded + values[:, start : start + LANES]
    return folded


def act_grad_body(cot_ref, down_ref, down_bias_ref, grad_act_ref, score_ref):
    for start, size in row_blocks(cot_ref.shape[0], 512):
        rows = pl.ds(start, size)
        grad_act_ref[rows, :] = mul_t(cot_ref[rows, :], down_ref[...]).astype(half_type)

        @pl.when(pl.program_id(0) == 0)
        def _():
            score_ref[rows, :] = fold_lanes(cot_ref[rows, :].astype(full_type) * down_bias_ref[...])


def act_grad(cot, down, down_bias, step=512):
    slots, feat = cot.shape
    hidden = down.shape[0]
    return call(
        act_grad_body,
        (out((slots, hidden), half_type), out((slots, LANES), full_type)),
        "act_grad",
        grid=(hidden // step,),
        in_specs=[whole(cot), pl.BlockSpec((step, feat), lambda f: (f, 0)), whole(down_bias)],
        out_specs=[pl.BlockSpec((slots, step), lambda f: (0, f)), pl.BlockSpec((slots, LANES), lambda f: (0, 0))],
    )(cot, down, down_bias)


def gelu_parts(values):
    area = 0.5 + 0.5 * lax.erf(values * 0.7071067811865476)
    bell = jnp.exp(values * values * -0.5) * 0.3989422804014327
    return values * area, area + values * bell


def expert_body(rows_ref, up_ref, up_bias_ref, grad_act_ref, start_ref, cot_ref, act_ref, grad_pre_ref, gate_ref, score_ref, sum_ref, x_ref, gated_ref, grad_ref, bias_ref, up_out_ref, down_out_ref, sems):
    slots, feat = cot_ref.shape
    replicas, share = up_out_ref.shape[1:3]
    steps = (sum_ref.shape[1] - EXTRA) // share // 2
    part = rows_ref.shape[0] // (rows_ref.shape[0] - slots) * EXTRA
    capacity = part - EXTRA
    number = pl.program_id(0)
    down_rows = steps * share
    size = min(down_rows, feat)

    def copies(step):
        pairs = [(up_out_ref.at[step % 2], sum_ref.at[:, pl.ds(step * share, share), :])]
        for piece in range(feat // size):
            row = step * feat + piece * size
            target = sum_ref.at[row // down_rows, pl.ds(down_rows + row % down_rows, size), :]
            pairs.append((down_out_ref.at[step % 2, pl.ds(piece * size, size)], target))
        return [pltpu.make_async_copy(a, b, sems.at[step, i]) for i, (a, b) in enumerate(pairs)]

    @pl.when(number == 0)
    def _():
        total = jnp.zeros((1, feat), full_type)
        for e in range(slots // capacity):
            rows = pl.ds(e * capacity, capacity)
            gate = thirds_to_lanes(rows_ref[pl.ds(e * part + capacity, EXTRA), 0:capacity])
            gate_ref[rows, :] = gate
            wide = jnp.concatenate([gate] * (feat // LANES), axis=1)
            x = rows_ref[pl.ds(e * part, capacity), :]
            x_ref[rows, :] = x
            gated_ref[rows, :] = (x.astype(full_type) * wide).astype(half_type)
            grad = (cot_ref[rows, :].astype(full_type) * wide).astype(half_type)
            grad_ref[rows, :] = grad
            total = total + jnp.sum(grad.astype(full_type), axis=0, keepdims=True)
        bias_ref[...] = jnp.zeros(bias_ref.shape, half_type)
        for z in range(replicas):
            bias_ref[z, 8:9, 0:share] = total[:, z * share : z * share + share].astype(half_type)
        score_ref[...] = start_ref[...]

    blocks = row_blocks(slots, 512)
    pre = mul(x_ref[pl.ds(*blocks[0]), :], up_ref[...])
    bias_grad = jnp.zeros((1, feat), full_type)
    for b, block in enumerate(blocks):
        rows = pl.ds(*block)
        if b + 1 < len(blocks):
            later = mul(x_ref[pl.ds(*blocks[b + 1]), :], up_ref[...])
        act, slope = gelu_parts(pre + up_bias_ref[...])
        act_ref[rows, :] = act.astype(half_type)
        grad_act = grad_act_ref[rows, :].astype(full_type)
        score_ref[rows, :] += fold_lanes(act * grad_act)
        grad_pre_ref[rows, :] = (grad_act * slope).astype(half_type)
        pre = later
    for step in range(2, steps):

        @pl.when(number == step)
        def _():
            for copy in copies(step - 2):
                copy.wait()

    up_out_ref[number % 2] = t_mul(gated_ref[...], grad_pre_ref[...]).astype(half_type).reshape(replicas, share, feat)
    down_out_ref[number % 2] = t_mul(act_ref[...], grad_ref[...]).astype(half_type)
    for start, size_b in blocks:
        rows = pl.ds(start, size_b)
        wide = jnp.concatenate([gate_ref[rows, :]] * (feat // LANES), axis=1)
        bias_grad = bias_grad + jnp.sum(grad_pre_ref[rows, :].astype(full_type) * wide, axis=0, keepdims=True)
    for step in range(steps):

        @pl.when(number == step)
        def _():
            for piece in range(feat // size):
                z = (step * feat + piece * size) // down_rows
                bias_ref[z, 0:1, 0:size] = bias_grad[:, piece * size : piece * size + size].astype(half_type)
            for copy in copies(step):
                copy.start()

    @pl.when(number == steps - 1)
    def _():
        last = pltpu.make_async_copy(bias_ref, sum_ref.at[:, pl.ds(2 * down_rows, EXTRA), :], sems.at[0, 0])
        last.start()
        score_ref[...] = score_ref[...] * gate_ref[...]
        for step in range(steps - 2, steps):
            for copy in copies(step):
                copy.wait()
        last.wait()


def expert(rows, up, up_bias, grad_act, start, cot, replicas):
    slots, feat = cot.shape
    hidden = up.shape[1]
    steps, share = hidden // feat, feat // replicas
    wide = pl.BlockSpec((slots, feat), lambda f: (0, f))
    once = lambda a: pl.BlockSpec(a.shape, lambda f: (0, 0), pipeline_mode=pl.Buffered(1))
    lanes = out((slots, LANES), full_type)
    return call(
        expert_body,
        (
            out((slots, hidden), half_type),
            out((slots, hidden), half_type),
            lanes,
            lanes,
            out((replicas, 2 * steps * share + EXTRA, feat), half_type),
        ),
        "expert",
        grid=(steps,),
        in_specs=[
            once(rows),
            pl.BlockSpec((feat, feat), lambda f: (0, f)),
            pl.BlockSpec((1, feat), lambda f: (0, f)),
            wide,
            once(start),
            once(cot),
        ],
        out_specs=[
            wide,
            wide,
            whole(lanes),
            whole(lanes),
            pl.BlockSpec(memory_space=pl.ANY),
        ],
        scratch_shapes=[
            pltpu.VMEM((slots, feat), half_type),
            pltpu.VMEM((slots, feat), half_type),
            pltpu.VMEM((slots, feat), half_type),
            pltpu.VMEM((replicas, EXTRA, feat), half_type),
            pltpu.VMEM((2, replicas, share, feat), half_type),
            pltpu.VMEM((2, feat, feat), half_type),
            pltpu.SemaphoreType.DMA((steps, 1 + max(1, feat // (steps * share)))),
        ],
    )(rows, up, up_bias, grad_act, start, cot)


def grad_in_body(capacity, grad_pre_ref, up_ref, gate_ref, score_ref, grad_in_ref):
    part = capacity + EXTRA
    size, feat = grad_pre_ref.shape[0], up_ref.shape[0]
    grad = mul_t(grad_pre_ref[...], up_ref[...])
    grad = grad * jnp.concatenate([gate_ref[...]] * (feat // LANES), axis=1)
    for e in range(size // capacity):
        grad_in_ref[pl.ds(e * part, capacity), :] = grad[e * capacity : e * capacity + capacity].astype(half_type)
        store_thirds(grad_in_ref, e * part + capacity, lanes_to_row(score_ref[e * capacity : e * capacity + capacity, :]))


def expert_grad_in(grad_pre, up, gate, score, capacity, after, step=512):
    slots, hidden = grad_pre.shape
    feat = up.shape[0]
    part = capacity + EXTRA
    lanes = pl.BlockSpec((step, LANES), lambda r: (r, 0))
    return call(
        functools.partial(grad_in_body, capacity),
        out((slots // capacity * part, feat), half_type),
        "grad_in",
        after,
        flops=4 * 10**11,
        grid=(slots // step,),
        in_specs=[pl.BlockSpec((step, hidden), lambda r: (r, 0)), whole(up), lanes, lanes],
        out_specs=pl.BlockSpec((step // capacity * part, feat), lambda r: (r, 0)),
    )(grad_pre, up, gate, score)


def result_body(act_ref, down_ref, down_bias_ref, result_ref):
    result_ref[...] = (mul(act_ref[...], down_ref[...]) + down_bias_ref[...]).astype(half_type)


def expert_result(act, down, down_bias, after=(), step=512):
    slots, hidden = act.shape
    feat = down.shape[1]
    return call(
        result_body,
        out((slots, feat), half_type),
        "result",
        after,
        grid=(slots // step,),
        in_specs=[pl.BlockSpec((step, hidden), lambda r: (r, 0)), whole(down), whole(down_bias)],
        out_specs=pl.BlockSpec((step, feat), lambda r: (r, 0)),
    )(act, down, down_bias)


def combine_body(
    expert_count,
    capacity,
    back_ref,
    slot_ref,
    probs_ref,
    middle_ref,
    cot_ref,
    attended_ref,
    wo_ref,
    router_ref,
    gain_ref,
    shift_ref,
    grad_middle_ref,
    grad_attended_ref,
    wo_grad_ref,
    router_grad_ref,
    vector_ref,
):
    tok_count, feat = cot_ref.shape
    slots = back_ref.shape[0]
    part = capacity + EXTRA
    lane = iota((capacity, LANES), 1)
    tables = []
    for e in range(expert_count):
        same = (lane == e) | (lane == e + expert_count) | (lane == e + 2 * expert_count)
        score = thirds_to_lanes(back_ref[pl.ds(e * part + capacity, EXTRA), 0:capacity])
        tables.append(split_thirds(jnp.where(same, score, 0.0), lane, expert_count))
        tables.append(jnp.zeros((EXTRA, LANES), half_type))
    table = jnp.concatenate(tables, axis=0)
    wo_grad = jnp.zeros(wo_grad_ref.shape, full_type)
    router_grad = jnp.zeros(router_grad_ref.shape, full_type)
    gain_grad = jnp.zeros((1, feat), full_type)
    shift_grad = jnp.zeros((1, feat), full_type)
    bias_grad = jnp.zeros((1, feat), full_type)
    for start, size in row_blocks(tok_count):
        rows = pl.ds(start, size)
        number = iota((size, slots), 1)
        hot = ones_where((number == slot_ref[rows, 0:1]) | (number == slot_ref[rows, 1:2]))
        lane = iota((size, LANES), 1)
        folded = mul(hot, table)
        folded = folded + pltpu.roll(folded, LANES - expert_count, 1) + pltpu.roll(folded, LANES - 2 * expert_count, 1)
        probs = jnp.where(lane < expert_count, probs_ref[rows, :], 0.0)
        scores = jnp.where(lane < expert_count, folded, 0.0)
        grad_logits = scores - probs * jnp.sum(scores, axis=1, keepdims=True)
        grad_logits = grad_logits + pltpu.roll(grad_logits, expert_count, 1) + pltpu.roll(grad_logits, 2 * expert_count, 1)
        thirds = split_thirds(grad_logits, lane, expert_count)
        upstream = mul_t(thirds, router_ref[...]) + mul(hot, back_ref[...])
        normed, inverse = normalize(middle_ref[rows, :])
        low = (normed * vec(gain_ref) + vec(shift_ref)).astype(half_type)
        router_grad = router_grad + t_mul(low, thirds)
        gain_grad = gain_grad + jnp.sum(upstream * normed, axis=0, keepdims=True)
        shift_grad = shift_grad + jnp.sum(upstream, axis=0, keepdims=True)
        grad_middle = cot_ref[rows, :].astype(full_type) + norm_backward(upstream, normed, inverse, vec(gain_ref))
        grad_middle_ref[rows, :] = grad_middle
        branch = grad_middle.astype(half_type)
        bias_grad = bias_grad + jnp.sum(branch.astype(full_type), axis=0, keepdims=True)
        grad_attended_ref[rows, :] = mul_t(branch, wo_ref[...]).astype(half_type)
        wo_grad = wo_grad + t_mul(attended_ref[rows, :], branch)
    wo_grad_ref[...] = wo_grad.astype(half_type)
    router_grad = router_grad + pltpu.roll(router_grad, LANES - expert_count, 1) + pltpu.roll(router_grad, LANES - 2 * expert_count, 1)
    router_grad_ref[...] = router_grad
    vector_ref[0:1, :] = gain_grad
    vector_ref[1:2, :] = shift_grad
    vector_ref[2:3, :] = bias_grad


def combine(back, slot, probs, middle, cot, attended, wo, router3, gain, shift, expert_count, capacity, after=()):
    tok_count, feat = cot.shape
    return call(
        functools.partial(combine_body, expert_count, capacity),
        (
            out((tok_count, feat), full_type),
            out((tok_count, feat), half_type),
            out((feat, feat), half_type),
            out((feat, LANES), full_type),
            out((3, feat), full_type),
        ),
        "combine",
        after,
    )(back, slot, probs, middle, cot, attended, wo, router3, gain, shift)


def attention_grad_body(first_head, q_ref, k_ref, v_ref, grad_ref, log_big_ref, log_small_ref, first_ref, dq_ref, dk_ref, dv_ref, weight_ref, bias_ref):
    tok_count, width = q_ref.shape
    scale = 64 ** (-0.5)

    def pair(number, carry):
        lanes = pl.ds(pl.multiple_of(number * LANES, LANES), LANES)
        for place, (start, size) in enumerate(images(tok_count)):
            rows = pl.ds(start, size)
            query, key, value, grad = q_ref[rows, lanes], k_ref[rows, lanes], v_ref[rows, lanes], grad_ref[rows, lanes]
            key = key * jnp.asarray(scale, half_type)
            log_ref = (log_big_ref, log_small_ref)[place]
            key_t = key.T
            halves = []
            grad_value = jnp.zeros((size, LANES), full_type)
            grad_key = jnp.zeros((size, LANES), full_type)
            for head in range(2):
                scores = mul_t(head_lanes(key, head), query)
                if place:
                    scores = jnp.where(image_mask(size), scores, masked_score)
                probs = jnp.exp(scores - log_ref[pl.ds(first_head + 2 * number + head, 1), :])
                grad_probs = mul_t(head_lanes(value, head), grad)
                inner = jnp.sum(grad_probs * probs, axis=0, keepdims=True)
                grad_scores = (probs * (grad_probs - inner)).astype(half_type)
                grad_value = grad_value + mul(probs.astype(half_type), head_lanes(grad, head))
                grad_key = grad_key + mul(grad_scores, head_lanes(query, head))
                halves.append(mul(key_t[head * 64 : head * 64 + 64], grad_scores))
            dv_ref[rows, lanes] = grad_value.astype(half_type)
            dk_ref[rows, lanes] = (grad_key * scale).astype(half_type)
            dq_ref[rows, lanes] = jnp.concatenate(halves, axis=0).T.astype(half_type)
        return carry

    lax.fori_loop(0, width // LANES, pair, 0)
    first = first_ref[...]
    for kind, grad_ref in enumerate((dq_ref, dk_ref, dv_ref)):
        weight_ref[:, kind * width : kind * width + width] = t_mul(first, grad_ref[...]).astype(half_type)
    bias_ref[0:1, :] = jnp.sum(dq_ref[...].astype(full_type), axis=0, keepdims=True)
    bias_ref[1:2, :] = jnp.sum(dv_ref[...].astype(full_type), axis=0, keepdims=True)


def attention_grad(group, q, k, v, grad, log_big, log_small, first, after=()):
    tok_count, feat = q.shape
    width = feat // HEAD_GROUPS
    columns = pl.BlockSpec((tok_count, width), lambda i: (0, group))
    low = out((tok_count, width), half_type)
    grads = out((feat, 3 * width + (LANES if group == HEAD_GROUPS - 1 else 0)), half_type)
    return call(
        functools.partial(attention_grad_body, group * HEADS // HEAD_GROUPS),
        (low, low, low, grads, out((2, width), full_type)),
        f"attention_grad_{group}",
        after,
        in_specs=[columns, columns, columns, columns, whole(log_big), whole(log_small), whole(first)],
    )(q, k, v, grad, log_big, log_small, first)


def input_grad_body(*refs):
    grads = refs[: 3 * HEAD_GROUPS]
    refs = refs[3 * HEAD_GROUPS :]
    wq_ref, wk_ref, wv_ref, tokens_ref, gain_ref, middle_ref, bias_a_ref, bias_b_ref, second_ref, router_ref = refs[:10]
    result_ref, sums_ref = refs[11:]
    tok_count, feat = tokens_ref.shape
    width = feat // HEAD_GROUPS
    gain_grad = jnp.zeros((1, feat), full_type)
    shift_grad = jnp.zeros((1, feat), full_type)
    for start, size in row_blocks(tok_count):
        rows = pl.ds(start, size)
        upstream = jnp.zeros((size, feat), full_type)
        for group in range(HEAD_GROUPS):
            lanes = pl.ds(group * width, width)
            for grad_ref, weight_ref in zip(grads[3 * group : 3 * group + 3], (wq_ref, wk_ref, wv_ref)):
                upstream = upstream + mul_t(grad_ref[rows, :], weight_ref[:, lanes])
        normed, inverse = normalize(tokens_ref[rows, :].astype(full_type))
        gain_grad = gain_grad + jnp.sum(upstream * normed, axis=0, keepdims=True)
        shift_grad = shift_grad + jnp.sum(upstream, axis=0, keepdims=True)
        grad = middle_ref[rows, :] + norm_backward(upstream, normed, inverse, vec(gain_ref))
        result_ref[rows, :] = grad.astype(half_type)
    biases = jnp.concatenate([bias_a_ref[...], bias_b_ref[...]], axis=1)
    vectors = [jnp.zeros((32, feat), full_type), gain_grad, shift_grad, biases, second_ref[...]]
    vectors.append(jnp.zeros((LANES - 39, feat), full_type))
    columns = jnp.concatenate(vectors, axis=0).T
    lane = iota(columns.shape, 1)
    sums_ref[...] = jnp.where(lane < 32, router_ref[...], columns).astype(half_type)


def input_grad(grads, wq, wk, wv, tokens, gain, grad_middle, bias_parts, second_parts, router_part, sums, after):
    tok_count, feat = tokens.shape
    operands = (*grads, wq, wk, wv, tokens, gain, grad_middle, *bias_parts, second_parts, router_part)
    block = sums.shape[1] // LANES - 1
    return call(
        input_grad_body,
        (out((tok_count, feat), half_type), out(sums.shape, half_type)),
        "input_grad",
        after,
        in_specs=[whole(a) for a in operands] + [pl.BlockSpec(memory_space=pl.ANY)],
        out_specs=[pl.BlockSpec((tok_count, feat), lambda i: (0, 0)), pl.BlockSpec((feat, LANES), lambda i: (0, block))],
        input_output_aliases={len(operands): 1},
    )(*operands, sums)


def output_body(expert_count, returned_ref, slot_ref, probs_ref, middle_ref, result_ref):
    tok_count, feat = middle_ref.shape
    slots = returned_ref.shape[0]
    capacity = slots // expert_count
    part = capacity + EXTRA
    place = iota((1, slots), 1)
    number = place // capacity * part + place % capacity
    for start, size in row_blocks(tok_count):
        rows = pl.ds(start, size)
        lane = iota((size, LANES), 1)
        probs = probs_ref[rows, :]
        table = jnp.zeros((size, slots), full_type)
        for k in range(2):
            slot = slot_ref[rows, k : k + 1]
            gate = jnp.sum(jnp.where(lane == slot // part, probs, 0.0), axis=1, keepdims=True)
            table = jnp.where(number == slot, gate, table)
        high = table.astype(half_type)
        low = (table - high.astype(full_type)).astype(half_type)
        mixed = mul(high, returned_ref[...]) + mul(low, returned_ref[...])
        result_ref[rows, :] = (middle_ref[rows, :] + mixed).astype(half_type)


def block_result(returned, slot, probs, middle, expert_count, after=()):
    return call(
        functools.partial(output_body, expert_count), out(middle.shape, half_type), "block_result", after
    )(returned, slot, probs, middle)


def together(values, before=()):
    anywhere = pl.BlockSpec(memory_space=pl.ANY)
    count = len(values)
    call_all = pl.pallas_call(
        lambda *refs: None,
        out_shape=[out(v.shape, v.dtype) for v in values],
        name="together",
        in_specs=[anywhere] * (count + len(before)),
        out_specs=[anywhere] * count,
        input_output_aliases={i: i for i in range(count)},
        cost_estimate=pl.CostEstimate(flops=1024, bytes_accessed=1024, transcendentals=0),
    )
    return list(call_all(*values, *before))


def behind(values, *before):
    return together([values], before)[0]


def exchange(values, expert_count):
    split = values.reshape(expert_count, -1, values.shape[1])
    swapped = lax.all_to_all(split, "expert", split_axis=0, concat_axis=0, tiled=True)
    return swapped.reshape(values.shape)


def swap(values, axis, bit):
    count = lax.axis_size(axis)
    return lax.ppermute(values, axis, [(i, i ^ (1 << bit)) for i in range(count)])


def bits_of(axis):
    return range(lax.axis_size(axis).bit_length() - 1)


def sum_replicas(pair, fill=()):
    bits = list(bits_of("dp"))
    for n in range(len(bits)):
        pair = together(pair)
        others = [swap(pair[0], "dp", bits[n]), swap(pair[1], "dp", bits[-1 - n])]
        if n == len(bits) - 1 and fill:
            others[0] = behind(others[0], *fill)
        pair = [(v.astype(full_type) + o.astype(full_type)).astype(v.dtype) for v, o in zip(pair, others)]
    return pair


def send_blocks(values, *before):
    split = behind(values, *before).reshape(lax.axis_size("expert"), -1, values.shape[1])
    return lax.all_to_all(split, "expert", split_axis=0, concat_axis=0, tiled=True)


def sum_blocks(parts):
    return jnp.sum(parts.astype(full_type), axis=0).astype(parts.dtype)


def scatter_step(values, low, radix, *before):
    place = lax.axis_index("expert")
    split = values.reshape(values.shape[0] // radix, radix, *values.shape[1:])
    own = (place >> low) & (radix - 1)
    terms = []
    for step in range(radix):
        part = lax.dynamic_slice_in_dim(split, own ^ step, 1, 1)[:, 0]
        if step:
            part = lax.ppermute(part, "expert", [(i, i ^ (step << low)) for i in range(lax.axis_size("expert"))])
        elif before:
            part = behind(part, *before)
        terms.append(part.astype(full_type))
    return functools.reduce(jnp.add, terms).astype(values.dtype)


def scatter_chips(values, *before):
    low = 1
    while values.shape[0] > 1:
        radix = min(4, values.shape[0])
        values = scatter_step(values, low, radix, *before)
        low += radix.bit_length() - 1
        before = ()
    return values[0]


def gather_chips(pair, fill=()):
    place = lax.axis_index("expert")
    bits = list(bits_of("expert"))[1:]
    shapes = [v.shape for v in pair]
    pair = [v.reshape((1,) * len(bits) + v.shape) for v in pair]
    for n in range(len(bits)):
        pair = together(pair)
        steps = [bits[n], bits[-1 - n]]
        others = [swap(v, "expert", bit) for v, bit in zip(pair, steps)]
        if n == len(bits) - 1 and fill:
            others[0] = behind(others[0], *fill)
        for k, bit in enumerate(steps):
            axis = len(bits) - bit
            both = [pair[k], others[k]]
            lower, upper = (jnp.concatenate(both[::d], axis=axis) for d in (1, -1))
            pair[k] = jnp.where((place >> bit) & 1 == 0, lower, upper)
    return [v.reshape(-1, *shape) for v, shape in zip(pair, shapes)]


def assemble_body(core_ref, early_ref, early_other_ref, late_ref, late_other_ref, out_ref, query_ref, key_ref, value_ref, small_ref):
    own = pl.program_id(0) % 2 == core_ref[0]
    feat = out_ref.shape[2]
    width = feat // HEAD_GROUPS
    early = jnp.where(own, early_ref[0].astype(full_type), early_other_ref[0].astype(full_type))
    late = jnp.where(own, late_ref[0].astype(full_type), late_other_ref[0].astype(full_type))
    out_ref[0] = early[:, :feat]
    for kind, ref in enumerate((query_ref, key_ref, value_ref)):
        start = kind * width
        ref[0, :, :width] = early[:, feat + start : feat + start + width]
        ref[0, :, width:] = late[:, start : start + width]
    small_ref[0] = late[:, 3 * width :]


def assemble(core, early, early_other, late, late_other):
    chips, rows, early_width = early.shape
    late_width = late.shape[2]
    feat = 2 * chips * rows
    part = lambda width: pl.BlockSpec((1, rows, width), lambda i: (i // 2, 0, 0))
    block = lambda width: pl.BlockSpec((1, rows, width), lambda i: (i, 0, 0))
    matrix, small = out((2 * chips, rows, feat), full_type), out((2 * chips, rows, LANES), full_type)
    results = call(
        assemble_body,
        (matrix,) * 4 + (small,),
        "assemble",
        grid=(2 * chips,),
        in_specs=[pl.BlockSpec(memory_space=pltpu.SMEM)] + [part(early_width)] * 2 + [part(late_width)] * 2,
        out_specs=[block(feat)] * 4 + [block(LANES)],
    )(core, early, early_other, late, late_other)
    return [a.reshape(feat, a.shape[2]) for a in results]


def widen_body(steps, sum_ref, up_ref, down_ref, up_bias_ref, down_bias_ref):
    share, feat = up_ref.shape[0], sum_ref.shape[1]
    for step in range(steps):
        up_ref[:, step * feat : step * feat + feat] = sum_ref[step * share : step * share + share, :].astype(full_type)
    ends = 2 * steps * share
    down_ref[...] = sum_ref[steps * share : ends, :].astype(full_type)
    last = sum_ref[ends:, :].astype(full_type)
    up_bias_ref[...] = last[0:1, : steps * share]
    down_bias_ref[...] = last[8:9, :share]


def widen(expert_sum, steps, share):
    feat = expert_sum.shape[1]
    return call(
        functools.partial(widen_body, steps),
        (
            out((share, steps * feat), full_type),
            out((steps * share, feat), full_type),
            out((1, steps * share), full_type),
            out((1, share), full_type),
        ),
        "widen",
    )(expert_sum)


def shards(
    tokens,
    first_gain,
    first_shift,
    query_weight,
    query_bias,
    key_weight,
    value_weight,
    value_bias,
    out_weight,
    out_bias,
    second_gain,
    second_shift,
    router,
    expert_up,
    expert_up_bias,
    expert_down,
    expert_down_bias,
    choices,
    priority,
    cotangent,
):
    tok_count, feat = tokens.shape
    expert_count = lax.axis_size("expert")
    capacity = (21 * tok_count + 80 * expert_count - 1) // (80 * expert_count) * 8
    router3 = jnp.pad(jnp.concatenate([router] * 3, axis=1), ((0, 0), (0, LANES - 3 * expert_count)))
    up, down = expert_up[0], expert_down[0]

    replicas = lax.axis_size("dp")
    choice_rows = choices.T
    place, cot_sent = route(choice_rows, priority, cotangent, expert_count, capacity)
    cot = exchange(cot_sent, expert_count)
    first, q, k, v, log_big, log_small, attended, middle, _, probs, sent = front(
        tokens,
        (first_gain, first_shift, query_bias, value_bias, out_bias, second_gain, second_shift),
        (query_weight, key_weight, value_weight, out_weight),
        router3,
        place,
        expert_count,
        capacity,
    )
    rows = exchange(behind(sent, cot), expert_count)
    grad_act, start = act_grad(cot, down, expert_down_bias)
    slot = slot_columns(choice_rows, place, capacity, (start,))
    act, grad_pre, gate, score, weight_part = expert(
        rows, up, expert_up_bias, grad_act, start, cot, replicas
    )
    expert_sum = lax.psum_scatter(weight_part, "dp", scatter_dimension=0, tiled=True)[0]
    grad_in = expert_grad_in(grad_pre, up, gate, score, capacity, (slot,))
    back = exchange(grad_in, expert_count)
    result = expert_result(act, down, expert_down_bias, (grad_in,))
    grad_middle, grad_attended, wo_grad, router_part, second_parts = combine(
        back,
        slot,
        probs,
        middle,
        cotangent,
        attended,
        out_weight,
        router3,
        second_gain,
        second_shift,
        expert_count,
        capacity,
        (result,),
    )
    out_blocks = send_blocks(wo_grad, back)
    grads, bias_parts, group_parts, before = [], [], [], ()
    for group in range(HEAD_GROUPS):
        dq, dk, dv, group_part, bias_part = attention_grad(
            group, q, k, v, grad_attended, log_big, log_small, first, before
        )
        grads += [dq, dk, dv]
        bias_parts.append(bias_part)
        group_parts.append(group_part)
        before = (dv, out_blocks)
    first_blocks = send_blocks(group_parts[0], out_blocks)
    token_grad, last_part = input_grad(
        grads,
        query_weight,
        key_weight,
        value_weight,
        tokens,
        first_gain,
        grad_middle,
        bias_parts,
        second_parts,
        router_part,
        group_parts[1],
        (),
    )
    late = behind(last_part, first_blocks).reshape(expert_count, -1, last_part.shape[1])
    late = scatter_chips(scatter_step(late, 0, 2))
    early = jnp.concatenate([sum_blocks(out_blocks), sum_blocks(first_blocks)], axis=1)
    returned = exchange(behind(result, late), expert_count)
    share, steps = feat // replicas, up.shape[1] // feat
    up_grad, down_grad, up_bias_grad, down_bias_grad = widen(expert_sum, steps, share)
    block_output = block_result(returned, slot, probs, middle, expert_count, (token_grad,))
    early, late = gather_chips(sum_replicas([early, late], (up_grad,)), (block_output,))
    early, late = together([early, late])
    core = (lax.axis_index("expert") & 1).reshape(1)
    out_grad, query_grad, key_grad, value_grad, small = assemble(
        core, early, swap(early, "expert", 0), late, swap(late, "expert", 0)
    )
    vectors = small[:, 32:40].T
    return (
        block_output,
        token_grad,
        vectors[0],
        vectors[1],
        query_grad,
        vectors[2],
        key_grad,
        value_grad,
        vectors[3],
        out_grad,
        vectors[6],
        vectors[4],
        vectors[5],
        small[:, :expert_count],
        up_grad[None],
        up_bias_grad,
        down_grad[None],
        down_bias_grad,
    )


def solution(mesh):
    tokens_spec = P(("dp", "expert"), None)
    return jax.shard_map(
        shards,
        mesh=mesh,
        in_specs=(tokens_spec,)
        + (P(),) * 12
        + (P("expert", None, None), P("expert", None), P("expert", None, None), P("expert", None))
        + (tokens_spec,) * 3,
        out_specs=(tokens_spec,) * 2
        + (P(),) * 12
        + (P("expert", "dp", None), P("expert", "dp"), P("expert", "dp", None), P("expert", "dp")),
        check_vma=False,
    )
```

```python
import functools

import jax
import jax.numpy as jnp
from jax import lax
from jax.experimental import pallas as pl
from jax.experimental.pallas import tpu as pltpu
from jax.sharding import PartitionSpec as P

HEADS = 12
BIG = 576
SMALL = 196
LANES = 128
EXTRA = 16
HEAD_GROUPS = 2

half_type = jnp.bfloat16
full_type = jnp.float32
norm_eps = 1e-06
masked_score = -1000000000.0
vmem_bytes = 56 * 2**20


def dot_full(left, right, dims):
    return lax.dot_general(left, right, (dims, ((), ())), preferred_element_type=full_type)


def mul(left, right):
    return dot_full(left, right, ((1,), (0,)))


def mul_t(left, right):
    return dot_full(left, right, ((1,), (1,)))


def t_mul(left, right):
    return dot_full(left, right, ((0,), (0,)))


def row_blocks(rows, step=256):
    return [(start, min(step, rows - start)) for start in range(0, rows, step)]


def iota(shape, dim):
    return lax.broadcasted_iota(jnp.int32, shape, dim)


def ones_where(mask):
    return jnp.where(mask, 1.0, 0.0).astype(half_type)


def normalize(values):
    row_mean = jnp.mean(values, axis=-1, keepdims=True)
    centered = values - row_mean
    inverse = lax.rsqrt(jnp.mean(centered * centered, axis=-1, keepdims=True) + norm_eps)
    return centered * inverse, inverse


def norm_backward(upstream, normed, inverse, norm_gain):
    scaled = upstream * norm_gain
    first_mean = jnp.mean(scaled, axis=-1, keepdims=True)
    second_mean = jnp.mean(scaled * normed, axis=-1, keepdims=True)
    return inverse * (scaled - first_mean - normed * second_mean)


def split_thirds(values, lane, expert_count):
    high = values.astype(half_type).astype(full_type)
    rest = values - high
    middle = rest.astype(half_type).astype(full_type)
    low = rest - middle
    picked = jnp.where(lane < expert_count, high, jnp.where(lane < 2 * expert_count, middle, low))
    return jnp.where(lane < 3 * expert_count, picked, 0.0).astype(half_type)


def call(body, out_shape, name, after=(), grid=(1,), in_specs=None, flops=1024, **kwargs):
    def build(*operands):
        specs = list(in_specs) if in_specs else [whole(a) for a in operands]
        used = len(specs)
        if "out_specs" not in kwargs:
            kwargs["out_specs"] = jax.tree.map(whole, out_shape)

        def inner(*refs):
            body(*refs[:used], *refs[used + len(after) :])

        return pl.pallas_call(
            inner,
            out_shape=out_shape,
            name=name,
            grid=grid,
            in_specs=specs + [pl.BlockSpec(memory_space=pl.ANY)] * len(after),
            compiler_params=pltpu.CompilerParams(vmem_limit_bytes=vmem_bytes),
            cost_estimate=pl.CostEstimate(flops=flops, bytes_accessed=1024, transcendentals=0),
            **kwargs,
        )(*operands, *after)

    return build


def whole(array):
    zeros = (0,) * len(array.shape)
    return pl.BlockSpec(array.shape, lambda *_: zeros)


def out(shape, dtype):
    return jax.ShapeDtypeStruct(shape, dtype)


def vec(ref):
    return ref[...].reshape(1, -1)


def for_experts(expert_count, step):
    if expert_count <= 8:
        for e in range(expert_count):
            step(e)
    else:
        lax.fori_loop(0, expert_count, lambda e, c: (step(e), c)[1], 0)


def expert_rows(e, capacity):
    if isinstance(e, int):
        return pl.ds(e * capacity, capacity)
    return pl.ds(pl.multiple_of(e * capacity, capacity), capacity)


def row_thirds(row):
    high = row.astype(half_type).astype(full_type)
    rest = row - high
    middle = rest.astype(half_type).astype(full_type)
    sub = iota((8, row.shape[1]), 0)
    picked = jnp.where(sub == 0, high, jnp.where(sub == 1, middle, jnp.where(sub == 2, rest - middle, 0.0)))
    return picked.astype(half_type)


def thirds_to_lanes(thirds):
    return t_mul(thirds, jnp.ones((thirds.shape[0], LANES), half_type))


def store_thirds(ref, start, row):
    ref[pl.ds(start, EXTRA), :] = jnp.zeros((EXTRA, ref.shape[1]), ref.dtype)
    thirds = jnp.concatenate([row_thirds(row), jnp.zeros((EXTRA - 8, row.shape[1]), half_type)], axis=0)
    ref[pl.ds(start, EXTRA), 0 : row.shape[1]] = thirds


def part_start(e, size, offset=0):
    if isinstance(e, int):
        return e * size + offset
    return pl.multiple_of(e * size + offset, 16)


def lanes_to_row(values):
    ones = jnp.ones((8, LANES), half_type)
    high = values.astype(half_type)
    rest = values - high.astype(full_type)
    middle = rest.astype(half_type)
    low = (rest - middle.astype(full_type)).astype(half_type)
    return (mul_t(ones, high) + mul_t(ones, middle) + mul_t(ones, low))[0:1]


def rank_column(rows):
    tok_count = rows.shape[1]
    rows = jnp.concatenate([rows, jnp.zeros((8 - rows.shape[0], tok_count), jnp.int32)], axis=0)
    return rows.astype(full_type).T.astype(jnp.int32)


def route_body(expert_count, capacity, rows_ref, rank_ref, cot_ref, place_ref, sent_ref):
    tok_count = cot_ref.shape[0]
    padded = place_ref.shape[0]
    sub = iota((padded, tok_count), 0)
    first, second = rows_ref[0:1, :], rows_ref[1:2, :]
    first_hot, second_hot = ones_where(first == sub), ones_where(second == sub)
    earlier = ones_where(rank_column(rank_ref[...])[:, 0:1] < rank_ref[...])
    first_total = jnp.sum(first_hot.astype(full_type), axis=1, keepdims=True)
    counts = mul(jnp.concatenate([first_hot, second_hot], axis=0), earlier)
    first_count, second_count = counts[:padded], counts[padded:] + first_total
    place = jnp.where(
        (first == sub) & (first_count < capacity),
        first_count,
        jnp.where((second == sub) & (second_count < capacity), second_count, -1.0),
    )
    place_ref[...] = place.astype(jnp.int32)
    cot = cot_ref[...]
    within = iota((capacity, tok_count), 0)

    def send(e):
        hot = ones_where(place_ref[pl.ds(e, 1), :] == within)
        sent_ref[pl.ds(part_start(e, capacity), capacity), :] = mul(hot, cot).astype(half_type)

    for_experts(expert_count, send)


def route(choice_rows, priority, cotangent, expert_count, capacity):
    tok_count, feat = cotangent.shape
    padded = -(-expert_count // 32) * 32
    return call(
        functools.partial(route_body, expert_count, capacity),
        (out((padded, tok_count), jnp.int32), out((expert_count * capacity, feat), half_type)),
        "route",
    )(choice_rows, priority, cotangent)


def slots_body(capacity, rows_ref, place_ref, slot_ref):
    part = capacity + EXTRA
    padded, tok_count = place_ref.shape
    sub = iota((padded, tok_count), 0)
    slots = []
    for k in range(2):
        place = jnp.sum(jnp.where(rows_ref[k : k + 1, :] == sub, place_ref[...], 0), axis=0, keepdims=True)
        slots.append(jnp.where(place < 0, -1, rows_ref[k : k + 1, :] * part + place))
    slot_ref[...] = rank_column(jnp.concatenate(slots, axis=0))[:, 0:2]


def slot_columns(choice_rows, place, capacity, after):
    return call(
        functools.partial(slots_body, capacity), out((choice_rows.shape[1], 2), jnp.int32), "slot_columns", after
    )(choice_rows, place)


def image_mask(size):
    key_image = iota((size, 1), 0) // SMALL
    query_image = iota((1, size), 1) // SMALL
    return key_image == query_image


def images(tok_count):
    return ((0, BIG), (BIG, tok_count - BIG))


def head_lanes(value, head):
    lane = iota((1, LANES), 1)
    return jnp.where((lane < LANES // 2) == (head == 0), value, jnp.zeros((), value.dtype))


def front_body(
    expert_count,
    capacity,
    tokens_ref,
    gain_ref,
    shift_ref,
    wq_ref,
    bq_ref,
    wk_ref,
    wv_ref,
    bv_ref,
    wo_ref,
    bo_ref,
    gain2_ref,
    shift2_ref,
    router_ref,
    place_ref,
    first_ref,
    q_ref,
    k_ref,
    v_ref,
    log_big_ref,
    log_small_ref,
    attended_ref,
    middle_ref,
    second_ref,
    probs_ref,
    sent_ref,
):
    tok_count, feat = tokens_ref.shape
    scale = (feat // HEADS) ** (-0.5)
    for start, size in row_blocks(tok_count):
        rows = pl.ds(start, size)
        normed, _ = normalize(tokens_ref[rows, :].astype(full_type))
        low = (normed * vec(gain_ref) + vec(shift_ref)).astype(half_type)
        first_ref[rows, :] = low
        q_ref[rows, :] = (mul(low, wq_ref[...]) + vec(bq_ref)).astype(half_type)
        k_ref[rows, :] = mul(low, wk_ref[...]).astype(half_type)
        v_ref[rows, :] = (mul(low, wv_ref[...]) + vec(bv_ref)).astype(half_type)

    def pair(number, carry):
        lanes = pl.ds(pl.multiple_of(number * LANES, LANES), LANES)
        for place, (start, size) in enumerate(images(tok_count)):
            rows = pl.ds(start, size)
            query, key, value = q_ref[rows, lanes], k_ref[rows, lanes], v_ref[rows, lanes]
            key = key * jnp.asarray(scale, half_type)
            log_ref = (log_big_ref, log_small_ref)[place]
            value_t = value.T
            halves = []
            for head in range(2):
                scores = mul_t(head_lanes(key, head), query)
                if place:
                    scores = jnp.where(image_mask(size), scores, masked_score)
                top = jnp.max(scores, axis=0, keepdims=True)
                weights = jnp.exp(scores - top)
                total = jnp.sum(weights, axis=0, keepdims=True)
                log_ref[pl.ds(2 * number + head, 1), :] = top + jnp.log(total)
                mixed = mul(value_t[head * 64 : head * 64 + 64], weights.astype(half_type))
                halves.append(mixed * (1.0 / total))
            attended_ref[rows, lanes] = jnp.concatenate(halves, axis=0).T.astype(half_type)
        return carry

    lax.fori_loop(0, HEADS // 2, pair, 0)

    for start, size in row_blocks(tok_count):
        rows = pl.ds(start, size)
        lane = iota((size, LANES), 1)
        middle = tokens_ref[rows, :].astype(full_type) + mul(attended_ref[rows, :], wo_ref[...]) + vec(bo_ref)
        middle_ref[rows, :] = middle
        normed, _ = normalize(middle)
        low = (normed * vec(gain2_ref) + vec(shift2_ref)).astype(half_type)
        second_ref[rows, :] = low
        logits = jnp.where(lane < 3 * expert_count, mul(low, router_ref[...]), masked_score)
        top = jnp.max(logits, axis=1, keepdims=True)
        raised = jnp.exp(logits - top)
        total = jnp.sum(jnp.where(lane < expert_count, raised, 0.0), axis=1, keepdims=True)
        probs_ref[rows, :] = raised / total

    low = second_ref[...]
    lane = iota((tok_count, LANES), 1)
    thirds = split_thirds(probs_ref[...], lane, expert_count)
    within = iota((capacity, tok_count), 0)
    slot_lane = iota((capacity, LANES), 1)

    def send(e):
        hot = ones_where(place_ref[pl.ds(e, 1), :] == within)
        rows = mul(hot, low).astype(half_type)
        part = capacity + EXTRA
        sent_ref[pl.ds(part_start(e, part), capacity), :] = rows
        gates = mul(hot, thirds)
        own = (slot_lane == e) | (slot_lane == e + expert_count) | (slot_lane == e + 2 * expert_count)
        picked = jnp.where(own, gates, 0.0).astype(half_type)
        store_thirds(sent_ref, part_start(e, part, capacity), mul_t(jnp.ones((8, LANES), half_type), picked)[0:1])

    for_experts(expert_count, send)


def front(tokens, vectors, weights, router3, place, expert_count, capacity):
    tok_count, feat = tokens.shape
    gain, shift, bq, bv, bo, gain2, shift2 = vectors
    wq, wk, wv, wo = weights
    low = out((tok_count, feat), half_type)
    return call(
        functools.partial(front_body, expert_count, capacity),
        (
            low,
            low,
            low,
            low,
            out((HEADS, BIG), full_type),
            out((HEADS, tok_count - BIG), full_type),
            low,
            out((tok_count, feat), full_type),
            low,
            out((tok_count, LANES), full_type),
            out((expert_count * (capacity + EXTRA), feat), half_type),
        ),
        "front",
    )(tokens, gain, shift, wq, bq, wk, wv, bv, wo, bo, gain2, shift2, router3, place)


def fold_lanes(values):
    folded = values[:, :LANES]
    for start in range(LANES, values.shape[1], LANES):
        folded = folded + values[:, start : start + LANES]
    return folded


def act_grad_body(cot_ref, down_ref, down_bias_ref, grad_act_ref, score_ref):
    for start, size in row_blocks(cot_ref.shape[0], 512):
        rows = pl.ds(start, size)
        grad_act_ref[rows, :] = mul_t(cot_ref[rows, :], down_ref[...]).astype(half_type)

        @pl.when(pl.program_id(0) == 0)
        def _():
            score_ref[rows, :] = fold_lanes(cot_ref[rows, :].astype(full_type) * down_bias_ref[...])


def act_grad(cot, down, down_bias, step=512):
    slots, feat = cot.shape
    hidden = down.shape[0]
    return call(
        act_grad_body,
        (out((slots, hidden), half_type), out((slots, LANES), full_type)),
        "act_grad",
        grid=(hidden // step,),
        in_specs=[whole(cot), pl.BlockSpec((step, feat), lambda f: (f, 0)), whole(down_bias)],
        out_specs=[pl.BlockSpec((slots, step), lambda f: (0, f)), pl.BlockSpec((slots, LANES), lambda f: (0, 0))],
    )(cot, down, down_bias)


def gelu_parts(values):
    area = 0.5 + 0.5 * lax.erf(values * 0.7071067811865476)
    bell = jnp.exp(values * values * -0.5) * 0.3989422804014327
    return values * area, area + values * bell


def expert_body(rows_ref, up_ref, up_bias_ref, grad_act_ref, start_ref, cot_ref, act_ref, grad_pre_ref, gate_ref, score_ref, sum_ref, x_ref, gated_ref, grad_ref, bias_ref, up_out_ref, down_out_ref, cot_held, start_held, sems, load_sems):
    slots, feat = cot_ref.shape
    replicas, share = up_out_ref.shape[1:3]
    steps = (sum_ref.shape[1] - EXTRA) // share // 2
    part = rows_ref.shape[0] // (rows_ref.shape[0] - slots) * EXTRA
    capacity = part - EXTRA
    number = pl.program_id(0)
    down_rows = steps * share
    size = min(down_rows, feat)

    def copies(step):
        pairs = [(up_out_ref.at[step % 2], sum_ref.at[:, pl.ds(step * share, share), :])]
        for piece in range(feat // size):
            row = step * feat + piece * size
            target = sum_ref.at[row // down_rows, pl.ds(down_rows + row % down_rows, size), :]
            pairs.append((down_out_ref.at[step % 2, pl.ds(piece * size, size)], target))
        return [pltpu.make_async_copy(a, b, sems.at[step, i]) for i, (a, b) in enumerate(pairs)]

    loads = [
        pltpu.make_async_copy(cot_ref, cot_held, load_sems.at[0]),
        pltpu.make_async_copy(start_ref, start_held, load_sems.at[1]),
    ]

    @pl.when(number == 0)
    def _():
        for load in loads:
            load.start()
        for e in range(slots // capacity):
            rows = pl.ds(e * capacity, capacity)
            gate_ref[rows, :] = thirds_to_lanes(rows_ref[pl.ds(e * part + capacity, EXTRA), 0:capacity])
            x_ref[rows, :] = rows_ref[pl.ds(e * part, capacity), :]
        score_ref[...] = jnp.zeros(score_ref.shape, full_type)

    blocks = row_blocks(slots, 512)
    pre = mul(x_ref[pl.ds(*blocks[0]), :], up_ref[...])
    bias_grad = jnp.zeros((1, feat), full_type)
    for b, block in enumerate(blocks):
        rows = pl.ds(*block)
        if b + 1 < len(blocks):
            later = mul(x_ref[pl.ds(*blocks[b + 1]), :], up_ref[...])
        act, slope = gelu_parts(pre + up_bias_ref[...])
        act_ref[rows, :] = act.astype(half_type)
        grad_act = grad_act_ref[rows, :].astype(full_type)
        score_ref[rows, :] += fold_lanes(act * grad_act)
        grad_pre_ref[rows, :] = (grad_act * slope).astype(half_type)
        pre = later
    @pl.when(number == 0)
    def _():
        for load in loads:
            load.wait()
        total = jnp.zeros((1, feat), full_type)
        for e in range(slots // capacity):
            rows = pl.ds(e * capacity, capacity)
            wide = jnp.concatenate([gate_ref[rows, :]] * (feat // LANES), axis=1)
            gated_ref[rows, :] = (x_ref[rows, :].astype(full_type) * wide).astype(half_type)
            grad = (cot_held[rows, :].astype(full_type) * wide).astype(half_type)
            grad_ref[rows, :] = grad
            total = total + jnp.sum(grad.astype(full_type), axis=0, keepdims=True)
        bias_ref[...] = jnp.zeros(bias_ref.shape, half_type)
        for z in range(replicas):
            bias_ref[z, 8:9, 0:share] = total[:, z * share : z * share + share].astype(half_type)

    for step in range(2, steps):

        @pl.when(number == step)
        def _():
            for copy in copies(step - 2):
                copy.wait()

    up_out_ref[number % 2] = t_mul(gated_ref[...], grad_pre_ref[...]).astype(half_type).reshape(replicas, share, feat)
    down_out_ref[number % 2] = t_mul(act_ref[...], grad_ref[...]).astype(half_type)
    for start, size_b in blocks:
        rows = pl.ds(start, size_b)
        wide = jnp.concatenate([gate_ref[rows, :]] * (feat // LANES), axis=1)
        bias_grad = bias_grad + jnp.sum(grad_pre_ref[rows, :].astype(full_type) * wide, axis=0, keepdims=True)
    for step in range(steps):

        @pl.when(number == step)
        def _():
            for piece in range(feat // size):
                z = (step * feat + piece * size) // down_rows
                bias_ref[z, 0:1, 0:size] = bias_grad[:, piece * size : piece * size + size].astype(half_type)
            for copy in copies(step):
                copy.start()

    @pl.when(number == steps - 1)
    def _():
        last = pltpu.make_async_copy(bias_ref, sum_ref.at[:, pl.ds(2 * down_rows, EXTRA), :], sems.at[0, 0])
        last.start()
        score_ref[...] = (score_ref[...] + start_held[...]) * gate_ref[...]
        for step in range(steps - 2, steps):
            for copy in copies(step):
                copy.wait()
        last.wait()


def expert(rows, up, up_bias, grad_act, start, cot, replicas):
    slots, feat = cot.shape
    hidden = up.shape[1]
    steps, share = hidden // feat, feat // replicas
    wide = pl.BlockSpec((slots, feat), lambda f: (0, f))
    once = lambda a: pl.BlockSpec(a.shape, lambda f: (0, 0), pipeline_mode=pl.Buffered(1))
    lanes = out((slots, LANES), full_type)
    return call(
        expert_body,
        (
            out((slots, hidden), half_type),
            out((slots, hidden), half_type),
            lanes,
            lanes,
            out((replicas, 2 * steps * share + EXTRA, feat), half_type),
        ),
        "expert",
        grid=(steps,),
        in_specs=[
            once(rows),
            pl.BlockSpec((feat, feat), lambda f: (0, f)),
            pl.BlockSpec((1, feat), lambda f: (0, f)),
            wide,
            pl.BlockSpec(memory_space=pl.ANY),
            pl.BlockSpec(memory_space=pl.ANY),
        ],
        out_specs=[
            wide,
            wide,
            whole(lanes),
            whole(lanes),
            pl.BlockSpec(memory_space=pl.ANY),
        ],
        scratch_shapes=[
            pltpu.VMEM((slots, feat), half_type),
            pltpu.VMEM((slots, feat), half_type),
            pltpu.VMEM((slots, feat), half_type),
            pltpu.VMEM((replicas, EXTRA, feat), half_type),
            pltpu.VMEM((2, replicas, share, feat), half_type),
            pltpu.VMEM((2, feat, feat), half_type),
            pltpu.VMEM((slots, feat), half_type),
            pltpu.VMEM((slots, LANES), full_type),
            pltpu.SemaphoreType.DMA((steps, 1 + max(1, feat // (steps * share)))),
            pltpu.SemaphoreType.DMA((2,)),
        ],
    )(rows, up, up_bias, grad_act, start, cot)


def grad_in_body(capacity, grad_pre_ref, up_ref, gate_ref, score_ref, grad_in_ref):
    part = capacity + EXTRA
    size, feat = grad_pre_ref.shape[0], up_ref.shape[0]
    grad = mul_t(grad_pre_ref[...], up_ref[...])
    grad = grad * jnp.concatenate([gate_ref[...]] * (feat // LANES), axis=1)
    for e in range(size // capacity):
        grad_in_ref[pl.ds(e * part, capacity), :] = grad[e * capacity : e * capacity + capacity].astype(half_type)
        store_thirds(grad_in_ref, e * part + capacity, lanes_to_row(score_ref[e * capacity : e * capacity + capacity, :]))


def expert_grad_in(grad_pre, up, gate, score, capacity, after, step=512):
    slots, hidden = grad_pre.shape
    feat = up.shape[0]
    part = capacity + EXTRA
    lanes = pl.BlockSpec((step, LANES), lambda r: (r, 0))
    return call(
        functools.partial(grad_in_body, capacity),
        out((slots // capacity * part, feat), half_type),
        "grad_in",
        after,
        flops=4 * 10**11,
        grid=(slots // step,),
        in_specs=[pl.BlockSpec((step, hidden), lambda r: (r, 0)), whole(up), lanes, lanes],
        out_specs=pl.BlockSpec((step // capacity * part, feat), lambda r: (r, 0)),
    )(grad_pre, up, gate, score)


def result_body(act_ref, down_ref, down_bias_ref, result_ref):
    result_ref[...] = (mul(act_ref[...], down_ref[...]) + down_bias_ref[...]).astype(half_type)


def expert_result(act, down, down_bias, after=(), step=512):
    slots, hidden = act.shape
    feat = down.shape[1]
    return call(
        result_body,
        out((slots, feat), half_type),
        "result",
        after,
        grid=(slots // step,),
        in_specs=[pl.BlockSpec((step, hidden), lambda r: (r, 0)), whole(down), whole(down_bias)],
        out_specs=pl.BlockSpec((step, feat), lambda r: (r, 0)),
    )(act, down, down_bias)


def combine_body(
    expert_count,
    capacity,
    back_ref,
    slot_ref,
    probs_ref,
    middle_ref,
    cot_ref,
    attended_ref,
    wo_ref,
    router_ref,
    gain_ref,
    shift_ref,
    grad_middle_ref,
    grad_attended_ref,
    wo_grad_ref,
    router_grad_ref,
    vector_ref,
):
    tok_count, feat = cot_ref.shape
    slots = back_ref.shape[0]
    part = capacity + EXTRA
    lane = iota((capacity, LANES), 1)
    tables = []
    for e in range(expert_count):
        same = (lane == e) | (lane == e + expert_count) | (lane == e + 2 * expert_count)
        score = thirds_to_lanes(back_ref[pl.ds(e * part + capacity, EXTRA), 0:capacity])
        tables.append(split_thirds(jnp.where(same, score, 0.0), lane, expert_count))
        tables.append(jnp.zeros((EXTRA, LANES), half_type))
    table = jnp.concatenate(tables, axis=0)
    wo_grad = jnp.zeros(wo_grad_ref.shape, full_type)
    router_grad = jnp.zeros(router_grad_ref.shape, full_type)
    gain_grad = jnp.zeros((1, feat), full_type)
    shift_grad = jnp.zeros((1, feat), full_type)
    bias_grad = jnp.zeros((1, feat), full_type)
    for start, size in row_blocks(tok_count):
        rows = pl.ds(start, size)
        number = iota((size, slots), 1)
        hot = ones_where((number == slot_ref[rows, 0:1]) | (number == slot_ref[rows, 1:2]))
        lane = iota((size, LANES), 1)
        folded = mul(hot, table)
        folded = folded + pltpu.roll(folded, LANES - expert_count, 1) + pltpu.roll(folded, LANES - 2 * expert_count, 1)
        probs = jnp.where(lane < expert_count, probs_ref[rows, :], 0.0)
        scores = jnp.where(lane < expert_count, folded, 0.0)
        grad_logits = scores - probs * jnp.sum(scores, axis=1, keepdims=True)
        grad_logits = grad_logits + pltpu.roll(grad_logits, expert_count, 1) + pltpu.roll(grad_logits, 2 * expert_count, 1)
        thirds = split_thirds(grad_logits, lane, expert_count)
        upstream = mul_t(thirds, router_ref[...]) + mul(hot, back_ref[...])
        normed, inverse = normalize(middle_ref[rows, :])
        low = (normed * vec(gain_ref) + vec(shift_ref)).astype(half_type)
        router_grad = router_grad + t_mul(low, thirds)
        gain_grad = gain_grad + jnp.sum(upstream * normed, axis=0, keepdims=True)
        shift_grad = shift_grad + jnp.sum(upstream, axis=0, keepdims=True)
        grad_middle = cot_ref[rows, :].astype(full_type) + norm_backward(upstream, normed, inverse, vec(gain_ref))
        grad_middle_ref[rows, :] = grad_middle
        branch = grad_middle.astype(half_type)
        bias_grad = bias_grad + jnp.sum(branch.astype(full_type), axis=0, keepdims=True)
        grad_attended_ref[rows, :] = mul_t(branch, wo_ref[...]).astype(half_type)
        wo_grad = wo_grad + t_mul(attended_ref[rows, :], branch)
    wo_grad_ref[...] = wo_grad.astype(half_type)
    router_grad = router_grad + pltpu.roll(router_grad, LANES - expert_count, 1) + pltpu.roll(router_grad, LANES - 2 * expert_count, 1)
    router_grad_ref[...] = router_grad
    vector_ref[0:1, :] = gain_grad
    vector_ref[1:2, :] = shift_grad
    vector_ref[2:3, :] = bias_grad


def combine(back, slot, probs, middle, cot, attended, wo, router3, gain, shift, expert_count, capacity, after=()):
    tok_count, feat = cot.shape
    return call(
        functools.partial(combine_body, expert_count, capacity),
        (
            out((tok_count, feat), full_type),
            out((tok_count, feat), half_type),
            out((feat, feat), half_type),
            out((feat, LANES), full_type),
            out((3, feat), full_type),
        ),
        "combine",
        after,
    )(back, slot, probs, middle, cot, attended, wo, router3, gain, shift)


def attention_grad_body(first_head, q_ref, k_ref, v_ref, grad_ref, log_big_ref, log_small_ref, first_ref, dq_ref, dk_ref, dv_ref, weight_ref, bias_ref):
    tok_count, width = q_ref.shape
    scale = 64 ** (-0.5)

    def pair(number, carry):
        lanes = pl.ds(pl.multiple_of(number * LANES, LANES), LANES)
        for place, (start, size) in enumerate(images(tok_count)):
            rows = pl.ds(start, size)
            query, key, value, grad = q_ref[rows, lanes], k_ref[rows, lanes], v_ref[rows, lanes], grad_ref[rows, lanes]
            key = key * jnp.asarray(scale, half_type)
            log_ref = (log_big_ref, log_small_ref)[place]
            key_t = key.T
            halves = []
            grad_value = jnp.zeros((size, LANES), full_type)
            grad_key = jnp.zeros((size, LANES), full_type)
            for head in range(2):
                scores = mul_t(head_lanes(key, head), query)
                if place:
                    scores = jnp.where(image_mask(size), scores, masked_score)
                probs = jnp.exp(scores - log_ref[pl.ds(first_head + 2 * number + head, 1), :])
                grad_probs = mul_t(head_lanes(value, head), grad)
                inner = jnp.sum(grad_probs * probs, axis=0, keepdims=True)
                grad_scores = (probs * (grad_probs - inner)).astype(half_type)
                grad_value = grad_value + mul(probs.astype(half_type), head_lanes(grad, head))
                grad_key = grad_key + mul(grad_scores, head_lanes(query, head))
                halves.append(mul(key_t[head * 64 : head * 64 + 64], grad_scores))
            dv_ref[rows, lanes] = grad_value.astype(half_type)
            dk_ref[rows, lanes] = (grad_key * scale).astype(half_type)
            dq_ref[rows, lanes] = jnp.concatenate(halves, axis=0).T.astype(half_type)
        return carry

    lax.fori_loop(0, width // LANES, pair, 0)
    first = first_ref[...]
    for kind, grad_ref in enumerate((dq_ref, dk_ref, dv_ref)):
        weight_ref[:, kind * width : kind * width + width] = t_mul(first, grad_ref[...]).astype(half_type)
    bias_ref[0:1, :] = jnp.sum(dq_ref[...].astype(full_type), axis=0, keepdims=True)
    bias_ref[1:2, :] = jnp.sum(dv_ref[...].astype(full_type), axis=0, keepdims=True)


def attention_grad(group, q, k, v, grad, log_big, log_small, first, after=()):
    tok_count, feat = q.shape
    width = feat // HEAD_GROUPS
    columns = pl.BlockSpec((tok_count, width), lambda i: (0, group))
    low = out((tok_count, width), half_type)
    grads = out((feat, 3 * width + (LANES if group == HEAD_GROUPS - 1 else 0)), half_type)
    return call(
        functools.partial(attention_grad_body, group * HEADS // HEAD_GROUPS),
        (low, low, low, grads, out((2, width), full_type)),
        f"attention_grad_{group}",
        after,
        in_specs=[columns, columns, columns, columns, whole(log_big), whole(log_small), whole(first)],
    )(q, k, v, grad, log_big, log_small, first)


def input_grad_body(*refs):
    grads = refs[: 3 * HEAD_GROUPS]
    refs = refs[3 * HEAD_GROUPS :]
    wq_ref, wk_ref, wv_ref, tokens_ref, gain_ref, middle_ref, bias_a_ref, bias_b_ref, second_ref, router_ref = refs[:10]
    result_ref, sums_ref = refs[11:]
    tok_count, feat = tokens_ref.shape
    width = feat // HEAD_GROUPS
    gain_grad = jnp.zeros((1, feat), full_type)
    shift_grad = jnp.zeros((1, feat), full_type)
    for start, size in row_blocks(tok_count):
        rows = pl.ds(start, size)
        upstream = jnp.zeros((size, feat), full_type)
        for group in range(HEAD_GROUPS):
            lanes = pl.ds(group * width, width)
            for grad_ref, weight_ref in zip(grads[3 * group : 3 * group + 3], (wq_ref, wk_ref, wv_ref)):
                upstream = upstream + mul_t(grad_ref[rows, :], weight_ref[:, lanes])
        normed, inverse = normalize(tokens_ref[rows, :].astype(full_type))
        gain_grad = gain_grad + jnp.sum(upstream * normed, axis=0, keepdims=True)
        shift_grad = shift_grad + jnp.sum(upstream, axis=0, keepdims=True)
        grad = middle_ref[rows, :] + norm_backward(upstream, normed, inverse, vec(gain_ref))
        result_ref[rows, :] = grad.astype(half_type)
    biases = jnp.concatenate([bias_a_ref[...], bias_b_ref[...]], axis=1)
    vectors = [jnp.zeros((32, feat), full_type), gain_grad, shift_grad, biases, second_ref[...]]
    vectors.append(jnp.zeros((LANES - 39, feat), full_type))
    columns = jnp.concatenate(vectors, axis=0).T
    lane = iota(columns.shape, 1)
    sums_ref[...] = jnp.where(lane < 32, router_ref[...], columns).astype(half_type)


def input_grad(grads, wq, wk, wv, tokens, gain, grad_middle, bias_parts, second_parts, router_part, sums, after):
    tok_count, feat = tokens.shape
    operands = (*grads, wq, wk, wv, tokens, gain, grad_middle, *bias_parts, second_parts, router_part)
    block = sums.shape[1] // LANES - 1
    return call(
        input_grad_body,
        (out((tok_count, feat), half_type), out(sums.shape, half_type)),
        "input_grad",
        after,
        in_specs=[whole(a) for a in operands] + [pl.BlockSpec(memory_space=pl.ANY)],
        out_specs=[pl.BlockSpec((tok_count, feat), lambda i: (0, 0)), pl.BlockSpec((feat, LANES), lambda i: (0, block))],
        input_output_aliases={len(operands): 1},
    )(*operands, sums)


def output_body(expert_count, returned_ref, slot_ref, probs_ref, middle_ref, result_ref):
    tok_count, feat = middle_ref.shape
    slots = returned_ref.shape[0]
    capacity = slots // expert_count
    part = capacity + EXTRA
    place = iota((1, slots), 1)
    number = place // capacity * part + place % capacity
    for start, size in row_blocks(tok_count):
        rows = pl.ds(start, size)
        lane = iota((size, LANES), 1)
        probs = probs_ref[rows, :]
        table = jnp.zeros((size, slots), full_type)
        for k in range(2):
            slot = slot_ref[rows, k : k + 1]
            gate = jnp.sum(jnp.where(lane == slot // part, probs, 0.0), axis=1, keepdims=True)
            table = jnp.where(number == slot, gate, table)
        high = table.astype(half_type)
        low = (table - high.astype(full_type)).astype(half_type)
        mixed = mul(high, returned_ref[...]) + mul(low, returned_ref[...])
        result_ref[rows, :] = (middle_ref[rows, :] + mixed).astype(half_type)


def block_result(returned, slot, probs, middle, expert_count, after=()):
    return call(
        functools.partial(output_body, expert_count), out(middle.shape, half_type), "block_result", after
    )(returned, slot, probs, middle)


def together(values, before=()):
    anywhere = pl.BlockSpec(memory_space=pl.ANY)
    count = len(values)
    call_all = pl.pallas_call(
        lambda *refs: None,
        out_shape=[out(v.shape, v.dtype) for v in values],
        name="together",
        in_specs=[anywhere] * (count + len(before)),
        out_specs=[anywhere] * count,
        input_output_aliases={i: i for i in range(count)},
        cost_estimate=pl.CostEstimate(flops=1024, bytes_accessed=1024, transcendentals=0),
    )
    return list(call_all(*values, *before))


def mark(values):
    return values.reshape(-1, values.shape[-1])[:8, :LANES]


def behind(values, *before):
    return together([values], before)[0]


def exchange(values, expert_count):
    split = values.reshape(expert_count, -1, values.shape[1])
    swapped = lax.all_to_all(split, "expert", split_axis=0, concat_axis=0, tiled=True)
    return swapped.reshape(values.shape)


def swap(values, axis, bit):
    count = lax.axis_size(axis)
    return lax.ppermute(values, axis, [(i, i ^ (1 << bit)) for i in range(count)])


def bits_of(axis):
    return range(lax.axis_size(axis).bit_length() - 1)


def sum_replicas(pair, fill=()):
    bits = list(bits_of("dp"))
    for n in range(len(bits)):
        pair = together(pair)
        others = [swap(pair[0], "dp", bits[n]), swap(pair[1], "dp", bits[-1 - n])]
        if n == len(bits) - 1 and fill:
            others[0] = behind(others[0], *fill)
        pair = [(v.astype(full_type) + o.astype(full_type)).astype(v.dtype) for v, o in zip(pair, others)]
    return pair


def send_blocks(values, *before):
    split = behind(values, *before).reshape(lax.axis_size("expert"), -1, values.shape[1])
    return lax.all_to_all(split, "expert", split_axis=0, concat_axis=0, tiled=True)


def sum_blocks(parts):
    return jnp.sum(parts.astype(full_type), axis=0).astype(parts.dtype)


def scatter_step(values, low, radix, *before):
    place = lax.axis_index("expert")
    split = values.reshape(values.shape[0] // radix, radix, *values.shape[1:])
    own = (place >> low) & (radix - 1)
    terms = []
    for step in range(radix):
        part = lax.dynamic_slice_in_dim(split, own ^ step, 1, 1)[:, 0]
        if step:
            part = lax.ppermute(part, "expert", [(i, i ^ (step << low)) for i in range(lax.axis_size("expert"))])
        elif before:
            part = behind(part, *before)
        terms.append(part.astype(full_type))
    return functools.reduce(jnp.add, terms).astype(values.dtype)


def scatter_chips(values, *before):
    low = 1
    while values.shape[0] > 1:
        radix = min(4, values.shape[0])
        values = scatter_step(values, low, radix, *before)
        low += radix.bit_length() - 1
        before = ()
    return values[0]


def gather_chips(pair, fill=()):
    bits = list(bits_of("expert"))[1:]
    shapes = [v.shape for v in pair]
    pair = [v.reshape((1,) * len(bits) + v.shape) for v in pair]
    for n in range(len(bits)):
        pair = together(pair)
        steps = [bits[n], bits[-1 - n]]
        others = [swap(v, "expert", bit) for v, bit in zip(pair, steps)]
        if n == len(bits) - 1 and fill:
            others[0] = behind(others[0], *fill)
        pair = [jnp.concatenate([v, o], axis=len(bits) - bit) for v, o, bit in zip(pair, others, steps)]
    return [v.reshape(-1, *shape) for v, shape in zip(pair, shapes)]


def assemble_body(place_ref, early_ref, early_other_ref, late_ref, late_other_ref, *refs):
    out_ref, query_ref, key_ref, value_ref, router_ref = refs[:5]
    vector_refs, held_ref = refs[5:-1], refs[-1]
    rows, feat = out_ref.shape[1:]
    width = feat // HEAD_GROUPS
    own = lax.rem(place_ref[0], 2)
    number = pl.program_id(0)
    for core, early_part, late_part in ((own, early_ref, late_ref), (1 - own, early_other_ref, late_other_ref)):
        early, late = early_part[0].astype(full_type), late_part[0].astype(full_type)
        out_ref[core] = early[:, :feat]
        for kind, ref in enumerate((query_ref, key_ref, value_ref)):
            start = kind * width
            moved = feat + start if kind < 2 else 3 * width + LANES
            ref[core, :, :width] = (early if kind < 2 else late)[:, moved : moved + width]
            ref[core, :, width:] = late[:, start : start + width]
        small = late[:, 3 * width : 3 * width + LANES]
        held_ref[pl.ds(pl.multiple_of((2 * number + core) * rows, 8), rows), :] = small

    @pl.when(number == pl.num_programs(0) - 1)
    def _():
        small = held_ref[...]
        columns = small.T
        router_ref[...] = columns[: router_ref.shape[0]]
        for k, ref in enumerate(vector_refs):
            ref[...] = columns[32 + k]


def assemble(place, early, early_other, late, late_other, expert_count):
    chips, rows, early_width = early.shape
    late_width = late.shape[2]
    feat = 2 * chips * rows
    part = lambda width: pl.BlockSpec((1, rows, width), lambda i, p: (lax.bitwise_xor(i, p[0] // 2), 0, 0))
    matrix, vector, router = out((2 * chips, rows, feat), full_type), out((feat,), full_type), out((expert_count, feat), full_type)
    results = pl.pallas_call(
        assemble_body,
        out_shape=(matrix,) * 4 + (router,) + (vector,) * 7,
        grid_spec=pltpu.PrefetchScalarGridSpec(
            num_scalar_prefetch=1,
            grid=(chips,),
            in_specs=[part(early_width)] * 2 + [part(late_width)] * 2,
            out_specs=[pl.BlockSpec((2, rows, feat), lambda i, p: (i, 0, 0))] * 4
            + [pl.BlockSpec((expert_count, feat), lambda i, p: (0, 0))]
            + [pl.BlockSpec((feat,), lambda i, p: (0,))] * 7,
            scratch_shapes=[pltpu.VMEM((feat, LANES), full_type)],
        ),
        name="assemble",
        compiler_params=pltpu.CompilerParams(vmem_limit_bytes=vmem_bytes),
        cost_estimate=pl.CostEstimate(flops=1024, bytes_accessed=1024, transcendentals=0),
    )(place, early, early_other, late, late_other)
    return [a.reshape(feat, feat) for a in results[:4]], results[4], results[5:]


def widen_body(steps, sum_ref, up_ref, down_ref, up_bias_ref, down_bias_ref):
    share, feat = up_ref.shape[0], sum_ref.shape[1]
    for step in range(steps):
        up_ref[:, step * feat : step * feat + feat] = sum_ref[step * share : step * share + share, :].astype(full_type)
    ends = 2 * steps * share
    down_ref[...] = sum_ref[steps * share : ends, :].astype(full_type)
    last = sum_ref[ends:, :].astype(full_type)
    up_bias_ref[...] = last[0:1, : steps * share]
    down_bias_ref[...] = last[8:9, :share]


def widen(expert_sum, steps, share):
    feat = expert_sum.shape[1]
    return call(
        functools.partial(widen_body, steps),
        (
            out((share, steps * feat), full_type),
            out((steps * share, feat), full_type),
            out((1, steps * share), full_type),
            out((1, share), full_type),
        ),
        "widen",
    )(expert_sum)


def shards(
    tokens,
    first_gain,
    first_shift,
    query_weight,
    query_bias,
    key_weight,
    value_weight,
    value_bias,
    out_weight,
    out_bias,
    second_gain,
    second_shift,
    router,
    expert_up,
    expert_up_bias,
    expert_down,
    expert_down_bias,
    choices,
    priority,
    cotangent,
):
    tok_count, feat = tokens.shape
    expert_count = lax.axis_size("expert")
    capacity = (21 * tok_count + 80 * expert_count - 1) // (80 * expert_count) * 8
    router3 = jnp.pad(jnp.concatenate([router] * 3, axis=1), ((0, 0), (0, LANES - 3 * expert_count)))
    up, down = expert_up[0], expert_down[0]

    replicas = lax.axis_size("dp")
    choice_rows = choices.T
    place, cot_sent = route(choice_rows, priority, cotangent, expert_count, capacity)
    cot = exchange(cot_sent, expert_count)
    first, q, k, v, log_big, log_small, attended, middle, _, probs, sent = front(
        tokens,
        (first_gain, first_shift, query_bias, value_bias, out_bias, second_gain, second_shift),
        (query_weight, key_weight, value_weight, out_weight),
        router3,
        place,
        expert_count,
        capacity,
    )
    rows = exchange(behind(sent, mark(cot)), expert_count)
    grad_act, start = act_grad(cot, down, expert_down_bias)
    slot = slot_columns(choice_rows, place, capacity, (start,))
    act, grad_pre, gate, score, weight_part = expert(
        rows, up, expert_up_bias, grad_act, start, cot, replicas
    )
    expert_sum = lax.psum_scatter(weight_part, "dp", scatter_dimension=0, tiled=True)[0]
    grad_in = expert_grad_in(grad_pre, up, gate, score, capacity, (slot,))
    back = exchange(grad_in, expert_count)
    result = expert_result(act, down, expert_down_bias, (grad_in,))
    grad_middle, grad_attended, wo_grad, router_part, second_parts = combine(
        back,
        slot,
        probs,
        middle,
        cotangent,
        attended,
        out_weight,
        router3,
        second_gain,
        second_shift,
        expert_count,
        capacity,
        (result,),
    )
    out_blocks = send_blocks(wo_grad, back)
    grads, bias_parts, group_parts, before = [], [], [], ()
    for group in range(HEAD_GROUPS):
        dq, dk, dv, group_part, bias_part = attention_grad(
            group, q, k, v, grad_attended, log_big, log_small, first, before
        )
        grads += [dq, dk, dv]
        bias_parts.append(bias_part)
        group_parts.append(group_part)
        before = (dv, out_blocks)
    first_blocks = send_blocks(group_parts[0], mark(out_blocks))
    token_grad, last_part = input_grad(
        grads,
        query_weight,
        key_weight,
        value_weight,
        tokens,
        first_gain,
        grad_middle,
        bias_parts,
        second_parts,
        router_part,
        group_parts[1],
        (),
    )
    late = behind(last_part, mark(first_blocks)).reshape(expert_count, -1, last_part.shape[1])
    late = scatter_chips(scatter_step(late, 0, 2))
    first_sum = sum_blocks(first_blocks)
    width = feat // HEAD_GROUPS
    early = jnp.concatenate([sum_blocks(out_blocks), first_sum[:, : 2 * width]], axis=1)
    returned = exchange(behind(result, late), expert_count)
    late = jnp.concatenate([late, first_sum[:, 2 * width :]], axis=1)
    share, steps = feat // replicas, up.shape[1] // feat
    up_grad, down_grad, up_bias_grad, down_bias_grad = widen(expert_sum, steps, share)
    block_output = block_result(returned, slot, probs, middle, expert_count, (token_grad,))
    early, late = gather_chips(sum_replicas([early, late], (up_grad,)), (block_output,))
    early, late = together([early, late])
    place_here = lax.axis_index("expert").reshape(1)
    (out_grad, query_grad, key_grad, value_grad), router_grad, vectors = assemble(
        place_here, early, swap(early, "expert", 0), late, swap(late, "expert", 0), expert_count
    )
    return (
        block_output,
        token_grad,
        vectors[0],
        vectors[1],
        query_grad,
        vectors[2],
        key_grad,
        value_grad,
        vectors[3],
        out_grad,
        vectors[6],
        vectors[4],
        vectors[5],
        router_grad.T,
        up_grad[None],
        up_bias_grad,
        down_grad[None],
        down_bias_grad,
    )


def solution(mesh):
    tokens_spec = P(("dp", "expert"), None)
    return jax.shard_map(
        shards,
        mesh=mesh,
        in_specs=(tokens_spec,)
        + (P(),) * 12
        + (P("expert", None, None), P("expert", None), P("expert", None, None), P("expert", None))
        + (tokens_spec,) * 3,
        out_specs=(tokens_spec,) * 2
        + (P(),) * 12
        + (P("expert", "dp", None), P("expert", "dp"), P("expert", "dp", None), P("expert", "dp")),
        check_vma=False,
    )
```

```python
import functools

import jax
import jax.numpy as jnp
from jax import lax
from jax.experimental import pallas as pl
from jax.experimental.pallas import tpu as pltpu
from jax.sharding import PartitionSpec as P

HEADS = 12
BIG = 576
SMALL = 196
LANES = 128
EXTRA = 16
HEAD_GROUPS = 2

half_type = jnp.bfloat16
full_type = jnp.float32
norm_eps = 1e-06
masked_score = -1000000000.0
vmem_bytes = 56 * 2**20


def dot_full(left, right, dims):
    return lax.dot_general(left, right, (dims, ((), ())), preferred_element_type=full_type)


def mul(left, right):
    return dot_full(left, right, ((1,), (0,)))


def mul_t(left, right):
    return dot_full(left, right, ((1,), (1,)))


def t_mul(left, right):
    return dot_full(left, right, ((0,), (0,)))


def row_blocks(rows, step=256):
    return [(start, min(step, rows - start)) for start in range(0, rows, step)]


def iota(shape, dim):
    return lax.broadcasted_iota(jnp.int32, shape, dim)


def ones_where(mask):
    return jnp.where(mask, 1.0, 0.0).astype(half_type)


def normalize(values):
    row_mean = jnp.mean(values, axis=-1, keepdims=True)
    centered = values - row_mean
    inverse = lax.rsqrt(jnp.mean(centered * centered, axis=-1, keepdims=True) + norm_eps)
    return centered * inverse, inverse


def norm_backward(upstream, normed, inverse, norm_gain):
    scaled = upstream * norm_gain
    first_mean = jnp.mean(scaled, axis=-1, keepdims=True)
    second_mean = jnp.mean(scaled * normed, axis=-1, keepdims=True)
    return inverse * (scaled - first_mean - normed * second_mean)


def split_thirds(values, lane, expert_count):
    high = values.astype(half_type).astype(full_type)
    rest = values - high
    middle = rest.astype(half_type).astype(full_type)
    low = rest - middle
    picked = jnp.where(lane < expert_count, high, jnp.where(lane < 2 * expert_count, middle, low))
    return jnp.where(lane < 3 * expert_count, picked, 0.0).astype(half_type)


def call(body, out_shape, name, after=(), grid=(1,), in_specs=None, flops=1024, **kwargs):
    def build(*operands):
        specs = list(in_specs) if in_specs else [whole(a) for a in operands]
        used = len(specs)
        if "out_specs" not in kwargs:
            kwargs["out_specs"] = jax.tree.map(whole, out_shape)

        def inner(*refs):
            body(*refs[:used], *refs[used + len(after) :])

        return pl.pallas_call(
            inner,
            out_shape=out_shape,
            name=name,
            grid=grid,
            in_specs=specs + [pl.BlockSpec(memory_space=pl.ANY)] * len(after),
            compiler_params=pltpu.CompilerParams(vmem_limit_bytes=vmem_bytes),
            cost_estimate=pl.CostEstimate(flops=flops, bytes_accessed=1024, transcendentals=0),
            **kwargs,
        )(*operands, *after)

    return build


def whole(array):
    zeros = (0,) * len(array.shape)
    return pl.BlockSpec(array.shape, lambda *_: zeros)


def out(shape, dtype):
    return jax.ShapeDtypeStruct(shape, dtype)


def vec(ref):
    return ref[...].reshape(1, -1)


def for_experts(expert_count, step):
    if expert_count <= 8:
        for e in range(expert_count):
            step(e)
    else:
        lax.fori_loop(0, expert_count, lambda e, c: (step(e), c)[1], 0)


def expert_rows(e, capacity):
    if isinstance(e, int):
        return pl.ds(e * capacity, capacity)
    return pl.ds(pl.multiple_of(e * capacity, capacity), capacity)


def row_thirds(row):
    high = row.astype(half_type).astype(full_type)
    rest = row - high
    middle = rest.astype(half_type).astype(full_type)
    sub = iota((8, row.shape[1]), 0)
    picked = jnp.where(sub == 0, high, jnp.where(sub == 1, middle, jnp.where(sub == 2, rest - middle, 0.0)))
    return picked.astype(half_type)


def thirds_to_lanes(thirds):
    return t_mul(thirds, jnp.ones((thirds.shape[0], LANES), half_type))


def store_thirds(ref, start, row):
    ref[pl.ds(start, EXTRA), :] = jnp.zeros((EXTRA, ref.shape[1]), ref.dtype)
    thirds = jnp.concatenate([row_thirds(row), jnp.zeros((EXTRA - 8, row.shape[1]), half_type)], axis=0)
    ref[pl.ds(start, EXTRA), 0 : row.shape[1]] = thirds


def part_start(e, size, offset=0):
    if isinstance(e, int):
        return e * size + offset
    return pl.multiple_of(e * size + offset, 16)


def lanes_to_row(values):
    ones = jnp.ones((8, LANES), half_type)
    high = values.astype(half_type)
    rest = values - high.astype(full_type)
    middle = rest.astype(half_type)
    low = (rest - middle.astype(full_type)).astype(half_type)
    return (mul_t(ones, high) + mul_t(ones, middle) + mul_t(ones, low))[0:1]


def rank_column(rows):
    tok_count = rows.shape[1]
    rows = jnp.concatenate([rows, jnp.zeros((8 - rows.shape[0], tok_count), jnp.int32)], axis=0)
    return rows.astype(full_type).T.astype(jnp.int32)


def route_body(expert_count, capacity, rows_ref, rank_ref, cot_ref, place_ref, sent_ref):
    tok_count = cot_ref.shape[0]
    padded = place_ref.shape[0]
    sub = iota((padded, tok_count), 0)
    first, second = rows_ref[0:1, :], rows_ref[1:2, :]
    first_hot, second_hot = ones_where(first == sub), ones_where(second == sub)
    earlier = ones_where(rank_column(rank_ref[...])[:, 0:1] < rank_ref[...])
    first_total = jnp.sum(first_hot.astype(full_type), axis=1, keepdims=True)
    counts = mul(jnp.concatenate([first_hot, second_hot], axis=0), earlier)
    first_count, second_count = counts[:padded], counts[padded:] + first_total
    place = jnp.where(
        (first == sub) & (first_count < capacity),
        first_count,
        jnp.where((second == sub) & (second_count < capacity), second_count, -1.0),
    )
    place_ref[...] = place.astype(jnp.int32)
    cot = cot_ref[...]
    within = iota((capacity, tok_count), 0)

    def send(e):
        hot = ones_where(place_ref[pl.ds(e, 1), :] == within)
        sent_ref[pl.ds(part_start(e, capacity), capacity), :] = mul(hot, cot).astype(half_type)

    for_experts(expert_count, send)


def route(choice_rows, priority, cotangent, expert_count, capacity):
    tok_count, feat = cotangent.shape
    padded = -(-expert_count // 32) * 32
    return call(
        functools.partial(route_body, expert_count, capacity),
        (out((padded, tok_count), jnp.int32), out((expert_count * capacity, feat), half_type)),
        "route",
    )(choice_rows, priority, cotangent)


def slots_body(capacity, rows_ref, place_ref, slot_ref):
    part = capacity + EXTRA
    padded, tok_count = place_ref.shape
    sub = iota((padded, tok_count), 0)
    slots = []
    for k in range(2):
        place = jnp.sum(jnp.where(rows_ref[k : k + 1, :] == sub, place_ref[...], 0), axis=0, keepdims=True)
        slots.append(jnp.where(place < 0, -1, rows_ref[k : k + 1, :] * part + place))
    slot_ref[...] = rank_column(jnp.concatenate(slots, axis=0))[:, 0:2]


def slot_columns(choice_rows, place, capacity, after):
    return call(
        functools.partial(slots_body, capacity), out((choice_rows.shape[1], 2), jnp.int32), "slot_columns", after
    )(choice_rows, place)


def image_mask(size):
    key_image = iota((size, 1), 0) // SMALL
    query_image = iota((1, size), 1) // SMALL
    return key_image == query_image


def images(tok_count):
    return ((0, BIG), (BIG, tok_count - BIG))


def head_lanes(value, head):
    lane = iota((1, LANES), 1)
    return jnp.where((lane < LANES // 2) == (head == 0), value, jnp.zeros((), value.dtype))


def front_body(
    expert_count,
    capacity,
    tokens_ref,
    gain_ref,
    shift_ref,
    wq_ref,
    bq_ref,
    wk_ref,
    wv_ref,
    bv_ref,
    wo_ref,
    bo_ref,
    gain2_ref,
    shift2_ref,
    router_ref,
    place_ref,
    first_ref,
    q_ref,
    k_ref,
    v_ref,
    log_big_ref,
    log_small_ref,
    attended_ref,
    middle_ref,
    second_ref,
    probs_ref,
    sent_ref,
):
    tok_count, feat = tokens_ref.shape
    scale = (feat // HEADS) ** (-0.5)
    for start, size in row_blocks(tok_count):
        rows = pl.ds(start, size)
        normed, _ = normalize(tokens_ref[rows, :].astype(full_type))
        low = (normed * vec(gain_ref) + vec(shift_ref)).astype(half_type)
        first_ref[rows, :] = low
        q_ref[rows, :] = (mul(low, wq_ref[...]) + vec(bq_ref)).astype(half_type)
        k_ref[rows, :] = mul(low, wk_ref[...]).astype(half_type)
        v_ref[rows, :] = (mul(low, wv_ref[...]) + vec(bv_ref)).astype(half_type)

    def pair(number, carry):
        lanes = pl.ds(pl.multiple_of(number * LANES, LANES), LANES)
        for place, (start, size) in enumerate(images(tok_count)):
            rows = pl.ds(start, size)
            query, key, value = q_ref[rows, lanes], k_ref[rows, lanes], v_ref[rows, lanes]
            key = key * jnp.asarray(scale, half_type)
            log_ref = (log_big_ref, log_small_ref)[place]
            value_t = value.T
            halves = []
            for head in range(2):
                scores = mul_t(head_lanes(key, head), query)
                if place:
                    scores = jnp.where(image_mask(size), scores, masked_score)
                top = jnp.max(scores, axis=0, keepdims=True)
                weights = jnp.exp(scores - top)
                total = jnp.sum(weights, axis=0, keepdims=True)
                log_ref[pl.ds(2 * number + head, 1), :] = top + jnp.log(total)
                mixed = mul(value_t[head * 64 : head * 64 + 64], weights.astype(half_type))
                halves.append(mixed * (1.0 / total))
            attended_ref[rows, lanes] = jnp.concatenate(halves, axis=0).T.astype(half_type)
        return carry

    lax.fori_loop(0, HEADS // 2, pair, 0)

    for start, size in row_blocks(tok_count):
        rows = pl.ds(start, size)
        lane = iota((size, LANES), 1)
        middle = tokens_ref[rows, :].astype(full_type) + mul(attended_ref[rows, :], wo_ref[...]) + vec(bo_ref)
        middle_ref[rows, :] = middle
        normed, _ = normalize(middle)
        low = (normed * vec(gain2_ref) + vec(shift2_ref)).astype(half_type)
        second_ref[rows, :] = low
        logits = jnp.where(lane < 3 * expert_count, mul(low, router_ref[...]), masked_score)
        top = jnp.max(logits, axis=1, keepdims=True)
        raised = jnp.exp(logits - top)
        total = jnp.sum(jnp.where(lane < expert_count, raised, 0.0), axis=1, keepdims=True)
        probs_ref[rows, :] = raised / total

    low = second_ref[...]
    lane = iota((tok_count, LANES), 1)
    thirds = split_thirds(probs_ref[...], lane, expert_count)
    within = iota((capacity, tok_count), 0)
    slot_lane = iota((capacity, LANES), 1)

    def send(e):
        hot = ones_where(place_ref[pl.ds(e, 1), :] == within)
        rows = mul(hot, low).astype(half_type)
        part = capacity + EXTRA
        sent_ref[pl.ds(part_start(e, part), capacity), :] = rows
        gates = mul(hot, thirds)
        own = (slot_lane == e) | (slot_lane == e + expert_count) | (slot_lane == e + 2 * expert_count)
        picked = jnp.where(own, gates, 0.0).astype(half_type)
        store_thirds(sent_ref, part_start(e, part, capacity), mul_t(jnp.ones((8, LANES), half_type), picked)[0:1])

    for_experts(expert_count, send)


def front(tokens, vectors, weights, router3, place, expert_count, capacity):
    tok_count, feat = tokens.shape
    gain, shift, bq, bv, bo, gain2, shift2 = vectors
    wq, wk, wv, wo = weights
    low = out((tok_count, feat), half_type)
    return call(
        functools.partial(front_body, expert_count, capacity),
        (
            low,
            low,
            low,
            low,
            out((HEADS, BIG), full_type),
            out((HEADS, tok_count - BIG), full_type),
            low,
            out((tok_count, feat), full_type),
            low,
            out((tok_count, LANES), full_type),
            out((expert_count * (capacity + EXTRA), feat), half_type),
        ),
        "front",
    )(tokens, gain, shift, wq, bq, wk, wv, bv, wo, bo, gain2, shift2, router3, place)


def fold_lanes(values):
    folded = values[:, :LANES]
    for start in range(LANES, values.shape[1], LANES):
        folded = folded + values[:, start : start + LANES]
    return folded


def act_grad_body(cot_ref, down_ref, down_bias_ref, grad_act_ref, score_ref):
    for start, size in row_blocks(cot_ref.shape[0], 512):
        rows = pl.ds(start, size)
        grad_act_ref[rows, :] = mul_t(cot_ref[rows, :], down_ref[...]).astype(half_type)

        @pl.when(pl.program_id(0) == 0)
        def _():
            score_ref[rows, :] = fold_lanes(cot_ref[rows, :].astype(full_type) * down_bias_ref[...])


def act_grad(cot, down, down_bias, step=512):
    slots, feat = cot.shape
    hidden = down.shape[0]
    return call(
        act_grad_body,
        (out((slots, hidden), half_type), out((slots, LANES), full_type)),
        "act_grad",
        grid=(hidden // step,),
        in_specs=[whole(cot), pl.BlockSpec((step, feat), lambda f: (f, 0)), whole(down_bias)],
        out_specs=[pl.BlockSpec((slots, step), lambda f: (0, f)), pl.BlockSpec((slots, LANES), lambda f: (0, 0))],
    )(cot, down, down_bias)


def gelu_parts(values):
    area = 0.5 + 0.5 * lax.erf(values * 0.7071067811865476)
    bell = jnp.exp(values * values * -0.5) * 0.3989422804014327
    return values * area, area + values * bell


def expert_body(rows_ref, up_ref, up_bias_ref, grad_act_ref, start_ref, cot_ref, act_ref, grad_pre_ref, gate_ref, score_ref, sum_ref, x_ref, gated_ref, grad_ref, bias_ref, up_out_ref, down_out_ref, cot_held, start_held, sems, load_sems):
    slots, feat = cot_ref.shape
    replicas, share = up_out_ref.shape[1:3]
    steps = (sum_ref.shape[1] - EXTRA) // share // 2
    part = rows_ref.shape[0] // (rows_ref.shape[0] - slots) * EXTRA
    capacity = part - EXTRA
    number = pl.program_id(0)
    down_rows = steps * share
    size = min(down_rows, feat)

    def copies(step):
        pairs = [(up_out_ref.at[step % 2], sum_ref.at[:, pl.ds(step * share, share), :])]
        for piece in range(feat // size):
            row = step * feat + piece * size
            target = sum_ref.at[row // down_rows, pl.ds(down_rows + row % down_rows, size), :]
            pairs.append((down_out_ref.at[step % 2, pl.ds(piece * size, size)], target))
        return [pltpu.make_async_copy(a, b, sems.at[step, i]) for i, (a, b) in enumerate(pairs)]

    loads = [
        pltpu.make_async_copy(cot_ref, cot_held, load_sems.at[0]),
        pltpu.make_async_copy(start_ref, start_held, load_sems.at[1]),
    ]

    @pl.when(number == 0)
    def _():
        for load in loads:
            load.start()
        for e in range(slots // capacity):
            rows = pl.ds(e * capacity, capacity)
            gate_ref[rows, :] = thirds_to_lanes(rows_ref[pl.ds(e * part + capacity, EXTRA), 0:capacity])
            x_ref[rows, :] = rows_ref[pl.ds(e * part, capacity), :]
        score_ref[...] = jnp.zeros(score_ref.shape, full_type)

    blocks = row_blocks(slots, 512)
    pre = mul(x_ref[pl.ds(*blocks[0]), :], up_ref[...])
    bias_grad = jnp.zeros((1, feat), full_type)
    for b, block in enumerate(blocks):
        rows = pl.ds(*block)
        if b + 1 < len(blocks):
            later = mul(x_ref[pl.ds(*blocks[b + 1]), :], up_ref[...])
        act, slope = gelu_parts(pre + up_bias_ref[...])
        act_ref[rows, :] = act.astype(half_type)
        grad_act = grad_act_ref[rows, :].astype(full_type)
        score_ref[rows, :] += fold_lanes(act * grad_act)
        grad_pre_ref[rows, :] = (grad_act * slope).astype(half_type)
        pre = later
    @pl.when(number == 0)
    def _():
        for load in loads:
            load.wait()
        total = jnp.zeros((1, feat), full_type)
        for e in range(slots // capacity):
            rows = pl.ds(e * capacity, capacity)
            wide = jnp.concatenate([gate_ref[rows, :]] * (feat // LANES), axis=1)
            gated_ref[rows, :] = (x_ref[rows, :].astype(full_type) * wide).astype(half_type)
            grad = (cot_held[rows, :].astype(full_type) * wide).astype(half_type)
            grad_ref[rows, :] = grad
            total = total + jnp.sum(grad.astype(full_type), axis=0, keepdims=True)
        bias_ref[...] = jnp.zeros(bias_ref.shape, half_type)
        for z in range(replicas):
            bias_ref[z, 8:9, 0:share] = total[:, z * share : z * share + share].astype(half_type)

    for step in range(2, steps):

        @pl.when(number == step)
        def _():
            for copy in copies(step - 2):
                copy.wait()

    up_out_ref[number % 2] = t_mul(gated_ref[...], grad_pre_ref[...]).astype(half_type).reshape(replicas, share, feat)
    down_out_ref[number % 2] = t_mul(act_ref[...], grad_ref[...]).astype(half_type)
    for start, size_b in blocks:
        rows = pl.ds(start, size_b)
        wide = jnp.concatenate([gate_ref[rows, :]] * (feat // LANES), axis=1)
        bias_grad = bias_grad + jnp.sum(grad_pre_ref[rows, :].astype(full_type) * wide, axis=0, keepdims=True)
    for step in range(steps):

        @pl.when(number == step)
        def _():
            for piece in range(feat // size):
                z = (step * feat + piece * size) // down_rows
                bias_ref[z, 0:1, 0:size] = bias_grad[:, piece * size : piece * size + size].astype(half_type)
            for copy in copies(step):
                copy.start()

    @pl.when(number == steps - 1)
    def _():
        last = pltpu.make_async_copy(bias_ref, sum_ref.at[:, pl.ds(2 * down_rows, EXTRA), :], sems.at[0, 0])
        last.start()
        score_ref[...] = (score_ref[...] + start_held[...]) * gate_ref[...]
        for step in range(steps - 2, steps):
            for copy in copies(step):
                copy.wait()
        last.wait()


def expert(rows, up, up_bias, grad_act, start, cot, replicas):
    slots, feat = cot.shape
    hidden = up.shape[1]
    steps, share = hidden // feat, feat // replicas
    wide = pl.BlockSpec((slots, feat), lambda f: (0, f))
    once = lambda a: pl.BlockSpec(a.shape, lambda f: (0, 0), pipeline_mode=pl.Buffered(1))
    lanes = out((slots, LANES), full_type)
    return call(
        expert_body,
        (
            out((slots, hidden), half_type),
            out((slots, hidden), half_type),
            lanes,
            lanes,
            out((replicas, 2 * steps * share + EXTRA, feat), half_type),
        ),
        "expert",
        grid=(steps,),
        in_specs=[
            once(rows),
            pl.BlockSpec((feat, feat), lambda f: (0, f)),
            pl.BlockSpec((1, feat), lambda f: (0, f)),
            wide,
            pl.BlockSpec(memory_space=pl.ANY),
            pl.BlockSpec(memory_space=pl.ANY),
        ],
        out_specs=[
            wide,
            wide,
            whole(lanes),
            whole(lanes),
            pl.BlockSpec(memory_space=pl.ANY),
        ],
        scratch_shapes=[
            pltpu.VMEM((slots, feat), half_type),
            pltpu.VMEM((slots, feat), half_type),
            pltpu.VMEM((slots, feat), half_type),
            pltpu.VMEM((replicas, EXTRA, feat), half_type),
            pltpu.VMEM((2, replicas, share, feat), half_type),
            pltpu.VMEM((2, feat, feat), half_type),
            pltpu.VMEM((slots, feat), half_type),
            pltpu.VMEM((slots, LANES), full_type),
            pltpu.SemaphoreType.DMA((steps, 1 + max(1, feat // (steps * share)))),
            pltpu.SemaphoreType.DMA((2,)),
        ],
    )(rows, up, up_bias, grad_act, start, cot)


def grad_in_body(capacity, grad_pre_ref, up_ref, gate_ref, score_ref, grad_in_ref):
    part = capacity + EXTRA
    size, feat = grad_pre_ref.shape[0], up_ref.shape[0]
    grad = mul_t(grad_pre_ref[...], up_ref[...])
    grad = grad * jnp.concatenate([gate_ref[...]] * (feat // LANES), axis=1)
    for e in range(size // capacity):
        grad_in_ref[pl.ds(e * part, capacity), :] = grad[e * capacity : e * capacity + capacity].astype(half_type)
        store_thirds(grad_in_ref, e * part + capacity, lanes_to_row(score_ref[e * capacity : e * capacity + capacity, :]))


def expert_grad_in(grad_pre, up, gate, score, capacity, after, step=512):
    slots, hidden = grad_pre.shape
    feat = up.shape[0]
    part = capacity + EXTRA
    lanes = pl.BlockSpec((step, LANES), lambda r: (r, 0))
    return call(
        functools.partial(grad_in_body, capacity),
        out((slots // capacity * part, feat), half_type),
        "grad_in",
        after,
        flops=4 * 10**11,
        grid=(slots // step,),
        in_specs=[pl.BlockSpec((step, hidden), lambda r: (r, 0)), whole(up), lanes, lanes],
        out_specs=pl.BlockSpec((step // capacity * part, feat), lambda r: (r, 0)),
    )(grad_pre, up, gate, score)


def result_body(act_ref, down_ref, down_bias_ref, result_ref):
    result_ref[...] = (mul(act_ref[...], down_ref[...]) + down_bias_ref[...]).astype(half_type)


def expert_result(act, down, down_bias, after=(), step=512):
    slots, hidden = act.shape
    feat = down.shape[1]
    return call(
        result_body,
        out((slots, feat), half_type),
        "result",
        after,
        grid=(slots // step,),
        in_specs=[pl.BlockSpec((step, hidden), lambda r: (r, 0)), whole(down), whole(down_bias)],
        out_specs=pl.BlockSpec((step, feat), lambda r: (r, 0)),
    )(act, down, down_bias)


def combine_body(
    expert_count,
    capacity,
    back_ref,
    slot_ref,
    probs_ref,
    middle_ref,
    cot_ref,
    attended_ref,
    wo_ref,
    router_ref,
    gain_ref,
    shift_ref,
    grad_middle_ref,
    grad_attended_ref,
    wo_grad_ref,
    router_grad_ref,
    vector_ref,
):
    tok_count, feat = cot_ref.shape
    slots = back_ref.shape[0]
    part = capacity + EXTRA
    lane = iota((capacity, LANES), 1)
    tables = []
    for e in range(expert_count):
        same = (lane == e) | (lane == e + expert_count) | (lane == e + 2 * expert_count)
        score = thirds_to_lanes(back_ref[pl.ds(e * part + capacity, EXTRA), 0:capacity])
        tables.append(split_thirds(jnp.where(same, score, 0.0), lane, expert_count))
        tables.append(jnp.zeros((EXTRA, LANES), half_type))
    table = jnp.concatenate(tables, axis=0)
    wo_grad = jnp.zeros(wo_grad_ref.shape, full_type)
    router_grad = jnp.zeros(router_grad_ref.shape, full_type)
    gain_grad = jnp.zeros((1, feat), full_type)
    shift_grad = jnp.zeros((1, feat), full_type)
    bias_grad = jnp.zeros((1, feat), full_type)
    for start, size in row_blocks(tok_count):
        rows = pl.ds(start, size)
        number = iota((size, slots), 1)
        hot = ones_where((number == slot_ref[rows, 0:1]) | (number == slot_ref[rows, 1:2]))
        lane = iota((size, LANES), 1)
        folded = mul(hot, table)
        folded = folded + pltpu.roll(folded, LANES - expert_count, 1) + pltpu.roll(folded, LANES - 2 * expert_count, 1)
        probs = jnp.where(lane < expert_count, probs_ref[rows, :], 0.0)
        scores = jnp.where(lane < expert_count, folded, 0.0)
        grad_logits = scores - probs * jnp.sum(scores, axis=1, keepdims=True)
        grad_logits = grad_logits + pltpu.roll(grad_logits, expert_count, 1) + pltpu.roll(grad_logits, 2 * expert_count, 1)
        thirds = split_thirds(grad_logits, lane, expert_count)
        upstream = mul_t(thirds, router_ref[...]) + mul(hot, back_ref[...])
        normed, inverse = normalize(middle_ref[rows, :])
        low = (normed * vec(gain_ref) + vec(shift_ref)).astype(half_type)
        router_grad = router_grad + t_mul(low, thirds)
        gain_grad = gain_grad + jnp.sum(upstream * normed, axis=0, keepdims=True)
        shift_grad = shift_grad + jnp.sum(upstream, axis=0, keepdims=True)
        grad_middle = cot_ref[rows, :].astype(full_type) + norm_backward(upstream, normed, inverse, vec(gain_ref))
        grad_middle_ref[rows, :] = grad_middle
        branch = grad_middle.astype(half_type)
        bias_grad = bias_grad + jnp.sum(branch.astype(full_type), axis=0, keepdims=True)
        grad_attended_ref[rows, :] = mul_t(branch, wo_ref[...]).astype(half_type)
        wo_grad = wo_grad + t_mul(attended_ref[rows, :], branch)
    wo_grad_ref[...] = wo_grad.astype(half_type)
    router_grad = router_grad + pltpu.roll(router_grad, LANES - expert_count, 1) + pltpu.roll(router_grad, LANES - 2 * expert_count, 1)
    router_grad_ref[...] = router_grad
    vector_ref[0:1, :] = gain_grad
    vector_ref[1:2, :] = shift_grad
    vector_ref[2:3, :] = bias_grad


def combine(back, slot, probs, middle, cot, attended, wo, router3, gain, shift, expert_count, capacity, after=()):
    tok_count, feat = cot.shape
    return call(
        functools.partial(combine_body, expert_count, capacity),
        (
            out((tok_count, feat), full_type),
            out((tok_count, feat), half_type),
            out((feat, feat), half_type),
            out((feat, LANES), full_type),
            out((3, feat), full_type),
        ),
        "combine",
        after,
    )(back, slot, probs, middle, cot, attended, wo, router3, gain, shift)


def attention_grad_body(first_head, q_ref, k_ref, v_ref, grad_ref, log_big_ref, log_small_ref, first_ref, dq_ref, dk_ref, dv_ref, weight_ref, bias_ref):
    tok_count, width = q_ref.shape
    scale = 64 ** (-0.5)

    def pair(number, carry):
        lanes = pl.ds(pl.multiple_of(number * LANES, LANES), LANES)
        for place, (start, size) in enumerate(images(tok_count)):
            rows = pl.ds(start, size)
            query, key, value, grad = q_ref[rows, lanes], k_ref[rows, lanes], v_ref[rows, lanes], grad_ref[rows, lanes]
            key = key * jnp.asarray(scale, half_type)
            log_ref = (log_big_ref, log_small_ref)[place]
            key_t = key.T
            halves = []
            grad_value = jnp.zeros((size, LANES), full_type)
            grad_key = jnp.zeros((size, LANES), full_type)
            for head in range(2):
                scores = mul_t(head_lanes(key, head), query)
                if place:
                    scores = jnp.where(image_mask(size), scores, masked_score)
                probs = jnp.exp(scores - log_ref[pl.ds(first_head + 2 * number + head, 1), :])
                grad_probs = mul_t(head_lanes(value, head), grad)
                inner = jnp.sum(grad_probs * probs, axis=0, keepdims=True)
                grad_scores = (probs * (grad_probs - inner)).astype(half_type)
                grad_value = grad_value + mul(probs.astype(half_type), head_lanes(grad, head))
                grad_key = grad_key + mul(grad_scores, head_lanes(query, head))
                halves.append(mul(key_t[head * 64 : head * 64 + 64], grad_scores))
            dv_ref[rows, lanes] = grad_value.astype(half_type)
            dk_ref[rows, lanes] = (grad_key * scale).astype(half_type)
            dq_ref[rows, lanes] = jnp.concatenate(halves, axis=0).T.astype(half_type)
        return carry

    lax.fori_loop(0, width // LANES, pair, 0)
    first = first_ref[...]
    for kind, grad_ref in enumerate((dq_ref, dk_ref, dv_ref)):
        weight_ref[:, kind * width : kind * width + width] = t_mul(first, grad_ref[...]).astype(half_type)
    bias_ref[0:1, :] = jnp.sum(dq_ref[...].astype(full_type), axis=0, keepdims=True)
    bias_ref[1:2, :] = jnp.sum(dv_ref[...].astype(full_type), axis=0, keepdims=True)


def attention_grad(group, q, k, v, grad, log_big, log_small, first, after=()):
    tok_count, feat = q.shape
    width = feat // HEAD_GROUPS
    columns = pl.BlockSpec((tok_count, width), lambda i: (0, group))
    low = out((tok_count, width), half_type)
    grads = out((feat, 3 * width + (LANES if group == HEAD_GROUPS - 1 else 0)), half_type)
    return call(
        functools.partial(attention_grad_body, group * HEADS // HEAD_GROUPS),
        (low, low, low, grads, out((2, width), full_type)),
        f"attention_grad_{group}",
        after,
        in_specs=[columns, columns, columns, columns, whole(log_big), whole(log_small), whole(first)],
    )(q, k, v, grad, log_big, log_small, first)


def input_grad_body(*refs):
    grads = refs[: 3 * HEAD_GROUPS]
    refs = refs[3 * HEAD_GROUPS :]
    wq_ref, wk_ref, wv_ref, tokens_ref, gain_ref, middle_ref, bias_a_ref, bias_b_ref, second_ref, router_ref = refs[:10]
    result_ref, sums_ref = refs[11:]
    tok_count, feat = tokens_ref.shape
    width = feat // HEAD_GROUPS
    gain_grad = jnp.zeros((1, feat), full_type)
    shift_grad = jnp.zeros((1, feat), full_type)
    for start, size in row_blocks(tok_count):
        rows = pl.ds(start, size)
        upstream = jnp.zeros((size, feat), full_type)
        for group in range(HEAD_GROUPS):
            lanes = pl.ds(group * width, width)
            for grad_ref, weight_ref in zip(grads[3 * group : 3 * group + 3], (wq_ref, wk_ref, wv_ref)):
                upstream = upstream + mul_t(grad_ref[rows, :], weight_ref[:, lanes])
        normed, inverse = normalize(tokens_ref[rows, :].astype(full_type))
        gain_grad = gain_grad + jnp.sum(upstream * normed, axis=0, keepdims=True)
        shift_grad = shift_grad + jnp.sum(upstream, axis=0, keepdims=True)
        grad = middle_ref[rows, :] + norm_backward(upstream, normed, inverse, vec(gain_ref))
        result_ref[rows, :] = grad.astype(half_type)
    biases = jnp.concatenate([bias_a_ref[...], bias_b_ref[...]], axis=1)
    vectors = [jnp.zeros((32, feat), full_type), gain_grad, shift_grad, biases, second_ref[...]]
    vectors.append(jnp.zeros((LANES - 39, feat), full_type))
    columns = jnp.concatenate(vectors, axis=0).T
    lane = iota(columns.shape, 1)
    sums_ref[...] = jnp.where(lane < 32, router_ref[...], columns).astype(half_type)


def input_grad(grads, wq, wk, wv, tokens, gain, grad_middle, bias_parts, second_parts, router_part, sums, after):
    tok_count, feat = tokens.shape
    operands = (*grads, wq, wk, wv, tokens, gain, grad_middle, *bias_parts, second_parts, router_part)
    block = sums.shape[1] // LANES - 1
    return call(
        input_grad_body,
        (out((tok_count, feat), half_type), out(sums.shape, half_type)),
        "input_grad",
        after,
        in_specs=[whole(a) for a in operands] + [pl.BlockSpec(memory_space=pl.ANY)],
        out_specs=[pl.BlockSpec((tok_count, feat), lambda i: (0, 0)), pl.BlockSpec((feat, LANES), lambda i: (0, block))],
        input_output_aliases={len(operands): 1},
    )(*operands, sums)


def output_body(expert_count, returned_ref, slot_ref, probs_ref, middle_ref, result_ref):
    tok_count, feat = middle_ref.shape
    slots = returned_ref.shape[0]
    capacity = slots // expert_count
    part = capacity + EXTRA
    place = iota((1, slots), 1)
    number = place // capacity * part + place % capacity
    for start, size in row_blocks(tok_count):
        rows = pl.ds(start, size)
        lane = iota((size, LANES), 1)
        probs = probs_ref[rows, :]
        table = jnp.zeros((size, slots), full_type)
        for k in range(2):
            slot = slot_ref[rows, k : k + 1]
            gate = jnp.sum(jnp.where(lane == slot // part, probs, 0.0), axis=1, keepdims=True)
            table = jnp.where(number == slot, gate, table)
        high = table.astype(half_type)
        low = (table - high.astype(full_type)).astype(half_type)
        mixed = mul(high, returned_ref[...]) + mul(low, returned_ref[...])
        result_ref[rows, :] = (middle_ref[rows, :] + mixed).astype(half_type)


def block_result(returned, slot, probs, middle, expert_count, after=()):
    return call(
        functools.partial(output_body, expert_count), out(middle.shape, half_type), "block_result", after
    )(returned, slot, probs, middle)


def together(values, before=()):
    anywhere = pl.BlockSpec(memory_space=pl.ANY)
    count = len(values)
    call_all = pl.pallas_call(
        lambda *refs: None,
        out_shape=[out(v.shape, v.dtype) for v in values],
        name="together",
        in_specs=[anywhere] * (count + len(before)),
        out_specs=[anywhere] * count,
        input_output_aliases={i: i for i in range(count)},
        cost_estimate=pl.CostEstimate(flops=1024, bytes_accessed=1024, transcendentals=0),
    )
    return list(call_all(*values, *before))


def mark(values):
    return values.reshape(-1, values.shape[-1])[:8, :LANES]


def behind(values, *before):
    return together([values], before)[0]


def exchange(values, expert_count):
    split = values.reshape(expert_count, -1, values.shape[1])
    swapped = lax.all_to_all(split, "expert", split_axis=0, concat_axis=0, tiled=True)
    return swapped.reshape(values.shape)


def swap(values, axis, bit):
    count = lax.axis_size(axis)
    return lax.ppermute(values, axis, [(i, i ^ (1 << bit)) for i in range(count)])


def bits_of(axis):
    return range(lax.axis_size(axis).bit_length() - 1)


def sum_replicas(pair, fill=()):
    bits = list(bits_of("dp"))
    for n in range(len(bits)):
        pair = together(pair)
        others = [swap(pair[0], "dp", bits[n]), swap(pair[1], "dp", bits[-1 - n])]
        if n == len(bits) - 1 and fill:
            others[0] = behind(others[0], *fill)
        pair = [(v.astype(full_type) + o.astype(full_type)).astype(v.dtype) for v, o in zip(pair, others)]
    return pair


def send_blocks(values, *before):
    split = behind(values, *before).reshape(lax.axis_size("expert"), -1, values.shape[1])
    return lax.all_to_all(split, "expert", split_axis=0, concat_axis=0, tiled=True)


def sum_blocks(parts):
    return jnp.sum(parts.astype(full_type), axis=0).astype(parts.dtype)


def scatter_step(values, low, radix, *before):
    place = lax.axis_index("expert")
    split = values.reshape(values.shape[0] // radix, radix, *values.shape[1:])
    own = (place >> low) & (radix - 1)
    terms = []
    for step in range(radix):
        part = lax.dynamic_slice_in_dim(split, own ^ step, 1, 1)[:, 0]
        if step:
            part = lax.ppermute(part, "expert", [(i, i ^ (step << low)) for i in range(lax.axis_size("expert"))])
        elif before:
            part = behind(part, *before)
        terms.append(part.astype(full_type))
    return functools.reduce(jnp.add, terms).astype(values.dtype)


def scatter_chips(values, *before):
    low = 1
    while values.shape[0] > 1:
        radix = min(4, values.shape[0])
        values = scatter_step(values, low, radix, *before)
        low += radix.bit_length() - 1
        before = ()
    return values[0]


def gather_chips(pair, fill=()):
    bits = list(bits_of("expert"))[1:]
    shapes = [v.shape for v in pair]
    pair = [v.reshape((1,) * len(bits) + v.shape) for v in pair]
    for n in range(len(bits)):
        pair = together(pair)
        steps = [bits[n], bits[-1 - n]]
        others = [swap(v, "expert", bit) for v, bit in zip(pair, steps)]
        if n < len(bits) - 1:
            pair = [jnp.concatenate([v, o], axis=len(bits) - bit) for v, o, bit in zip(pair, others, steps)]
    if fill:
        others = together(others, fill)
    return [[a.reshape(-1, *shape) for a in both] for *both, shape in zip(pair, others, shapes)]


def assemble_body(place_ref, *refs):
    pieces, refs = refs[:8], refs[8:]
    out_ref, query_ref, key_ref, value_ref, router_ref = refs[:5]
    vector_refs, held_ref = refs[5:-1], refs[-1]
    rows, feat = out_ref.shape[1:]
    width = feat // HEAD_GROUPS
    own = lax.rem(place_ref[0], 2)
    number, chips = pl.program_id(0), pl.num_programs(0)
    chip = lax.bitwise_xor(number, place_ref[0] // 2)

    def early_part(core, ref):
        early = ref[0].astype(full_type)
        out_ref[core] = early[:, :feat]
        query_ref[core, :, :width] = early[:, feat : feat + width]
        key_ref[core, :, :width] = early[:, feat + width :]

    def late_part(core, ref):
        late = ref[0].astype(full_type)
        for kind, target in enumerate((query_ref, key_ref, value_ref)):
            target[core, :, width:] = late[:, kind * width : kind * width + width]
        value_ref[core, :, :width] = late[:, 3 * width + LANES :]
        small = late[:, 3 * width : 3 * width + LANES]
        held_ref[pl.ds(pl.multiple_of((2 * chip + core) * rows, 8), rows), :] = small

    for core, side in ((own, 0), (1 - own, 4)):
        for half in range(2):

            @pl.when((number >= chips // 2) == (half == 1))
            def _():
                early_part(core, pieces[side + half])

            @pl.when((lax.rem(number, 2) == 1) == (half == 1))
            def _():
                late_part(core, pieces[side + 2 + half])

    @pl.when(number == chips - 1)
    def _():
        columns = held_ref[...].T
        router_ref[...] = columns[: router_ref.shape[0]]
        for k, ref in enumerate(vector_refs):
            ref[...] = columns[32 + k]


def assemble(place, own, other, expert_count):
    half, rows, early_width = own[0].shape
    late_width = own[2].shape[2]
    chips = 2 * half
    feat = 2 * chips * rows
    first = pl.BlockSpec((1, rows, early_width), lambda i, p: (jnp.minimum(i, half - 1), 0, 0))
    second = pl.BlockSpec((1, rows, early_width), lambda i, p: (jnp.maximum(i - half, 0), 0, 0))
    paired = pl.BlockSpec((1, rows, late_width), lambda i, p: (i // 2, 0, 0))
    matrix, vector, router = out((2 * chips, rows, feat), full_type), out((feat,), full_type), out((expert_count, feat), full_type)
    results = pl.pallas_call(
        assemble_body,
        out_shape=(matrix,) * 4 + (router,) + (vector,) * 7,
        grid_spec=pltpu.PrefetchScalarGridSpec(
            num_scalar_prefetch=1,
            grid=(chips,),
            in_specs=[first, second, paired, paired] * 2,
            out_specs=[pl.BlockSpec((2, rows, feat), lambda i, p: (lax.bitwise_xor(i, p[0] // 2), 0, 0))] * 4
            + [pl.BlockSpec((expert_count, feat), lambda i, p: (0, 0))]
            + [pl.BlockSpec((feat,), lambda i, p: (0,))] * 7,
            scratch_shapes=[pltpu.VMEM((feat, LANES), full_type)],
        ),
        name="assemble",
        compiler_params=pltpu.CompilerParams(vmem_limit_bytes=vmem_bytes),
        cost_estimate=pl.CostEstimate(flops=1024, bytes_accessed=1024, transcendentals=0),
    )(place, *own, *other)
    return [a.reshape(feat, feat) for a in results[:4]], results[4], results[5:]


def widen_body(steps, sum_ref, up_ref, down_ref, up_bias_ref, down_bias_ref):
    share, feat = up_ref.shape[0], sum_ref.shape[1]
    for step in range(steps):
        up_ref[:, step * feat : step * feat + feat] = sum_ref[step * share : step * share + share, :].astype(full_type)
    ends = 2 * steps * share
    down_ref[...] = sum_ref[steps * share : ends, :].astype(full_type)
    last = sum_ref[ends:, :].astype(full_type)
    up_bias_ref[...] = last[0:1, : steps * share]
    down_bias_ref[...] = last[8:9, :share]


def widen(expert_sum, steps, share):
    feat = expert_sum.shape[1]
    return call(
        functools.partial(widen_body, steps),
        (
            out((share, steps * feat), full_type),
            out((steps * share, feat), full_type),
            out((1, steps * share), full_type),
            out((1, share), full_type),
        ),
        "widen",
    )(expert_sum)


def shards(
    tokens,
    first_gain,
    first_shift,
    query_weight,
    query_bias,
    key_weight,
    value_weight,
    value_bias,
    out_weight,
    out_bias,
    second_gain,
    second_shift,
    router,
    expert_up,
    expert_up_bias,
    expert_down,
    expert_down_bias,
    choices,
    priority,
    cotangent,
):
    tok_count, feat = tokens.shape
    expert_count = lax.axis_size("expert")
    capacity = (21 * tok_count + 80 * expert_count - 1) // (80 * expert_count) * 8
    router3 = jnp.pad(jnp.concatenate([router] * 3, axis=1), ((0, 0), (0, LANES - 3 * expert_count)))
    up, down = expert_up[0], expert_down[0]

    replicas = lax.axis_size("dp")
    choice_rows = choices.T
    place, cot_sent = route(choice_rows, priority, cotangent, expert_count, capacity)
    cot = exchange(cot_sent, expert_count)
    first, q, k, v, log_big, log_small, attended, middle, _, probs, sent = front(
        tokens,
        (first_gain, first_shift, query_bias, value_bias, out_bias, second_gain, second_shift),
        (query_weight, key_weight, value_weight, out_weight),
        router3,
        place,
        expert_count,
        capacity,
    )
    rows = exchange(behind(sent, mark(cot)), expert_count)
    grad_act, start = act_grad(cot, down, expert_down_bias)
    slot = slot_columns(choice_rows, place, capacity, (start,))
    act, grad_pre, gate, score, weight_part = expert(
        rows, up, expert_up_bias, grad_act, start, cot, replicas
    )
    expert_sum = lax.psum_scatter(weight_part, "dp", scatter_dimension=0, tiled=True)[0]
    grad_in = expert_grad_in(grad_pre, up, gate, score, capacity, (slot,))
    back = exchange(grad_in, expert_count)
    result = expert_result(act, down, expert_down_bias, (grad_in,))
    grad_middle, grad_attended, wo_grad, router_part, second_parts = combine(
        back,
        slot,
        probs,
        middle,
        cotangent,
        attended,
        out_weight,
        router3,
        second_gain,
        second_shift,
        expert_count,
        capacity,
        (result,),
    )
    out_blocks = send_blocks(wo_grad, back)
    grads, bias_parts, group_parts, before = [], [], [], ()
    for group in range(HEAD_GROUPS):
        dq, dk, dv, group_part, bias_part = attention_grad(
            group, q, k, v, grad_attended, log_big, log_small, first, before
        )
        grads += [dq, dk, dv]
        bias_parts.append(bias_part)
        group_parts.append(group_part)
        before = (dv, out_blocks)
    first_blocks = send_blocks(group_parts[0], mark(out_blocks))
    token_grad, last_part = input_grad(
        grads,
        query_weight,
        key_weight,
        value_weight,
        tokens,
        first_gain,
        grad_middle,
        bias_parts,
        second_parts,
        router_part,
        group_parts[1],
        (),
    )
    late = behind(last_part, mark(first_blocks)).reshape(expert_count, -1, last_part.shape[1])
    late = scatter_chips(scatter_step(late, 0, 2))
    first_sum = sum_blocks(first_blocks)
    width = feat // HEAD_GROUPS
    early = jnp.concatenate([sum_blocks(out_blocks), first_sum[:, : 2 * width]], axis=1)
    returned = exchange(behind(result, late), expert_count)
    late = jnp.concatenate([late, first_sum[:, 2 * width :]], axis=1)
    share, steps = feat // replicas, up.shape[1] // feat
    up_grad, down_grad, up_bias_grad, down_bias_grad = widen(expert_sum, steps, share)
    block_output = block_result(returned, slot, probs, middle, expert_count, (token_grad,))
    early, late = gather_chips(sum_replicas([early, late], (up_grad,)), (block_output,))
    place_here = lax.axis_index("expert").reshape(1)
    own = [*early, *late]
    other = [swap(a, "expert", 0) for a in own]
    (out_grad, query_grad, key_grad, value_grad), router_grad, vectors = assemble(place_here, own, other, expert_count)
    return (
        block_output,
        token_grad,
        vectors[0],
        vectors[1],
        query_grad,
        vectors[2],
        key_grad,
        value_grad,
        vectors[3],
        out_grad,
        vectors[6],
        vectors[4],
        vectors[5],
        router_grad.T,
        up_grad[None],
        up_bias_grad,
        down_grad[None],
        down_bias_grad,
    )


def solution(mesh):
    tokens_spec = P(("dp", "expert"), None)
    return jax.shard_map(
        shards,
        mesh=mesh,
        in_specs=(tokens_spec,)
        + (P(),) * 12
        + (P("expert", None, None), P("expert", None), P("expert", None, None), P("expert", None))
        + (tokens_spec,) * 3,
        out_specs=(tokens_spec,) * 2
        + (P(),) * 12
        + (P("expert", "dp", None), P("expert", "dp"), P("expert", "dp", None), P("expert", "dp")),
        check_vma=False,
    )
```
